32 devices in a mesh: depth: 4 (over x, core), plane: 8 (over z, y).
Axes of the slice: x: 2, y: 2, z: 4, core: 2. Of those that a mesh axis runs over, the one named last changes fastest.
Arguments:
- magnet: float32 [3, 32, 32, 1024], P(None, 'depth', 'plane'), may hold values from -1 to 1, as said below
- mask: int32 [32, 1024], P('plane'), may hold values 0 or 1
- materials: int32 [32], P('depth'), may hold values from 0 to 3
- exchange_strength: float32 [4], replicated, may hold values from 0.5 to 2
- anisotropy: float32 [4], replicated, may hold values from 0.5 to 3
- damping: float32 [4], replicated, may hold values from 0.05 to 0.6
- source_strength: float32 [4], replicated, may hold values from 0.3 to 1.5
- thermal_strength: float32 [4], replicated, may hold values from 0.5 to 2
- pivots: float32 [32, 3, 3], replicated, may hold values from -1 to 1, as said below
- lower: float32 [32, 3, 3], replicated, may hold values from -1 to 1, as said below
- upper: float32 [32, 3, 3], replicated, may hold values from -1 to 1, as said below
- noise_stream: int32 [1], replicated, may hold values from 0 to 999999
- counter: int32 [1], replicated, may hold values from 0 to 99999
Outputs:
- magnet_next: float32 [3, 32, 32, 1024], P(None, 'depth', 'plane')
- accumulation: float32 [3, 32, 32, 1024], P(None, 'depth', 'plane')
The draws below stay inside these ranges and needn't reach their ends.
Inputs may be any that keep to these rules, and one draw needn't show every extreme that they name: `magnet`: unit vectors. `pivots`: each block has spectral norm below 0.98. `lower`: each block has spectral norm below 1. `upper`: each block has spectral norm below 1.
All inputs are finite; a program needn't handle non-finite values. No bound on the sum of `mask` on one device may be relied on, other than what follows from the above.
Results may differ from the reference program's by a relative error of at most 0.000073.
Values sent between devices are 32-bit elements; how exact they have to be, the bound alone decides.
No kernel may reach another device: no remote copies, remote signals or barrier semaphores. Data moves between devices by JAX's collectives and lax.ppermute only.
A program may use at most 128 MiB of HBM per device.

```python
import math
import jax
import jax.numpy as jnp
from jax import lax

NY = 1024
NMAT = 4
NX = 32
LZ = 32


def draw_magnet(key, part):
    key_z, key_phi = jax.random.split(key)
    height = jax.random.uniform(key_z, (LZ, NX, NY), jnp.float32, -1.0, 1.0)
    phase = jax.random.uniform(key_phi, (LZ, NX, NY), jnp.float32, -3.14159265, 3.14159265)
    radius = jnp.sqrt(jnp.maximum(1.0 - height * height, 0.0))
    return jnp.stack([radius * jnp.cos(phase), radius * jnp.sin(phase), height]).astype(jnp.float32)


def antisym_blocks(key, diag_lo, diag_hi, sign, spread):
    key_d, key_w = jax.random.split(key)
    diag = sign * jax.random.uniform(key_d, (LZ, 1, 1), jnp.float32, diag_lo, diag_hi)
    twist = jax.random.uniform(key_w, (LZ, 3), jnp.float32, -spread, spread)
    zero = jnp.zeros((LZ,), jnp.float32)
    rows = [jnp.stack([zero, -twist[:, 2], twist[:, 1]], axis=1), jnp.stack([twist[:, 2], zero, -twist[:, 0]], axis=1), jnp.stack([-twist[:, 1], twist[:, 0], zero], axis=1)]
    skew = jnp.stack(rows, axis=1)
    return (diag * jnp.eye(3, dtype=jnp.float32)[None] + skew).astype(jnp.float32)


def draw_pivots(key, part):
    return antisym_blocks(jax.random.fold_in(key, 11), 0.75, 0.95, 1.0, 0.12)


def draw_lower(key, part):
    return antisym_blocks(jax.random.fold_in(key, 23), 0.85, 0.96, -1.0, 0.1)


def draw_upper(key, part):
    return antisym_blocks(jax.random.fold_in(key, 37), 0.75, 0.93, -1.0, 0.12)


def with_ends(values, stream_key, low, largest):
    place = [jax.random.randint(jax.random.fold_in(stream_key, axis), (), 0, length) for axis, length in enumerate(values.shape)]
    longest = values.shape.index(max(values.shape))
    neighbour = place[:longest] + [(place[longest] + 1) % values.shape[longest]] + place[longest + 1:]
    return values.at[tuple(place)].set(low).at[tuple(neighbour)].set(largest)


def setup_inputs(seed: int = 0) -> dict:
    keys = jax.random.split(jax.random.key(seed), 14)
    return {
        "magnet": draw_magnet(jax.random.fold_in(keys[13], 71), 0),
        "mask": with_ends((jax.random.randint(keys[1], (NX, NY), 0, 10) < 9).astype(jnp.int32), jax.random.fold_in(keys[1], 1), 0, 1),
        "materials": with_ends(jax.random.randint(keys[2], (LZ,), 0, NMAT), jax.random.fold_in(keys[2], 1), 0, NMAT - 1).astype(jnp.int32),
        "exchange_strength": jnp.clip(jnp.exp(jax.random.uniform(keys[3], (NMAT,), jnp.float32, math.log(0.5), math.log(2.0))), 0.5, 2.0),
        "anisotropy": jnp.clip(jax.random.uniform(keys[4], (NMAT,), jnp.float32, 0.5, 3.0), 0.5, 3.0),
        "damping": jnp.clip(jax.random.uniform(keys[5], (NMAT,), jnp.float32, 0.05, 0.6), 0.05, 0.6),
        "source_strength": jnp.clip(jax.random.uniform(keys[6], (NMAT,), jnp.float32, 0.3, 1.5), 0.3, 1.5),
        "thermal_strength": jnp.clip(jax.random.uniform(keys[7], (NMAT,), jnp.float32, 0.5, 2.0), 0.5, 2.0),
        "pivots": draw_pivots(jax.random.fold_in(keys[13], 71), 0),
        "lower": draw_lower(jax.random.fold_in(keys[13], 71), 0),
        "upper": draw_upper(jax.random.fold_in(keys[13], 71), 0),
        "noise_stream": jax.random.randint(keys[11], (1,), 0, 1000000).astype(jnp.int32),
        "counter": jax.random.randint(keys[12], (1,), 0, 100000).astype(jnp.int32),
    }


def cross(a, b):
    return jnp.stack([a[1] * b[2] - a[2] * b[1], a[2] * b[0] - a[0] * b[2], a[0] * b[1] - a[1] * b[0]])

def apply_block(block, vec):
    return jnp.stack([block[row, 0] * vec[0] + block[row, 1] * vec[1] + block[row, 2] * vec[2] for row in range(3)])

def solve_columns(source, pivots, lower, upper):
    layer_count = source.shape[1]
    previous = jnp.zeros_like(source[:, 0])
    forward_values = []
    for layer_pos in range(layer_count):
        previous = apply_block(pivots[layer_pos], source[:, layer_pos] - apply_block(lower[layer_pos], previous))
        forward_values.append(previous)
    after = jnp.zeros_like(source[:, 0])
    solved = [None] * layer_count
    for layer_pos in range(layer_count - 1, -1, -1):
        after = forward_values[layer_pos] - apply_block(upper[layer_pos], after)
        solved[layer_pos] = after
    return jnp.stack(solved, axis=1)

def hash_uniform(index, stream, counter):
    mixed = index * 739982445 + stream * 695872825 + counter * 1597334677
    mixed = mixed ^ lax.shift_right_logical(mixed, jnp.int32(16))
    mixed = mixed * 739982445
    mixed = mixed ^ lax.shift_right_logical(mixed, jnp.int32(15))
    mixed = mixed * 695872825
    mixed = mixed ^ lax.shift_right_logical(mixed, jnp.int32(16))
    return (mixed & 65535).astype(jnp.float32) / 32767.5 - 1.0

def layer_values(materials, table):
    onehot = (materials[:, None] == jnp.arange(table.shape[0], dtype=jnp.int32)[None, :]).astype(jnp.float32)
    return lax.optimization_barrier(jnp.sum(onehot * table[None, :], axis=1))[None, :, None, None]

def normalize(vec):
    return vec / jnp.sqrt(lax.optimization_barrier(jnp.sum(vec * vec, axis=0, keepdims=True)))

def reference(magnet, mask, materials, exchange_strength, anisotropy, damping, source_strength, thermal_strength, pivots, lower, upper, noise_stream, counter):
    maskf = mask.astype(jnp.float32)[None, None]
    stiff = layer_values(materials, exchange_strength)
    aniso = layer_values(materials, anisotropy)
    alpha = layer_values(materials, damping)
    beta = layer_values(materials, source_strength)
    theta = layer_values(materials, thermal_strength)
    comp = jnp.arange(3, dtype=jnp.int32)[:, None, None, None]
    layer = jnp.arange(LZ, dtype=jnp.int32)[None, :, None, None]
    xrow = jnp.arange(NX, dtype=jnp.int32)[None, None, :, None]
    ycol = jnp.arange(NY, dtype=jnp.int32)[None, None, None, :]
    index = ((comp * LZ + layer) * NX + xrow) * NY + ycol
    noise = theta * hash_uniform(index, noise_stream[0], counter[0])
    axis_z = jnp.array([0.0, 0.0, 1.0], dtype=jnp.float32)[:, None, None, None]

    def rate(field):
        masked = field * maskf
        near = jnp.roll(masked, 1, 2) + jnp.roll(masked, -1, 2) + jnp.roll(masked, 1, 3) + jnp.roll(masked, -1, 3)
        far = jnp.roll(masked, 2, 2) + jnp.roll(masked, -2, 2) + jnp.roll(masked, 2, 3) + jnp.roll(masked, -2, 3)
        planar = 4.0 / 3.0 * near - 1.0 / 12.0 * far
        padded = jnp.pad(masked, ((0, 0), (1, 1), (0, 0), (0, 0)))
        vertical = padded[:, 2:] + padded[:, :-2]
        accum = solve_columns(beta * field, pivots, lower, upper)
        heff = stiff * (planar + 0.5 * vertical) + aniso * field * axis_z + noise + 0.5 * accum
        torque = cross(field, heff)
        change = -(torque + alpha * cross(field, torque)) / (1.0 + alpha * alpha) * maskf
        return (change, accum)
    first, _ = rate(magnet)
    middle = normalize(magnet + 0.03 * first)
    second, accum = rate(middle)
    magnet_next = normalize(magnet + 0.015 * (first + second))
    return (magnet_next, accum)
```

```python
import functools

import jax
import jax.numpy as jnp
from jax import lax
from jax.experimental import pallas as pl
from jax.experimental.pallas import tpu as pltpu
from jax.sharding import PartitionSpec as P

LANES = 128
NEAR = 4.0 / 3.0
FAR = -1.0 / 12.0
HALO = 2
F32 = jnp.float32


def wrapped(value):
    value &= 0xFFFFFFFF
    return value - (1 << 32) if value >= (1 << 31) else value


HASH_A = wrapped(739982445)
HASH_B = wrapped(695872825)
HASH_C = wrapped(1597334677)


class Dims:
    def __init__(self, layers, rows, width, depth, plane):
        self.layers = layers
        self.rows = rows
        self.width = width
        self.chunks = width // LANES
        self.depth = depth
        self.plane = plane
        self.tile = (self.chunks, LANES)

    def field(self):
        return (3, self.layers, self.rows) + self.tile


def shape(*dims):
    return jax.ShapeDtypeStruct(dims, F32)


def vmem():
    return pl.BlockSpec(memory_space=pltpu.VMEM)


def smem():
    return pl.BlockSpec(memory_space=pltpu.SMEM)


def cells(dims, comp, layer, row):
    base = (comp * dims.layers + layer) * (dims.chunks * dims.rows) + row
    return pl.ds(base, dims.chunks, stride=dims.rows)


def mask_tile(dims, mask_ref, row):
    return mask_ref[pl.ds(row, dims.chunks, stride=dims.rows), :].astype(F32)


def matvec(get, vec):
    return [get(i, 0) * vec[0] + get(i, 1) * vec[1] + get(i, 2) * vec[2] for i in range(3)]


def add(a, b):
    return [x + y for x, y in zip(a, b)]


def cross(a, b):
    return [
        a[1] * b[2] - a[2] * b[1],
        a[2] * b[0] - a[0] * b[2],
        a[0] * b[1] - a[1] * b[0],
    ]


def unit(vec):
    scale = lax.rsqrt(vec[0] * vec[0] + vec[1] * vec[1] + vec[2] * vec[2])
    return [v * scale for v in vec]


def edges_kernel(dims, magnet, mask, low, high):
    for r in range(HALO):
        top = dims.rows - HALO + r
        mask_low = mask_tile(dims, mask, r)
        mask_high = mask_tile(dims, mask, top)
        for c in range(3):
            for l in range(dims.layers):
                low[c, l, r] = magnet[cells(dims, c, l, r), :] * mask_low
                high[c, l, r] = magnet[cells(dims, c, l, top), :] * mask_high


def sweep_kernel(dims, natural, field, mask, materials, source, pivots, lower, upper, *refs):
    messages, local = refs[: dims.depth - 1], refs[dims.depth - 1]
    group = lax.axis_index("depth")

    def load(c, l, r):
        if natural:
            return field[cells(dims, c, l, r), :]
        return field[c, l, r]

    def block(ref, layer):
        at = group * dims.layers + layer
        return lambda i, j: ref[at, i, j]

    rows = range(dims.rows)

    def forward(l, prev):
        beta = source[materials[l]]
        out = []
        for r in rows:
            f = [beta * load(c, l, r) for c in range(3)]
            low = matvec(block(lower, l), prev[r])
            y = matvec(block(pivots, l), [a - b for a, b in zip(f, low)])
            for c in range(3):
                local[c, l, r] = y[c]
            out.append(y)
        return out

    def backward(k, after):
        l = dims.layers - 1 - k
        out = []
        for r in rows:
            up = matvec(block(upper, l), after[r])
            s = [local[c, l, r] - up[c] for c in range(3)]
            for c in range(3):
                local[c, l, r] = s[c]
            out.append(s)
        return out

    zero = [[jnp.zeros(dims.tile, F32)] * 3 for _ in rows]
    last = lax.fori_loop(0, dims.layers, forward, zero)
    first = lax.fori_loop(0, dims.layers, backward, zero)
    for k, message in enumerate(messages, 1):
        for r in rows:
            for c in range(3):
                message[c, r] = last[r][c]
                message[3 + c, r] = first[r][c]
        at = 6
        for take, l in ((k == 1, dims.layers - 1), (k == dims.depth - 1, 0)):
            if take:
                for r in rows:
                    mask_row = mask_tile(dims, mask, r)
                    for c in range(3):
                        message[at + c, r] = load(c, l, r) * mask_row
                at += 3


def response_kernel(dims, pivots, lower, upper, out):
    total = dims.layers * dims.depth
    lane = lax.broadcasted_iota(jnp.int32, (1, LANES), 1)
    for g in range(dims.depth):
        y = [(lane == c).astype(F32) for c in range(3)]
        s = [(lane == 3 + c).astype(F32) for c in range(3)]

        def forward(k, y):
            l = g * dims.layers + k
            low = matvec(lambda i, j: lower[l, i, j], y)
            y = matvec(lambda i, j: pivots[l, i, j], [-a for a in low])
            for c in range(3):
                out[l, pl.ds(c, 1)] = y[c]
            return y

        def backward(k, s):
            l = (g + 1) * dims.layers - 1 - k
            up = matvec(lambda i, j: upper[l, i, j], s)
            s = [out[l, pl.ds(c, 1)] - up[c] for c in range(3)]
            for c in range(3):
                out[l, pl.ds(c, 1)] = s[c]
            return s

        y = lax.fori_loop(0, dims.layers, forward, y)
        for c in range(3):
            out[total + g, pl.ds(c, 1)] = y[c]
        lax.fori_loop(0, dims.layers, backward, s)


def shifted_sum(dims, w, lane):
    after = pltpu.roll(w, dims.chunks - 1, 0)
    before = pltpu.roll(w, 1, 0)
    near = pltpu.roll(jnp.where(lane < 1, after, w), LANES - 1, 1)
    near += pltpu.roll(jnp.where(lane >= LANES - 1, before, w), 1, 1)
    far = pltpu.roll(jnp.where(lane < 2, after, w), LANES - 2, 1)
    far += pltpu.roll(jnp.where(lane >= LANES - 2, before, w), 2, 1)
    return NEAR * near + FAR * far


def hash_uniform(mixed):
    mixed = mixed ^ lax.shift_right_logical(mixed, jnp.int32(16))
    mixed = mixed * HASH_A
    mixed = mixed ^ lax.shift_right_logical(mixed, jnp.int32(15))
    mixed = mixed * HASH_B
    mixed = mixed ^ lax.shift_right_logical(mixed, jnp.int32(16))
    return (mixed & 65535).astype(F32) * (1.0 / 32767.5) - 1.0


def local_kernel(dims, first, field, mask, local, materials, stiffness, anisotropy, *refs):
    if first:
        thermal, stream, counter, heff, noise, masked = refs
        group = lax.axis_index("depth")
        block = lax.axis_index("plane")
        within = (
            lax.broadcasted_iota(jnp.int32, dims.tile, 0) * LANES
            + lax.broadcasted_iota(jnp.int32, dims.tile, 1)
        ) * HASH_A
        seed = stream[0] * HASH_B + counter[0] * HASH_C
    else:
        noise, heff, masked = refs
    lane = lax.broadcasted_iota(jnp.int32, dims.tile, 1)
    rows = range(dims.rows)

    def load(c, l, r):
        if first:
            return field[cells(dims, c, l, r), :]
        return field[c, l, r]

    for c in range(3):
        for r in rows:
            masked[c, 0, r] = jnp.zeros(dims.tile, F32)
            masked[c, dims.layers + 1, r] = jnp.zeros(dims.tile, F32)

    def fill(l, carry):
        for r in rows:
            mask_row = mask_tile(dims, mask, r)
            for c in range(3):
                masked[c, l + 1, r] = load(c, l, r) * mask_row
        return carry

    lax.fori_loop(0, dims.layers, fill, 0)

    def body(l, carry):
        material = materials[l]
        stiff = stiffness[material]
        aniso = anisotropy[material]
        for c in range(3):
            w = [masked[c, l + 1, r] for r in rows]
            for r in rows:
                total = shifted_sum(dims, w[r], lane)
                for step, weight in ((1, NEAR), (2, FAR)):
                    inside = [w[q] for q in (r - step, r + step) if 0 <= q < dims.rows]
                    if inside:
                        total += weight * functools.reduce(jnp.add, inside)
                total += 0.5 * (masked[c, l, r] + masked[c, l + 2, r])
                h = stiff * total + 0.5 * local[c, l, r]
                if c == 2:
                    h += aniso * load(c, l, r)
                if first:
                    layer = group * dims.layers + l
                    line = (c * (dims.depth * dims.layers) + layer) * (
                        dims.plane * dims.rows
                    ) + (block * dims.rows + r)
                    start = line * dims.width * HASH_A + seed
                    value = thermal[material] * hash_uniform(within + start)
                    noise[c, l, r] = value
                    h += value
                else:
                    h += noise[c, l, r]
                heff[c, l, r] = h
        return carry

    lax.fori_loop(0, dims.layers, body, 0)


def finish_kernel(
    dims,
    first,
    field,
    mask,
    heff,
    own,
    response,
    materials,
    stiffness,
    damping,
    before,
    after,
    *refs,
):
    others, refs = refs[: dims.depth - 1], refs[dims.depth - 1 :]
    if first:
        middle, base, low, high, bound, edge = refs
    else:
        base, local, result, accum, bound, edge = refs
    group = lax.axis_index("depth")
    total = dims.layers * dims.depth
    rows = range(dims.rows)

    def load(c, l, r):
        if first:
            return field[cells(dims, c, l, r), :]
        return field[c, l, r]

    def carry_y(g):
        return lambda i, j: response[total + g, i, j]

    def first_y(g):
        return lambda i, j: response[g * dims.layers, i, j]

    def first_s(g):
        return lambda i, j: response[g * dims.layers, i, 3 + j]

    for g in range(dims.depth):

        @pl.when(group == g)
        def _():
            def message(h):
                return own if h == g else others[(g - h) % dims.depth - 1]

            for r in rows:
                end = [
                    [message(h)[c, r] for c in range(3)] for h in range(dims.depth - 1)
                ]
                ys = {0: None}
                for h in range(1, dims.depth):
                    ys[h] = end[h - 1]
                    if ys[h - 1] is not None:
                        ys[h] = add(ys[h], matvec(carry_y(h - 1), ys[h - 1]))
                s = None
                for h in range(dims.depth - 1, g, -1):
                    value = [message(h)[3 + c, r] for c in range(3)]
                    value = add(value, matvec(first_y(h), ys[h]))
                    if s is not None:
                        value = add(value, matvec(first_s(h), s))
                    s = value
                for c in range(3):
                    zero = jnp.zeros(dims.tile, F32)
                    bound[c, r] = zero if ys[g] is None else ys[g][c]
                    bound[3 + c, r] = zero if s is None else s[c]
                    edge[c, r] = zero if g == 0 else others[0][6 + c, r]
                    at = 9 if dims.depth == 2 else 6
                    top = others[dims.depth - 2]
                    edge[3 + c, r] = zero if g == dims.depth - 1 else top[at + c, r]

    def body(l, carry):
        material = materials[l]
        stiff = stiffness[material]
        alpha = damping[material]
        layer = group * dims.layers + l
        scale = 1.0 / (1.0 + jnp.full(dims.tile, alpha, F32) * alpha)
        down = jnp.where(l == 0, 0.5 * stiff, 0.0)
        up = jnp.where(l == dims.layers - 1, 0.5 * stiff, 0.0)
        for r in rows:
            v = [load(c, l, r) for c in range(3)]
            h = [heff[c, l, r] for c in range(3)]
            y = [bound[c, r] for c in range(3)]
            s = [bound[3 + c, r] for c in range(3)]
            fix = add(
                matvec(lambda i, j: response[layer, i, j], y),
                matvec(lambda i, j: response[layer, i, 3 + j], s),
            )
            for c in range(3):
                for step, weight in ((1, NEAR), (2, FAR)):
                    if r - step < 0:
                        h[c] += (stiff * weight) * before[c, l, r - step + HALO]
                    if r + step >= dims.rows:
                        h[c] += (stiff * weight) * after[c, l, r + step - dims.rows]
                h[c] += down * edge[c, r] + up * edge[3 + c, r] + 0.5 * fix[c]
            torque = cross(v, h)
            twice = cross(v, torque)
            mask_row = mask_tile(dims, mask, r)
            gain = scale * mask_row
            rate = [(torque[c] + alpha * twice[c]) * gain for c in range(3)]
            if first:
                m1 = unit([v[c] - 0.03 * rate[c] for c in range(3)])
                for c in range(3):
                    middle[c, l, r] = m1[c]
                    base[c, l, r] = v[c] - 0.015 * rate[c]
                    if r < HALO:
                        low[c, l, r] = m1[c] * mask_row
                    if r >= dims.rows - HALO:
                        high[c, l, r - dims.rows + HALO] = m1[c] * mask_row
            else:
                new = unit([base[c, l, r] - 0.015 * rate[c] for c in range(3)])
                for c in range(3):
                    result[cells(dims, c, l, r), :] = new[c]
                    accum[cells(dims, c, l, r), :] = local[c, l, r] + fix[c]
        return carry

    lax.fori_loop(0, dims.layers, body, 0)


def call(kernel, outs, ins, args, scratch=(), flops=1000000):
    return pl.pallas_call(
        kernel,
        out_shape=outs,
        in_specs=[smem() if i else vmem() for i in ins],
        out_specs=[vmem()] * len(outs),
        scratch_shapes=scratch,
        cost_estimate=pl.CostEstimate(flops=flops, bytes_accessed=1000000, transcendentals=0),
    )(*args)


def ring(count, step):
    return [(i, (i + step) % count) for i in range(count)]


def local(
    magnet,
    mask,
    materials,
    exchange_strength,
    anisotropy,
    damping,
    source_strength,
    thermal_strength,
    pivots,
    lower,
    upper,
    noise_stream,
    counter,
):
    dims = Dims(
        magnet.shape[1],
        magnet.shape[2],
        magnet.shape[3],
        lax.axis_size("depth"),
        lax.axis_size("plane"),
    )
    lines = (3, dims.layers, dims.rows, dims.chunks, LANES)
    view = magnet.reshape(lines).transpose(0, 1, 3, 2, 4).reshape(-1, LANES)
    mask_view = mask.reshape(lines[2:]).transpose(1, 0, 2).reshape(-1, LANES)
    halo = shape(3, dims.layers, HALO, *dims.tile)
    field = shape(*dims.field())
    planes = 3 * dims.rows

    def bind(kernel, *static):
        return functools.partial(kernel, dims, *static)

    def swap_plane(low, high):
        after = lax.ppermute(low, "plane", ring(dims.plane, -1))
        before = lax.ppermute(high, "plane", ring(dims.plane, 1))
        return before, after

    messages = []
    for k in range(1, dims.depth):
        parts = 6 + 3 * (k == 1) + 3 * (k == dims.depth - 1)
        messages.append(shape(parts, dims.rows, *dims.tile))

    def swap_depth(sent):
        return [
            lax.ppermute(message, "depth", ring(dims.depth, k)) for k, message in enumerate(sent, 1)
        ]

    def sweep(natural, values):
        out = call(
            bind(sweep_kernel, natural),
            messages + [field],
            [0, 0, 1, 1, 1, 1, 1],
            (values, mask_view, materials, source_strength, pivots, lower, upper),
        )
        return out[:-1], out[-1]

    padded = pltpu.VMEM((3, dims.layers + 2, dims.rows) + dims.tile, F32)
    bounds = [pltpu.VMEM((6, dims.rows) + dims.tile, F32)] * 2

    low, high = call(bind(edges_kernel), [halo, halo], [0, 0], (view, mask_view))
    before, after = swap_plane(low, high)
    sent, solved = sweep(True, view)
    others = swap_depth(sent)
    (response,) = call(
        bind(response_kernel),
        [shape(dims.depth * (dims.layers + 1), 3, LANES)],
        [1, 1, 1],
        (pivots, lower, upper),
    )
    heff, noise = call(
        bind(local_kernel, True),
        [field, field],
        [0, 0, 0, 1, 1, 1, 1, 1, 1],
        (
            view,
            mask_view,
            solved,
            materials,
            exchange_strength,
            anisotropy,
            thermal_strength,
            noise_stream,
            counter,
        ),
        [padded],
    )
    kinds = [0, 0, 0, 0, 1, 1, 1, 1] + [0] * (1 + dims.depth)
    middle, base, low, high = call(
        bind(finish_kernel, True),
        [field, field, halo, halo],
        kinds,
        (
            view,
            mask_view,
            heff,
            sent[0],
            response,
            materials,
            exchange_strength,
            damping,
            before,
            after,
            *others,
        ),
        bounds,
    )
    before, after = swap_plane(low, high)
    sent, solved = sweep(False, middle)
    others = swap_depth(sent)
    (heff,) = call(
        bind(local_kernel, False),
        [field],
        [0, 0, 0, 1, 1, 1, 0],
        (middle, mask_view, solved, materials, exchange_strength, anisotropy, noise),
        [padded],
    )
    lined = shape(*view.shape)
    result, accum = call(
        bind(finish_kernel, False),
        [lined, lined],
        kinds + [0, 0],
        (
            middle,
            mask_view,
            heff,
            sent[0],
            response,
            materials,
            exchange_strength,
            damping,
            before,
            after,
            *others,
            base,
            solved,
        ),
        bounds,
    )

    def whole(lines_view):
        cut = lines_view.reshape(3, dims.layers, dims.chunks, dims.rows, LANES)
        return cut.transpose(0, 1, 3, 2, 4).reshape(magnet.shape)

    return whole(result), whole(accum)


def solution(mesh):
    placed = (
        P(None, "depth", "plane", None),
        P("plane", None),
        P("depth"),
    ) + (P(),) * 10
    return jax.shard_map(
        local,
        mesh=mesh,
        in_specs=placed,
        out_specs=(P(None, "depth", "plane", None), P(None, "depth", "plane", None)),
        check_vma=False,
    )
```

```python
import functools

import jax
import jax.numpy as jnp
from jax import lax
from jax.experimental import pallas as pl
from jax.experimental.pallas import tpu as pltpu
from jax.sharding import PartitionSpec as P

LANES = 128
NEAR = 4.0 / 3.0
FAR = -1.0 / 12.0
HALO = 2
VMEM_LIMIT = 16 * 1024 * 1024
F32 = jnp.float32


def wrapped(value):
    value &= 0xFFFFFFFF
    return value - (1 << 32) if value >= (1 << 31) else value


HASH_A = wrapped(739982445)
HASH_B = wrapped(695872825)
HASH_C = wrapped(1597334677)


class Dims:
    def __init__(self, layers, rows, width, depth, plane):
        self.layers = layers
        self.rows = rows
        self.width = width
        self.chunks = width // LANES
        self.depth = depth
        self.plane = plane
        self.tile = (self.chunks, LANES)

    def field(self):
        return (3, self.layers, self.rows) + self.tile


def shape(*dims):
    return jax.ShapeDtypeStruct(dims, F32)


def vmem():
    return pl.BlockSpec(memory_space=pltpu.VMEM)


def smem():
    return pl.BlockSpec(memory_space=pltpu.SMEM)


def cells(dims, comp, layer, row):
    base = (comp * dims.layers + layer) * (dims.chunks * dims.rows) + row
    return pl.ds(base, dims.chunks, stride=dims.rows)


def mask_tile(dims, mask_ref, row):
    return mask_ref[pl.ds(row, dims.chunks, stride=dims.rows), :].astype(F32)


def matvec(get, vec):
    return [get(i, 0) * vec[0] + get(i, 1) * vec[1] + get(i, 2) * vec[2] for i in range(3)]


def add(a, b):
    return [x + y for x, y in zip(a, b)]


def cross(a, b):
    return [
        a[1] * b[2] - a[2] * b[1],
        a[2] * b[0] - a[0] * b[2],
        a[0] * b[1] - a[1] * b[0],
    ]


def unit(vec):
    scale = lax.rsqrt(vec[0] * vec[0] + vec[1] * vec[1] + vec[2] * vec[2])
    return [v * scale for v in vec]


def edges_kernel(dims, magnet, mask, low, high):
    for r in range(HALO):
        top = dims.rows - HALO + r
        mask_low = mask_tile(dims, mask, r)
        mask_high = mask_tile(dims, mask, top)
        for c in range(3):
            for l in range(dims.layers):
                low[c, l, r] = magnet[cells(dims, c, l, r), :] * mask_low
                high[c, l, r] = magnet[cells(dims, c, l, top), :] * mask_high


def sweep_kernel(dims, natural, field, mask, materials, source, pivots, lower, upper, *refs):
    messages, local = refs[: dims.depth - 1], refs[dims.depth - 1]
    group = lax.axis_index("depth")

    def load(c, l, r):
        if natural:
            return field[cells(dims, c, l, r), :]
        return field[c, l, r]

    def block(ref, layer):
        at = group * dims.layers + layer
        return lambda i, j: ref[i, j, at]

    rows = range(dims.rows)

    def forward(l, prev):
        beta = source[materials[l]]
        out = []
        for r in rows:
            f = [beta * load(c, l, r) for c in range(3)]
            low = matvec(block(lower, l), prev[r])
            y = matvec(block(pivots, l), [a - b for a, b in zip(f, low)])
            for c in range(3):
                local[c, l, r] = y[c]
            out.append(y)
        return out

    def backward(k, after):
        l = dims.layers - 1 - k
        out = []
        for r in rows:
            up = matvec(block(upper, l), after[r])
            s = [local[c, l, r] - up[c] for c in range(3)]
            for c in range(3):
                local[c, l, r] = s[c]
            out.append(s)
        return out

    zero = [[jnp.zeros(dims.tile, F32)] * 3 for _ in rows]
    last = lax.fori_loop(0, dims.layers, forward, zero)
    first = lax.fori_loop(0, dims.layers, backward, zero)
    for k, message in enumerate(messages, 1):
        for r in rows:
            for c in range(3):
                message[c, r] = last[r][c]
                message[3 + c, r] = first[r][c]
        at = 6
        for take, l in ((k == 1, dims.layers - 1), (k == dims.depth - 1, 0)):
            if take:
                for r in rows:
                    mask_row = mask_tile(dims, mask, r)
                    for c in range(3):
                        message[at + c, r] = load(c, l, r) * mask_row
                at += 3


def response_kernel(dims, pivots, lower, upper, out, table):
    total = dims.layers * dims.depth
    groups = range(dims.depth)
    lane = lax.broadcasted_iota(jnp.int32, (1, LANES), 1)
    table[...] = jnp.zeros_like(table)

    def forward(k, ys):
        done = []
        for g in groups:
            l = g * dims.layers + k
            low = matvec(lambda i, j: lower[i, j, l], ys[g])
            y = matvec(lambda i, j: pivots[i, j, l], [-a for a in low])
            for c in range(3):
                table[pl.ds(3 * l + c, 1), :] = y[c]
            done.append(y)
        return done

    def backward(k, after):
        done = []
        for g in groups:
            l = (g + 1) * dims.layers - 1 - k
            up = matvec(lambda i, j: upper[i, j, l], after[g])
            s = [table[pl.ds(3 * l + c, 1), :] - up[c] for c in range(3)]
            for c in range(3):
                table[pl.ds(3 * l + c, 1), :] = s[c]
            done.append(s)
        return done

    start = [[(lane == c).astype(F32) for c in range(3)] for _ in groups]
    ends = lax.fori_loop(0, dims.layers, forward, start)
    for g in groups:
        for c in range(3):
            table[pl.ds(3 * (total + g) + c, 1), :] = ends[g][c]
    start = [[(lane == 3 + c).astype(F32) for c in range(3)] for _ in groups]
    lax.fori_loop(0, dims.layers, backward, start)
    out[...] = table[...].T[:8]


def shifted_sum(dims, w, lane):
    after = pltpu.roll(w, dims.chunks - 1, 0)
    before = pltpu.roll(w, 1, 0)
    near = pltpu.roll(jnp.where(lane < 1, after, w), LANES - 1, 1)
    near += pltpu.roll(jnp.where(lane >= LANES - 1, before, w), 1, 1)
    far = pltpu.roll(jnp.where(lane < 2, after, w), LANES - 2, 1)
    far += pltpu.roll(jnp.where(lane >= LANES - 2, before, w), 2, 1)
    return NEAR * near + FAR * far


def hash_uniform(mixed):
    mixed = mixed ^ lax.shift_right_logical(mixed, jnp.int32(16))
    mixed = mixed * HASH_A
    mixed = mixed ^ lax.shift_right_logical(mixed, jnp.int32(15))
    mixed = mixed * HASH_B
    mixed = mixed ^ lax.shift_right_logical(mixed, jnp.int32(16))
    return (mixed & 65535).astype(F32) * (1.0 / 32767.5) - 1.0


def local_kernel(dims, first, field, mask, local, materials, stiffness, anisotropy, *refs):
    if first:
        thermal, stream, counter, heff, noise, masked = refs
        group = lax.axis_index("depth")
        block = lax.axis_index("plane")
        within = (
            lax.broadcasted_iota(jnp.int32, dims.tile, 0) * LANES
            + lax.broadcasted_iota(jnp.int32, dims.tile, 1)
        ) * HASH_A
        seed = stream[0] * HASH_B + counter[0] * HASH_C
    else:
        noise, heff, masked = refs
    lane = lax.broadcasted_iota(jnp.int32, dims.tile, 1)
    rows = range(dims.rows)

    def load(c, l, r):
        if first:
            return field[cells(dims, c, l, r), :]
        return field[c, l, r]

    for c in range(3):
        for r in rows:
            masked[c, 0, r] = jnp.zeros(dims.tile, F32)
            masked[c, dims.layers + 1, r] = jnp.zeros(dims.tile, F32)

    def fill(l, carry):
        for r in rows:
            mask_row = mask_tile(dims, mask, r)
            for c in range(3):
                masked[c, l + 1, r] = load(c, l, r) * mask_row
        return carry

    lax.fori_loop(0, dims.layers, fill, 0)

    def body(l, carry):
        material = materials[l]
        stiff = stiffness[material]
        aniso = anisotropy[material]
        for c in range(3):
            w = [masked[c, l + 1, r] for r in rows]
            for r in rows:
                total = shifted_sum(dims, w[r], lane)
                for step, weight in ((1, NEAR), (2, FAR)):
                    inside = [w[q] for q in (r - step, r + step) if 0 <= q < dims.rows]
                    if inside:
                        total += weight * functools.reduce(jnp.add, inside)
                total += 0.5 * (masked[c, l, r] + masked[c, l + 2, r])
                h = stiff * total + 0.5 * local[c, l, r]
                if c == 2:
                    h += aniso * load(c, l, r)
                if first:
                    layer = group * dims.layers + l
                    line = (c * (dims.depth * dims.layers) + layer) * (
                        dims.plane * dims.rows
                    ) + (block * dims.rows + r)
                    start = line * dims.width * HASH_A + seed
                    value = thermal[material] * hash_uniform(within + start)
                    noise[c, l, r] = value
                    h += value
                else:
                    h += noise[c, l, r]
                heff[c, l, r] = h
        return carry

    lax.fori_loop(0, dims.layers, body, 0)


def finish_kernel(
    dims,
    first,
    field,
    mask,
    heff,
    own,
    response,
    materials,
    stiffness,
    damping,
    before,
    after,
    *refs,
):
    others, refs = refs[: dims.depth - 1], refs[dims.depth - 1 :]
    if first:
        middle, base, low, high, bound, edge = refs
    else:
        base, local, result, accum, bound, edge = refs
    group = lax.axis_index("depth")
    total = dims.layers * dims.depth
    rows = range(dims.rows)

    def load(c, l, r):
        if first:
            return field[cells(dims, c, l, r), :]
        return field[c, l, r]

    def carry_y(g):
        return lambda i, j: response[j, 3 * (total + g) + i]

    def first_y(g):
        return lambda i, j: response[j, 3 * g * dims.layers + i]

    def first_s(g):
        return lambda i, j: response[3 + j, 3 * g * dims.layers + i]

    for g in range(dims.depth):

        @pl.when(group == g)
        def _():
            def message(h):
                return own if h == g else others[(g - h) % dims.depth - 1]

            for r in rows:
                end = [
                    [message(h)[c, r] for c in range(3)] for h in range(dims.depth - 1)
                ]
                ys = {0: None}
                for h in range(1, dims.depth):
                    ys[h] = end[h - 1]
                    if ys[h - 1] is not None:
                        ys[h] = add(ys[h], matvec(carry_y(h - 1), ys[h - 1]))
                s = None
                for h in range(dims.depth - 1, g, -1):
                    value = [message(h)[3 + c, r] for c in range(3)]
                    value = add(value, matvec(first_y(h), ys[h]))
                    if s is not None:
                        value = add(value, matvec(first_s(h), s))
                    s = value
                for c in range(3):
                    zero = jnp.zeros(dims.tile, F32)
                    bound[c, r] = zero if ys[g] is None else ys[g][c]
                    bound[3 + c, r] = zero if s is None else s[c]
                    edge[c, r] = zero if g == 0 else others[0][6 + c, r]
                    at = 9 if dims.depth == 2 else 6
                    top = others[dims.depth - 2]
                    edge[3 + c, r] = zero if g == dims.depth - 1 else top[at + c, r]

    def body(l, carry):
        material = materials[l]
        stiff = stiffness[material]
        alpha = damping[material]
        layer = group * dims.layers + l
        scale = 1.0 / (1.0 + jnp.full(dims.tile, alpha, F32) * alpha)
        down = jnp.where(l == 0, 0.5 * stiff, 0.0)
        up = jnp.where(l == dims.layers - 1, 0.5 * stiff, 0.0)
        for r in rows:
            v = [load(c, l, r) for c in range(3)]
            h = [heff[c, l, r] for c in range(3)]
            y = [bound[c, r] for c in range(3)]
            s = [bound[3 + c, r] for c in range(3)]
            fix = add(
                matvec(lambda i, j: response[j, 3 * layer + i], y),
                matvec(lambda i, j: response[3 + j, 3 * layer + i], s),
            )
            for c in range(3):
                for step, weight in ((1, NEAR), (2, FAR)):
                    if r - step < 0:
                        h[c] += (stiff * weight) * before[c, l, r - step + HALO]
                    if r + step >= dims.rows:
                        h[c] += (stiff * weight) * after[c, l, r + step - dims.rows]
                h[c] += down * edge[c, r] + up * edge[3 + c, r] + 0.5 * fix[c]
            torque = cross(v, h)
            twice = cross(v, torque)
            mask_row = mask_tile(dims, mask, r)
            gain = scale * mask_row
            rate = [(torque[c] + alpha * twice[c]) * gain for c in range(3)]
            if first:
                m1 = unit([v[c] - 0.03 * rate[c] for c in range(3)])
                for c in range(3):
                    middle[c, l, r] = m1[c]
                    base[c, l, r] = v[c] - 0.015 * rate[c]
                    if r < HALO:
                        low[c, l, r] = m1[c] * mask_row
                    if r >= dims.rows - HALO:
                        high[c, l, r - dims.rows + HALO] = m1[c] * mask_row
            else:
                new = unit([base[c, l, r] - 0.015 * rate[c] for c in range(3)])
                for c in range(3):
                    result[cells(dims, c, l, r), :] = new[c]
                    accum[cells(dims, c, l, r), :] = local[c, l, r] + fix[c]
        return carry

    lax.fori_loop(0, dims.layers, body, 0)


def call(kernel, outs, ins, args, scratch=(), flops=1000000):
    return pl.pallas_call(
        kernel,
        out_shape=outs,
        in_specs=[smem() if i else vmem() for i in ins],
        out_specs=[vmem()] * len(outs),
        scratch_shapes=scratch,
        compiler_params=pltpu.CompilerParams(vmem_limit_bytes=VMEM_LIMIT),
        cost_estimate=pl.CostEstimate(flops=flops, bytes_accessed=1000000, transcendentals=0),
    )(*args)


def ring(count, step):
    return [(i, (i + step) % count) for i in range(count)]


def local(
    magnet,
    mask,
    materials,
    exchange_strength,
    anisotropy,
    damping,
    source_strength,
    thermal_strength,
    pivots,
    lower,
    upper,
    noise_stream,
    counter,
):
    dims = Dims(
        magnet.shape[1],
        magnet.shape[2],
        magnet.shape[3],
        lax.axis_size("depth"),
        lax.axis_size("plane"),
    )
    lines = (3, dims.layers, dims.rows, dims.chunks, LANES)
    view = magnet.reshape(lines).transpose(0, 1, 3, 2, 4).reshape(-1, LANES)
    mask_view = mask.reshape(lines[2:]).transpose(1, 0, 2).reshape(-1, LANES)
    halo = shape(3, dims.layers, HALO, *dims.tile)
    field = shape(*dims.field())
    table = -(-3 * dims.depth * (dims.layers + 1) // LANES) * LANES
    pivots, lower, upper = (block.transpose(1, 2, 0) for block in (pivots, lower, upper))

    def bind(kernel, *static):
        return functools.partial(kernel, dims, *static)

    def swap_plane(low, high):
        after = lax.ppermute(low, "plane", ring(dims.plane, -1))
        before = lax.ppermute(high, "plane", ring(dims.plane, 1))
        return before, after

    messages = []
    for k in range(1, dims.depth):
        parts = 6 + 3 * (k == 1) + 3 * (k == dims.depth - 1)
        messages.append(shape(parts, dims.rows, *dims.tile))

    def swap_depth(sent):
        return [
            lax.ppermute(message, "depth", ring(dims.depth, k)) for k, message in enumerate(sent, 1)
        ]

    def sweep(natural, values):
        out = call(
            bind(sweep_kernel, natural),
            messages + [field],
            [0, 0, 1, 1, 1, 1, 1],
            (values, mask_view, materials, source_strength, pivots, lower, upper),
        )
        return out[:-1], out[-1]

    padded = pltpu.VMEM((3, dims.layers + 2, dims.rows) + dims.tile, F32)
    bounds = [pltpu.VMEM((6, dims.rows) + dims.tile, F32)] * 2

    low, high = call(bind(edges_kernel), [halo, halo], [0, 0], (view, mask_view))
    before, after = swap_plane(low, high)
    sent, solved = sweep(True, view)
    others = swap_depth(sent)
    (response,) = call(
        bind(response_kernel),
        [shape(8, table)],
        [1, 1, 1],
        (pivots, lower, upper),
        [pltpu.VMEM((table, LANES), F32)],
    )
    heff, noise = call(
        bind(local_kernel, True),
        [field, field],
        [0, 0, 0, 1, 1, 1, 1, 1, 1],
        (
            view,
            mask_view,
            solved,
            materials,
            exchange_strength,
            anisotropy,
            thermal_strength,
            noise_stream,
            counter,
        ),
        [padded],
    )
    kinds = [0, 0, 0, 0, 1, 1, 1, 1] + [0] * (1 + dims.depth)
    middle, base, low, high = call(
        bind(finish_kernel, True),
        [field, field, halo, halo],
        kinds,
        (
            view,
            mask_view,
            heff,
            sent[0],
            response,
            materials,
            exchange_strength,
            damping,
            before,
            after,
            *others,
        ),
        bounds,
    )
    before, after = swap_plane(low, high)
    sent, solved = sweep(False, middle)
    others = swap_depth(sent)
    (heff,) = call(
        bind(local_kernel, False),
        [field],
        [0, 0, 0, 1, 1, 1, 0],
        (middle, mask_view, solved, materials, exchange_strength, anisotropy, noise),
        [padded],
    )
    lined = shape(*view.shape)
    result, accum = call(
        bind(finish_kernel, False),
        [lined, lined],
        kinds + [0, 0],
        (
            middle,
            mask_view,
            heff,
            sent[0],
            response,
            materials,
            exchange_strength,
            damping,
            before,
            after,
            *others,
            base,
            solved,
        ),
        bounds,
    )

    def whole(lines_view):
        cut = lines_view.reshape(3, dims.layers, dims.chunks, dims.rows, LANES)
        return cut.transpose(0, 1, 3, 2, 4).reshape(magnet.shape)

    return whole(result), whole(accum)


def solution(mesh):
    placed = (
        P(None, "depth", "plane", None),
        P("plane", None),
        P("depth"),
    ) + (P(),) * 10
    return jax.shard_map(
        local,
        mesh=mesh,
        in_specs=placed,
        out_specs=(P(None, "depth", "plane", None), P(None, "depth", "plane", None)),
        check_vma=False,
    )
```

```python
import functools

import jax
import jax.numpy as jnp
from jax import lax
from jax.experimental import pallas as pl
from jax.experimental.pallas import tpu as pltpu
from jax.sharding import PartitionSpec as P

LANES = 128
NEAR = 4.0 / 3.0
FAR = -1.0 / 12.0
HALO = 2
VMEM_LIMIT = 16 * 1024 * 1024
UNROLL = 4
F32 = jnp.float32


def wrapped(value):
    value &= 0xFFFFFFFF
    return value - (1 << 32) if value >= (1 << 31) else value


HASH_A = wrapped(739982445)
HASH_B = wrapped(695872825)
HASH_C = wrapped(1597334677)


class Dims:
    def __init__(self, layers, rows, width, depth, plane):
        self.layers = layers
        self.rows = rows
        self.width = width
        self.chunks = width // LANES
        self.depth = depth
        self.plane = plane
        self.tile = (self.chunks, LANES)

    def field(self):
        return (3, self.layers, self.rows) + self.tile


def shape(*dims):
    return jax.ShapeDtypeStruct(dims, F32)


def vmem():
    return pl.BlockSpec(memory_space=pltpu.VMEM)


def hbm():
    return pl.BlockSpec(memory_space=pltpu.HBM)


def pick(parts, comp, layer, row):
    rows = parts[0].shape[2]
    return parts[row // rows][comp, layer, row % rows]


def cells(dims, comp, layer, row):
    base = (comp * dims.layers + layer) * (dims.chunks * dims.rows) + row
    return pl.ds(base, dims.chunks, stride=dims.rows)


def matvec(get, vec):
    return [get(i, 0) * vec[0] + get(i, 1) * vec[1] + get(i, 2) * vec[2] for i in range(3)]


def add(a, b):
    return [x + y for x, y in zip(a, b)]


def cross(a, b):
    return [
        a[1] * b[2] - a[2] * b[1],
        a[2] * b[0] - a[0] * b[2],
        a[0] * b[1] - a[1] * b[0],
    ]


def unit(vec):
    scale = lax.rsqrt(vec[0] * vec[0] + vec[1] * vec[1] + vec[2] * vec[2])
    return [v * scale for v in vec]


PIVOT_SOURCE, PIVOT_LOWER, UPPER, FROM_Y, FROM_S, LAYER_COEFS = 0, 9, 18, 27, 36, 45
LAST_Y, FIRST_Y, FIRST_S, GROUP_COEFS = 0, 9, 18, 27
STIFF, ANISO, DAMP, THERMAL, SCALE, LAYER_VALUES = 0, 1, 2, 3, 4, 5


def table(ref, at, first):
    return lambda i, j: ref[at, first + 3 * i + j]


def sweep_back(dims, local, upper, rows):
    def backward(l, after):
        done = []
        for r in rows:
            up = matvec(upper(l), after[r])
            s = [local[c, l, r] - up[c] for c in range(3)]
            for c in range(3):
                local[c, l, r] = s[c]
            done.append(s)
        return done

    zero = [[jnp.zeros(dims.tile, F32)] * 3 for _ in rows]
    return loop(dims.layers, lambda k, after: backward(dims.layers - 1 - k, after), zero)


def loop(count, body, start):
    step = max(k for k in range(1, UNROLL + 1) if count % k == 0)

    def steps(k, carry):
        for i in range(step):
            carry = body(k * step + i, carry)
        return carry

    if step == count:
        return steps(0, start)
    return lax.fori_loop(0, count // step, steps, start)


def message_parts(dims, k):
    last, first = (k == 1) * 3, (k == dims.depth - 1) * 3
    return [range(0, 6)] + [range(6, 9)] * (last > 0) + [range(9, 12)] * (first > 0)


def fetch(inputs, held, sems):
    copies = [
        pltpu.make_async_copy(src, dst, sems.at[k])
        for k, (src, dst) in enumerate(zip(inputs, held))
    ]
    for copy in copies:
        copy.start()
    for copy in copies:
        copy.wait()


def enter_kernel(dims, *refs):
    inputs, refs = refs[:7], refs[7:]
    field, maskf, low, high, local, *messages = refs[: 4 + dims.depth]
    *held, sems = refs[4 + dims.depth :]
    magnet, mask, materials, source, pivots, lower, upper = held
    fetch(inputs, held, sems)
    group = lax.axis_index("depth")
    rows = range(dims.rows)
    for r in rows:
        maskf[r] = mask[pl.ds(r, dims.chunks, stride=dims.rows), :].astype(F32)

    def block(ref, l):
        at = group * dims.layers + l
        return lambda i, j: ref[i, j, at]

    def forward(l, prev):
        beta = source[materials[l]]
        done = []
        for r in rows:
            v = [magnet[cells(dims, c, l, r), :] for c in range(3)]
            mask_row = maskf[r]
            for c in range(3):
                field[c, l, r] = v[c]
                if r < HALO:
                    low[c, l, r] = v[c] * mask_row
                if r >= dims.rows - HALO:
                    high[c, l, r - dims.rows + HALO] = v[c] * mask_row
            drop = matvec(block(lower, l), prev[r])
            y = matvec(block(pivots, l), [beta * v[c] - drop[c] for c in range(3)])
            for c in range(3):
                local[c, l, r] = y[c]
            done.append(y)
        return done

    zero = [[jnp.zeros(dims.tile, F32)] * 3 for _ in rows]
    last = loop(dims.layers, forward, zero)
    first = sweep_back(dims, local, lambda l: block(upper, l), rows)
    for r in rows:
        values = [last[r][c] for c in range(3)] + [first[r][c] for c in range(3)]
        for l in (dims.layers - 1, 0):
            values += [field[c, l, r] * maskf[r] for c in range(3)]
        for k, message in enumerate(messages, 1):
            at = 0
            for part in message_parts(dims, k):
                for p in part:
                    message[at, r] = values[p]
                    at += 1


def coefficient_kernel(dims, *refs):
    inputs, refs = refs[:9], refs[9:]
    coefs, groups, values, trail = refs[:4]
    fetch(inputs, refs[4:13], refs[13])
    materials, stiffness, anisotropy, damping, source, thermal, pivots, lower, upper = refs[4:13]
    group = lax.axis_index("depth")
    lane = lax.broadcasted_iota(jnp.int32, dims.tile, 1)
    every = range(dims.depth)

    def splat(value):
        return jnp.full(dims.tile, value, F32)

    def column(value, j):
        return jnp.broadcast_to(value[:, j : j + 1], dims.tile)

    def forward(k, ys):
        done = []
        for g in every:
            l = g * dims.layers + k
            low = matvec(lambda i, j: lower[i, j, l], ys[g])
            y = matvec(lambda i, j: pivots[i, j, l], [-a for a in low])
            for c in range(3):
                trail[g, k, c] = y[c]
            done.append(y)
        return done

    def backward(k, after):
        done = []
        for g in every:
            at = dims.layers - 1 - k
            l = g * dims.layers + at
            up = matvec(lambda i, j: upper[i, j, l], after[g])
            s = [trail[g, at, c] - up[c] for c in range(3)]
            for c in range(3):
                trail[g, at, c] = s[c]
            done.append(s)
        return done

    start = [[(lane == c).astype(F32) for c in range(3)] for _ in every]
    last = lax.fori_loop(0, dims.layers, forward, start)
    start = [[(lane == 3 + c).astype(F32) for c in range(3)] for _ in every]
    first = lax.fori_loop(0, dims.layers, backward, start)
    for g in every:
        for i in range(3):
            for j in range(3):
                groups[g, LAST_Y + 3 * i + j] = column(last[g][i], j)
                groups[g, FIRST_Y + 3 * i + j] = column(first[g][i], j)
                groups[g, FIRST_S + 3 * i + j] = column(first[g][i], 3 + j)

    def layer(l, carry):
        at = group * dims.layers + l
        material = materials[l]
        alpha = splat(damping[material])
        values[l, STIFF] = splat(stiffness[material])
        values[l, ANISO] = splat(anisotropy[material])
        values[l, DAMP] = alpha
        values[l, THERMAL] = splat(thermal[material])
        values[l, SCALE] = 1.0 / (1.0 + alpha * alpha)
        beta = splat(source[material])
        pivot = [[splat(pivots[i, j, at]) for j in range(3)] for i in range(3)]
        low = [[splat(lower[i, j, at]) for j in range(3)] for i in range(3)]
        for i in range(3):
            for j in range(3):
                coefs[l, PIVOT_SOURCE + 3 * i + j] = pivot[i][j] * beta
                coefs[l, PIVOT_LOWER + 3 * i + j] = (
                    pivot[i][0] * low[0][j] + pivot[i][1] * low[1][j] + pivot[i][2] * low[2][j]
                )
                coefs[l, UPPER + 3 * i + j] = splat(upper[i, j, at])
                coefs[l, FROM_Y + 3 * i + j] = column(trail[group, l, i], j)
                coefs[l, FROM_S + 3 * i + j] = column(trail[group, l, i], 3 + j)
        return carry

    lax.fori_loop(0, dims.layers, layer, 0)


def shifted_sum(dims, w, lane):
    after = pltpu.roll(w, dims.chunks - 1, 0)
    before = pltpu.roll(w, 1, 0)
    near = pltpu.roll(jnp.where(lane < 1, after, w), LANES - 1, 1)
    near += pltpu.roll(jnp.where(lane >= LANES - 1, before, w), 1, 1)
    far = pltpu.roll(jnp.where(lane < 2, after, w), LANES - 2, 1)
    far += pltpu.roll(jnp.where(lane >= LANES - 2, before, w), 2, 1)
    return NEAR * near + FAR * far


def hash_uniform(mixed):
    mixed = mixed ^ lax.shift_right_logical(mixed, jnp.int32(16))
    mixed = mixed * HASH_A
    mixed = mixed ^ lax.shift_right_logical(mixed, jnp.int32(15))
    mixed = mixed * HASH_B
    mixed = mixed ^ lax.shift_right_logical(mixed, jnp.int32(16))
    return (mixed & 65535).astype(F32) * (1.0 / 32767.5) - 1.0


def local_kernel(dims, first, parts, *refs):
    fields, refs = refs[:parts], refs[parts:]
    solved, refs = refs[:parts], refs[parts:]
    maskf, values = refs[:2]
    if first:
        seed, heff, noise, masked = refs[2:]
        group = lax.axis_index("depth")
        place = lax.axis_index("plane")
        within = (
            lax.broadcasted_iota(jnp.int32, dims.tile, 0) * LANES
            + lax.broadcasted_iota(jnp.int32, dims.tile, 1)
        ) * HASH_A + seed[...]
    else:
        noise, heff, masked = refs[2:]
    lane = lax.broadcasted_iota(jnp.int32, dims.tile, 1)
    rows = range(dims.rows)

    for c in range(3):
        for r in rows:
            masked[c, 0, r] = jnp.zeros(dims.tile, F32)
            masked[c, dims.layers + 1, r] = jnp.zeros(dims.tile, F32)

    def fill(l, carry):
        for r in rows:
            mask_row = maskf[r]
            for c in range(3):
                masked[c, l + 1, r] = pick(fields, c, l, r) * mask_row
        return carry

    lax.fori_loop(0, dims.layers, fill, 0)

    def body(l, carry):
        stiff = values[l, STIFF]
        aniso = values[l, ANISO]
        for c in range(3):
            w = [masked[c, l + 1, r] for r in rows]
            for r in rows:
                total = shifted_sum(dims, w[r], lane)
                for step, weight in ((1, NEAR), (2, FAR)):
                    inside = [w[q] for q in (r - step, r + step) if 0 <= q < dims.rows]
                    if inside:
                        total += weight * functools.reduce(jnp.add, inside)
                total += 0.5 * (masked[c, l, r] + masked[c, l + 2, r])
                h = stiff * total + 0.5 * pick(solved, c, l, r)
                if c == 2:
                    h += aniso * pick(fields, c, l, r)
                if first:
                    layer = group * dims.layers + l
                    line = (c * (dims.depth * dims.layers) + layer) * (
                        dims.plane * dims.rows
                    ) + (place * dims.rows + r)
                    value = values[l, THERMAL] * hash_uniform(within + line * dims.width * HASH_A)
                    noise[c, l, r] = value
                    h += value
                else:
                    h += noise[c, l, r]
                heff[c, l, r] = h
        return carry

    lax.fori_loop(0, dims.layers, body, 0)


def true_bounds(dims, groups, own, others, rows, start, bound, edge):
    group = lax.axis_index("depth")
    for g in range(dims.depth):

        @pl.when(group == g)
        def _():
            def message(h):
                return own if h == g else others[(g - h) % dims.depth - 1]

            for r in rows:
                at = start + r
                ys = {}
                for h in range(1, dims.depth):
                    ys[h] = [message(h - 1)[c, at] for c in range(3)]
                    if h > 1:
                        ys[h] = add(ys[h], matvec(table(groups, h - 1, LAST_Y), ys[h - 1]))
                s = None
                for h in range(dims.depth - 1, g, -1):
                    value = [message(h)[3 + c, at] for c in range(3)]
                    value = add(value, matvec(table(groups, h, FIRST_Y), ys[h]))
                    if s is not None:
                        value = add(value, matvec(table(groups, h, FIRST_S), s))
                    s = value
                zero = jnp.zeros(dims.tile, F32)
                above = 9 if dims.depth == 2 else 6
                for c in range(3):
                    bound[c, r] = zero if g == 0 else ys[g][c]
                    bound[3 + c, r] = zero if s is None else s[c]
                    edge[c, r] = zero if g == 0 else others[0][6 + c, at]
                    edge[3 + c, r] = (
                        zero if g == dims.depth - 1 else others[dims.depth - 2][above + c, at]
                    )


def finish_kernel(dims, first, upper_half, parts, *refs):
    field, refs = refs[:parts], refs[parts:]
    maskf, heff, halo, own, *refs = refs
    others, refs = refs[: dims.depth - 1], refs[dims.depth - 1 :]
    coefs, groups, values, *refs = refs
    count = dims.rows // 2
    start = count if upper_half else 0
    rows = range(count)
    if first and upper_half:
        mate, middle, base, local, out_halo, *messages, bound, edge = refs
    elif first:
        middle, base, local, out_halo, ends, bound, edge = refs
    elif upper_half:
        base, local, result, accum, bound, edge = refs
    else:
        base, local, *mates, result_out, accum_out, bound, edge, result, accum, sems = refs
        pairs = ((result, result_out), (accum, accum_out))
    true_bounds(dims, groups, own, others, rows, start, bound, edge)

    def body(l, prev):
        stiff = values[l, STIFF]
        near, far = stiff * NEAR, stiff * FAR
        alpha = values[l, DAMP]
        scale = values[l, SCALE]
        down = jnp.where(l == 0, 0.5, 0.0) * stiff
        up = jnp.where(l == dims.layers - 1, 0.5, 0.0) * stiff
        done = []
        for r in rows:
            at = start + r
            v = [pick(field, c, l, at) for c in range(3)]
            h = [heff[c, l, at] for c in range(3)]
            y = [bound[c, r] for c in range(3)]
            s = [bound[3 + c, r] for c in range(3)]
            fix = add(matvec(table(coefs, l, FROM_Y), y), matvec(table(coefs, l, FROM_S), s))
            for c in range(3):
                for step, weight in ((1, near), (2, far)):
                    if at - step < 0:
                        h[c] += weight * halo[c, l, at - step + HALO]
                    if at + step >= dims.rows:
                        h[c] += weight * halo[c, l, at + step - dims.rows]
                h[c] += down * edge[c, r] + up * edge[3 + c, r] + 0.5 * fix[c]
            torque = cross(v, h)
            twice = cross(v, torque)
            mask_row = maskf[at]
            gain = scale * mask_row
            rate = [(torque[c] + alpha * twice[c]) * gain for c in range(3)]
            if first:
                m1 = unit([v[c] - 0.03 * rate[c] for c in range(3)])
                edge_row = at - (dims.rows - HALO) if upper_half else at
                for c in range(3):
                    middle[c, l, r] = m1[c]
                    base[c, l, r] = v[c] - 0.015 * rate[c]
                    if 0 <= edge_row < HALO:
                        out_halo[c, l, edge_row] = m1[c] * mask_row
                y = matvec(table(coefs, l, PIVOT_SOURCE), m1)
                drop = matvec(table(coefs, l, PIVOT_LOWER), prev[r])
                y = [a - b for a, b in zip(y, drop)]
                for c in range(3):
                    local[c, l, r] = y[c]
                done.append(y)
            else:
                new = unit([base[c, l, r] - 0.015 * rate[c] for c in range(3)])
                for c in range(3):
                    spin = local[c, l, r] + fix[c]
                    if upper_half:
                        result[c, l, r] = new[c]
                        accum[c, l, r] = spin
                    else:
                        result[cells(dims, c, l, r), :] = new[c]
                        accum[cells(dims, c, l, r), :] = spin
                        result[cells(dims, c, l, r + count), :] = mates[0][c, l, r]
                        accum[cells(dims, c, l, r + count), :] = mates[1][c, l, r]
        if not first and not upper_half:
            for k, (src, dst) in enumerate(pairs):
                for c in range(3):
                    lines = dims.chunks * dims.rows
                    where = pl.ds((c * dims.layers + l) * lines, lines)
                    pltpu.make_async_copy(src.at[where], dst.at[where], sems.at[k]).start()
        return done

    if not first:
        loop(dims.layers, lambda l, carry: (body(l, None), carry)[1], 0)
        if not upper_half:
            for k, (src, dst) in enumerate(pairs):
                pltpu.make_async_copy(src, dst, sems.at[k]).wait()
        return
    zero = [[jnp.zeros(dims.tile, F32)] * 3 for _ in rows]
    last = loop(dims.layers, body, zero)
    head = sweep_back(dims, local, lambda l: table(coefs, l, UPPER), rows)
    for r in rows:
        sent = [last[r][c] for c in range(3)] + [head[r][c] for c in range(3)]
        for l in (dims.layers - 1, 0):
            sent += [middle[c, l, r] * maskf[start + r] for c in range(3)]
        if not upper_half:
            for p in range(12):
                ends[p, r] = sent[p]
            continue
        for k, message in enumerate(messages, 1):
            at = 0
            for part in message_parts(dims, k):
                for p in part:
                    message[at, r] = mate[p, r]
                    message[at, start + r] = sent[p]
                    at += 1


def call(kernel, outs, args, scratch=(), ins=vmem, results=vmem):
    return pl.pallas_call(
        kernel,
        out_shape=outs,
        in_specs=[ins()] * len(args),
        out_specs=[results()] * len(outs),
        scratch_shapes=list(scratch),
        compiler_params=pltpu.CompilerParams(vmem_limit_bytes=VMEM_LIMIT),
        cost_estimate=pl.CostEstimate(flops=1000000, bytes_accessed=1000000, transcendentals=0),
    )(*args)


def ring(count, step):
    return [(i, (i + step) % count) for i in range(count)]


def local(
    magnet,
    mask,
    materials,
    exchange_strength,
    anisotropy,
    damping,
    source_strength,
    thermal_strength,
    pivots,
    lower,
    upper,
    noise_stream,
    counter,
):
    dims = Dims(
        magnet.shape[1],
        magnet.shape[2],
        magnet.shape[3],
        lax.axis_size("depth"),
        lax.axis_size("plane"),
    )
    lines = (3, dims.layers, dims.rows, dims.chunks, LANES)
    view = magnet.reshape(lines).transpose(0, 1, 3, 2, 4).reshape(-1, LANES)
    mask_view = mask.reshape(lines[2:]).transpose(1, 0, 2).reshape(-1, LANES)
    halo = shape(3, dims.layers, HALO, *dims.tile)
    field = shape(*dims.field())
    half = shape(3, dims.layers, dims.rows // 2, *dims.tile)
    blocks = [values.transpose(1, 2, 0) for values in (pivots, lower, upper)]
    bounds = [pltpu.VMEM((6, dims.rows // 2) + dims.tile, F32)] * 2
    padded = [pltpu.VMEM((3, dims.layers + 2, dims.rows) + dims.tile, F32)]
    messages = [
        shape(sum(len(part) for part in message_parts(dims, k)), dims.rows, *dims.tile)
        for k in range(1, dims.depth)
    ]

    def forward(values):
        return lax.ppermute(values, "plane", ring(dims.plane, 1))

    def backward(values):
        return lax.ppermute(values, "plane", ring(dims.plane, -1))

    def swap_depth(sent):
        return [
            lax.ppermute(message, "depth", ring(dims.depth, k)) for k, message in enumerate(sent, 1)
        ]

    def local_field(first, fields, solved, extra, outs):
        kernel = functools.partial(local_kernel, dims, first, len(fields))
        return call(kernel, outs, (*fields, *solved, maskf, values, *extra), padded)

    def finish(first, upper_half, fields, heff, rows, own, others, extra, outs, *rest):
        kernel = functools.partial(finish_kernel, dims, first, upper_half, len(fields))
        args = (*fields, maskf, heff, rows, own, *others, coefs, groups, values, *extra)
        return call(kernel, outs, args, bounds + list(rest[:1] and rest[0]), *rest[1:])

    inputs = (view, mask_view, materials, source_strength, *blocks)
    seed = jnp.full(dims.tile, noise_stream[0] * HASH_B + counter[0] * HASH_C, jnp.int32)
    constants = (
        materials,
        exchange_strength,
        anisotropy,
        damping,
        source_strength,
        thermal_strength,
        *blocks,
    )
    inputs = [pltpu.with_memory_space_constraint(x, pltpu.HBM) for x in inputs]
    constants = [pltpu.with_memory_space_constraint(x, pltpu.HBM) for x in constants]
    spaces = [pltpu.VMEM] * 2 + [pltpu.SMEM] * 5
    held = [space(x.shape, x.dtype) for space, x in zip(spaces, inputs)]
    tiles, maskf, low, high, solved, *sent = call(
        functools.partial(enter_kernel, dims),
        [
            field,
            shape(dims.rows, *dims.tile),
            halo,
            halo,
            field,
        ]
        + messages,
        inputs,
        held + [pltpu.SemaphoreType.DMA((len(inputs),))],
        hbm,
    )
    before = forward(high)
    others = swap_depth(sent)
    after = backward(low)
    coefs, groups, values = call(
        functools.partial(coefficient_kernel, dims),
        [
            shape(dims.layers, LAYER_COEFS, *dims.tile),
            shape(dims.depth, GROUP_COEFS, *dims.tile),
            shape(dims.layers, LAYER_VALUES, *dims.tile),
        ],
        constants,
        [pltpu.VMEM((dims.depth, dims.layers, 3) + dims.tile, F32)]
        + [pltpu.SMEM(x.shape, x.dtype) for x in constants]
        + [pltpu.SemaphoreType.DMA((len(constants),))],
        hbm,
    )
    heff, noise = local_field(True, [tiles], [solved], (seed,), [field, field])
    middle_low, base_low, solved_low, low, ends = finish(
        True,
        False,
        [tiles],
        heff,
        before,
        sent[0],
        others,
        (),
        [half, half, half, halo, shape(12, dims.rows // 2, *dims.tile)],
    )
    next_after = backward(low)
    middle_high, base_high, solved_high, high, *sent2 = finish(
        True,
        True,
        [tiles],
        heff,
        after,
        sent[0],
        others,
        (ends,),
        [half, half, half, halo] + messages,
    )
    next_before = forward(high)
    others2 = swap_depth(sent2)
    middle = [middle_low, middle_high]
    (heff2,) = local_field(False, middle, [solved_low, solved_high], (noise,), [field])
    new_high = finish(
        False,
        True,
        middle,
        heff2,
        next_after,
        sent2[0],
        others2,
        (base_high, solved_high),
        [half, half],
    )
    lined = shape(*view.shape)
    result, accum = finish(
        False,
        False,
        middle,
        heff2,
        next_before,
        sent2[0],
        others2,
        (base_low, solved_low, *new_high),
        [lined, lined],
        [pltpu.VMEM(view.shape, F32)] * 2 + [pltpu.SemaphoreType.DMA((2,))],
        vmem,
        hbm,
    )

    def whole(lines_view):
        cut = lines_view.reshape(3, dims.layers, dims.chunks, dims.rows, LANES)
        return cut.transpose(0, 1, 3, 2, 4).reshape(magnet.shape)

    return whole(result), whole(accum)


def solution(mesh):
    placed = (
        P(None, "depth", "plane", None),
        P("plane", None),
        P("depth"),
    ) + (P(),) * 10
    return jax.shard_map(
        local,
        mesh=mesh,
        in_specs=placed,
        out_specs=(P(None, "depth", "plane", None), P(None, "depth", "plane", None)),
        check_vma=False,
    )
```

```python
import functools

import jax
import jax.numpy as jnp
from jax import lax
from jax.experimental import pallas as pl
from jax.experimental.pallas import tpu as pltpu
from jax.sharding import PartitionSpec as P

LANES = 128
NEAR = 4.0 / 3.0
FAR = -1.0 / 12.0
HALO = 2
VMEM_LIMIT = 16 * 1024 * 1024
UNROLL = 4
F32 = jnp.float32


def wrapped(value):
    value &= 0xFFFFFFFF
    return value - (1 << 32) if value >= (1 << 31) else value


HASH_A = wrapped(739982445)
HASH_B = wrapped(695872825)
HASH_C = wrapped(1597334677)


class Dims:
    def __init__(self, layers, rows, width, depth, plane):
        self.layers = layers
        self.rows = rows
        self.width = width
        self.chunks = width // LANES
        self.depth = depth
        self.plane = plane
        self.tile = (self.chunks, LANES)

    def field(self):
        return (3, self.layers, self.rows) + self.tile


def shape(*dims):
    return jax.ShapeDtypeStruct(dims, F32)


def vmem():
    return pl.BlockSpec(memory_space=pltpu.VMEM)


def hbm():
    return pl.BlockSpec(memory_space=pltpu.HBM)


def turned(dims, position):
    odd = lax.axis_index("plane") % 2 == 1
    return jnp.where(odd, dims.rows - 1 - position, position)


def cells(dims, comp, layer, row):
    base = (comp * dims.layers + layer) * (dims.chunks * dims.rows) + row
    return pl.ds(base, dims.chunks, stride=dims.rows)


def matvec(get, vec):
    return [get(i, 0) * vec[0] + get(i, 1) * vec[1] + get(i, 2) * vec[2] for i in range(3)]


def add(a, b):
    return [x + y for x, y in zip(a, b)]


def cross(a, b):
    return [
        a[1] * b[2] - a[2] * b[1],
        a[2] * b[0] - a[0] * b[2],
        a[0] * b[1] - a[1] * b[0],
    ]


def unit(vec):
    scale = lax.rsqrt(vec[0] * vec[0] + vec[1] * vec[1] + vec[2] * vec[2])
    return [v * scale for v in vec]


PIVOT, LOWER, UPPER, BLOCK_COEFS = 0, 9, 18, 27
PIVOT_SOURCE, PIVOT_LOWER, FROM_Y, FROM_S, LAYER_COEFS = 0, 9, 18, 27, 36
STIFF, ANISO, DAMP, THERMAL, SCALE, SOURCE, LAYER_VALUES = 0, 1, 2, 3, 4, 5, 6
LAST, FIRST, TOP, BOTTOM, PARTS = 0, 3, 6, 9, 12
LAST_Y, FIRST_Y, FIRST_S, THROUGH, ECHO, LINKS = 0, 9, 18, 27, 36, 45
SECOND = 8
GROUPS = 4


def table(ref, at, first):
    return lambda i, j: ref[at, first + 3 * i + j]


def column(value, j):
    return jnp.broadcast_to(value[:, j : j + 1], value.shape)


def columns(values, first):
    return [[column(values[i], first + j) for j in range(3)] for i in range(3)]


def entries(matrix):
    return lambda i, j: matrix[i][j]


def entries_by_column(matrix):
    return lambda i, j: matrix[j][i]


def sweep_back(dims, lines, upper, start):
    def backward(k, after):
        l = dims.layers - 1 - k
        done = []
        for (ref, r), s in zip(lines, after):
            up = matvec(upper(l), s)
            s = [ref[c, l, r] - up[c] for c in range(3)]
            for c in range(3):
                ref[c, l, r] = s[c]
            done.append(s)
        return done

    return loop(dims.layers, backward, start)


def loop(count, body, start):
    step = max(k for k in range(1, UNROLL + 1) if count % k == 0)

    def steps(k, carry):
        for i in range(step):
            carry = body(k * step + i, carry)
        return carry

    if step == count:
        return steps(0, start)
    return lax.fori_loop(0, count // step, steps, start)


def fetch(inputs, held, sems):
    copies = [
        pltpu.make_async_copy(src, dst, sems.at[k])
        for k, (src, dst) in enumerate(zip(inputs, held))
    ]
    for copy in copies:
        copy.start()
    for copy in copies:
        copy.wait()


def enter_kernel(dims, *refs):
    inputs, refs = refs[:11], refs[11:]
    field, maskf, near, blocks, values, *held, sems = refs
    fetch(inputs, held, sems)
    magnet, mask, materials, stiffness, anisotropy, damping, source, thermal, *matrices = held
    group = lax.axis_index("depth")
    rows = range(dims.rows)
    lines = [turned(dims, r) for r in rows]
    for r in rows:
        maskf[r] = mask[pl.ds(lines[r], dims.chunks, stride=dims.rows), :].astype(F32)

    def layer(l, carry):
        for r in rows:
            mask_row = maskf[r]
            for c in range(3):
                v = magnet[cells(dims, c, l, lines[r]), :]
                field[c, l, r] = v
                if r >= dims.rows - HALO:
                    near[c, l, dims.rows - 1 - r] = v * mask_row
        at = group * dims.layers + l
        material = materials[l]
        for k, ref in enumerate(matrices):
            for i in range(3):
                for j in range(3):
                    blocks[l, 9 * k + 3 * i + j] = jnp.full(dims.tile, ref[i, j, at], F32)
        alpha = jnp.full(dims.tile, damping[material], F32)
        values[l, DAMP] = alpha
        values[l, SCALE] = 1.0 / (1.0 + alpha * alpha)
        rest = ((STIFF, stiffness), (ANISO, anisotropy), (THERMAL, thermal), (SOURCE, source))
        for k, ref in rest:
            values[l, k] = jnp.full(dims.tile, ref[material], F32)
        return carry

    loop(dims.layers, layer, 0)


def sweep_kernel(dims, field, maskf, blocks, values, local, trail, message, far):
    rows = range(dims.rows)

    def forward(l, prev):
        beta = values[l, SOURCE]
        done = []
        for r in [*rows, None]:
            drop = matvec(table(blocks, l, LOWER), prev[len(done)])
            f = [-a for a in drop] if r is None else [beta * field[c, l, r] - drop[c] for c in range(3)]
            y = matvec(table(blocks, l, PIVOT), f)
            for c in range(3):
                if r is None:
                    trail[c, l, 0] = y[c]
                else:
                    local[c, l, r] = y[c]
                    if r < HALO:
                        far[c, l, r] = field[c, l, r] * maskf[r]
            done.append(y)
        return done

    zero = [[jnp.zeros(dims.tile, F32)] * 3 for _ in rows]
    lane = lax.broadcasted_iota(jnp.int32, dims.tile, 1)
    before, after = [[(lane == first + c).astype(F32) for c in range(3)] for first in (0, 3)]
    last = loop(dims.layers, forward, zero + [before])
    lines = [(local, r) for r in rows] + [(trail, 0)]
    first = sweep_back(dims, lines, lambda l: table(blocks, l, UPPER), zero + [after])
    for c in range(3):
        message[PARTS * dims.rows + LAST + c] = last[-1][c]
        message[PARTS * dims.rows + FIRST + c] = first[-1][c]
    for r in rows:
        sent = [last[r][c] for c in range(3)] + [first[r][c] for c in range(3)]
        for l in (dims.layers - 1, 0):
            sent += [field[c, l, r] * maskf[r] for c in range(3)]
        for p in range(PARTS):
            message[p * dims.rows + r] = sent[p]


def coefficient_kernel(dims, trail, blocks, values, coefs):
    def layer(l, carry):
        pivot, low = table(blocks, l, PIVOT), table(blocks, l, LOWER)
        beta = values[l, SOURCE]
        for i in range(3):
            for j in range(3):
                coefs[l, PIVOT_SOURCE + 3 * i + j] = pivot(i, j) * beta
                coefs[l, PIVOT_LOWER + 3 * i + j] = (
                    pivot(i, 0) * low(0, j) + pivot(i, 1) * low(1, j) + pivot(i, 2) * low(2, j)
                )
                coefs[l, FROM_Y + 3 * i + j] = column(trail[i, l, 0], j)
                coefs[l, FROM_S + 3 * i + j] = column(trail[i, l, 0], 3 + j)
        return carry

    loop(dims.layers, layer, 0)


def for_each_group(body):
    group = lax.axis_index("depth")
    for g in range(GROUPS):

        @pl.when(group == g)
        def _():
            body(g)


def getter(dims, ref):
    return lambda part, r: [ref[(part + c) * dims.rows + r] for c in range(3)]


def getter(dims, ref):
    return lambda part, r: [ref[(part + c) * dims.rows + r] for c in range(3)]


def spread(dims, ref):
    base = PARTS * dims.rows
    return lambda part: [ref[base + part + c] for c in range(3)]


def cross_kernel(dims, own, mate, out):
    def body(g):
        even, odd = (own, mate) if g % 2 == 0 else (mate, own)
        get_even, get_odd = getter(dims, even), getter(dims, odd)
        if g < 2:
            odd_y = entries(columns(spread(dims, odd)(LAST), 0))
        else:
            odd_first = entries(columns(spread(dims, odd)(FIRST), 0))
            even_s = entries(columns(spread(dims, even)(FIRST), 3))
        for r in range(dims.rows):
            if g < 2:
                value = add(get_odd(LAST, r), matvec(odd_y, get_even(LAST, r)))
                side = get_odd(TOP, r)
            else:
                value = add(get_odd(FIRST, r), matvec(odd_first, get_even(LAST, r)))
                value = add(get_even(FIRST, r), matvec(even_s, value))
                side = get_even(BOTTOM, r)
            for c in range(3):
                out[c * dims.rows + r] = value[c]
                out[(3 + c) * dims.rows + r] = side[c]
        lane = lax.broadcasted_iota(jnp.int32, dims.tile, 1)
        for part in (LAST, FIRST):
            pair = zip(spread(dims, even)(part), spread(dims, odd)(part))
            for c, (a, b) in enumerate(pair):
                both = jnp.where(lane < SECOND, a, pltpu.roll(b, SECOND, 1))
                out[6 * dims.rows + part + c] = both

    for_each_group(body)


def first_bound_kernel(dims, own, mate, cross, other, links, bound, edge):
    def body(g):
        base = 6 * dims.rows
        even, odd = (own, mate) if g % 2 == 0 else (mate, own)
        for pair, ref in enumerate((cross, other) if g < 2 else (other, cross)):
            for h in range(2):
                values = [[ref[base + part + c] for c in range(3)] for part in (LAST, FIRST)]
                matrices = (
                    (LAST_Y, columns(values[0], SECOND * h)),
                    (FIRST_Y, columns(values[1], SECOND * h)),
                    (FIRST_S, columns(values[1], SECOND * h + 3)),
                )
                for at, matrix in matrices:
                    for i in range(3):
                        for j in range(3):
                            links[2 * pair + h, at + 3 * i + j] = matrix[i][j]
        for h in range(GROUPS - 1, -1, -1):
            every = [[table(links, h, at)(i, j) for j in range(3) for i in range(3)] for at in (LAST_Y, FIRST_Y, FIRST_S)]
            last_y, through, first_s = [[m[3 * j : 3 * j + 3] for j in range(3)] for m in every]
            if h < GROUPS - 1:
                ahead = table(links, h + 1, THROUGH)
                echo = [matvec(entries_by_column(first_s), [ahead(i, j) for i in range(3)]) for j in range(3)]
                for j in range(3):
                    through[j] = add(through[j], matvec(entries_by_column(echo), last_y[j]))
                    for i in range(3):
                        links[h, ECHO + 3 * i + j] = echo[j][i]
            else:
                for k in range(9):
                    links[h, ECHO + k] = jnp.zeros(dims.tile, F32)
            for j in range(3):
                for i in range(3):
                    links[h, THROUGH + 3 * i + j] = through[j][i]
        get_even, get_odd = getter(dims, even), getter(dims, odd)
        get_cross, get_other, get_mate = (getter(dims, ref) for ref in (cross, other, mate))
        zero = [jnp.zeros(dims.tile, F32)] * 3
        first = 0 if g < 2 else 2
        for r in range(dims.rows):
            if g < 2:
                s = matvec(table(links, 2, LAST_Y), get_cross(0, r))
                s = matvec(table(links, 2, FIRST_S), matvec(table(links, 3, FIRST_Y), s))
                s = add(s, matvec(table(links, 2, FIRST_Y), get_cross(0, r)))
                s = add(s, get_other(0, r))
                if g == 0:
                    y = zero
                    s = matvec(table(links, 1, FIRST_S), s)
                    s = add(s, matvec(table(links, 1, FIRST_Y), get_even(LAST, r)))
                    s = add(s, get_odd(FIRST, r))
                else:
                    y = get_even(LAST, r)
            else:
                y = get_other(0, r)
                after = add(get_even(LAST, r), matvec(table(links, 2, LAST_Y), y))
                if g == 2:
                    s = add(get_odd(FIRST, r), matvec(table(links, 3, FIRST_Y), after))
                else:
                    y, s = after, zero
            if g % 2 == 0:
                down = zero if g == 0 else get_other(3, r)
                up = get_mate(BOTTOM, r)
            else:
                down = get_mate(TOP, r)
                up = zero if g == GROUPS - 1 else get_other(3, r)
            for c in range(3):
                bound[c, r] = y[c]
                bound[3 + c, r] = s[c]
                edge[c, r] = down[c]
                edge[3 + c, r] = up[c]

    for_each_group(body)


def beside_part(k):
    return [*range(TOP, TOP + 3)] * (k == 1) + [*range(BOTTOM, PARTS)] * (k == GROUPS - 1)


def bound_kernel(dims, links, own, *refs):
    others, (bound, edge) = refs[: GROUPS - 1], refs[GROUPS - 1 :]

    def body(g):
        got = [getter(dims, own if h == g else others[(g - h) % GROUPS - 1]) for h in range(GROUPS)]
        zero = [jnp.zeros(dims.tile, F32)] * 3
        for r in range(dims.rows):
            y = zero
            for h in range(g):
                value = got[h](0, r)
                y = value if h == 0 else add(value, matvec(table(links, h, LAST_Y), y))
            s = zero
            if g < GROUPS - 1:
                s = got[g](LAST, r)
                if g:
                    s = add(s, matvec(table(links, g, LAST_Y), y))
                s = matvec(table(links, g + 1, THROUGH), s)
                after = got[GROUPS - 1](0, r)
                for h in range(GROUPS - 2, g, -1):
                    after = add(got[h](0, r), matvec(table(links, h, FIRST_S), after))
                s = add(s, after)
            down = zero if g == 0 else got[g - 1](3, r)
            up = zero if g == GROUPS - 1 else got[g + 1](3, r)
            for c in range(3):
                bound[c, r] = y[c]
                bound[3 + c, r] = s[c]
                edge[c, r] = down[c]
                edge[3 + c, r] = up[c]

    for_each_group(body)


def absorb_kernel(dims, heff, bound, edge, coefs, values, *refs):
    if len(refs) == 1:
        (out,) = refs
    else:
        local, out, accum_out, accum, sem = refs

    def body(l, carry):
        stiff = values[l, STIFF]
        down = jnp.where(l == 0, 0.5, 0.0) * stiff
        up = jnp.where(l == dims.layers - 1, 0.5, 0.0) * stiff
        for r in range(dims.rows):
            y = [bound[c, r] for c in range(3)]
            s = [bound[3 + c, r] for c in range(3)]
            fix = add(matvec(table(coefs, l, FROM_Y), y), matvec(table(coefs, l, FROM_S), s))
            for c in range(3):
                sides = down * edge[c, r] + up * edge[3 + c, r]
                out[c, l, r] = heff[c, l, r] + 0.5 * fix[c] + sides
                if len(refs) > 1:
                    accum[cells(dims, c, l, turned(dims, r)), :] = local[c, l, r] + fix[c]
        if len(refs) > 1:
            send_lines(dims, l, accum, accum_out, sem.at[0])
        return carry

    loop(dims.layers, body, 0)
    if len(refs) > 1:
        pltpu.make_async_copy(accum, accum_out, sem.at[0]).wait()


def send_lines(dims, layer, src, dst, sem):
    lines = dims.chunks * dims.rows
    for c in range(3):
        where = pl.ds((c * dims.layers + layer) * lines, lines)
        pltpu.make_async_copy(src.at[where], dst.at[where], sem).start()


def shifted_sum(dims, w, lane):
    after = pltpu.roll(w, dims.chunks - 1, 0)
    before = pltpu.roll(w, 1, 0)
    near = pltpu.roll(jnp.where(lane < 1, after, w), LANES - 1, 1)
    near += pltpu.roll(jnp.where(lane >= LANES - 1, before, w), 1, 1)
    far = pltpu.roll(jnp.where(lane < 2, after, w), LANES - 2, 1)
    far += pltpu.roll(jnp.where(lane >= LANES - 2, before, w), 2, 1)
    return NEAR * near + FAR * far


def hash_uniform(mixed):
    mixed = mixed ^ lax.shift_right_logical(mixed, jnp.int32(16))
    mixed = mixed * HASH_A
    mixed = mixed ^ lax.shift_right_logical(mixed, jnp.int32(15))
    mixed = mixed * HASH_B
    mixed = mixed ^ lax.shift_right_logical(mixed, jnp.int32(16))
    return (mixed & 65535).astype(F32) * (1.0 / 32767.5) - 1.0


def local_kernel(dims, first, *refs):
    field, solved, maskf, values, *refs = refs
    if first:
        seed, heff, noise, masked = refs
        group = lax.axis_index("depth")
        place = lax.axis_index("plane")
        within = (
            lax.broadcasted_iota(jnp.int32, dims.tile, 0) * LANES
            + lax.broadcasted_iota(jnp.int32, dims.tile, 1)
        ) * HASH_A + seed[...]
    else:
        noise, heff, masked = refs
    lane = lax.broadcasted_iota(jnp.int32, dims.tile, 1)
    rows = range(dims.rows)

    for c in range(3):
        for r in rows:
            masked[c, 0, r] = jnp.zeros(dims.tile, F32)
            masked[c, dims.layers + 1, r] = jnp.zeros(dims.tile, F32)

    def fill(l, carry):
        for r in rows:
            mask_row = maskf[r]
            for c in range(3):
                masked[c, l + 1, r] = field[c, l, r] * mask_row
        return carry

    lax.fori_loop(0, dims.layers, fill, 0)

    def body(l, carry):
        stiff = values[l, STIFF]
        aniso = values[l, ANISO]
        for c in range(3):
            w = [masked[c, l + 1, r] for r in rows]
            for r in rows:
                total = shifted_sum(dims, w[r], lane)
                for step, weight in ((1, NEAR), (2, FAR)):
                    inside = [w[q] for q in (r - step, r + step) if 0 <= q < dims.rows]
                    if inside:
                        total += weight * functools.reduce(jnp.add, inside)
                total += 0.5 * (masked[c, l, r] + masked[c, l + 2, r])
                h = stiff * total + 0.5 * solved[c, l, r]
                if c == 2:
                    h += aniso * field[c, l, r]
                if first:
                    layer = group * dims.layers + l
                    line = (c * (dims.depth * dims.layers) + layer) * (
                        dims.plane * dims.rows
                    ) + (place * dims.rows + turned(dims, r))
                    value = values[l, THERMAL] * hash_uniform(within + line * dims.width * HASH_A)
                    noise[c, l, r] = value
                    h += value
                else:
                    h += noise[c, l, r]
                heff[c, l, r] = h
        return carry

    lax.fori_loop(0, dims.layers, body, 0)


def finish_kernel(dims, first, start, stop, closing, *refs):
    rows = range(start, stop)
    ends = [(start == 0, 0), (stop == dims.rows, dims.rows - 1)]
    halos, refs = refs[: sum(there for there, _ in ends)], refs[sum(there for there, _ in ends) :]
    halos = list(zip([position for there, position in ends if there], halos))
    field, maskf, heff, coefs, blocks, values, *refs = refs
    last_call = not first and closing
    mate_rows = range(start) if start else range(stop, dims.rows)
    offset = mate_rows[0]
    if first and closing:
        links, mate_middle, mate_base, mate_local, mate_ends, middle, base, local, out_halo, own, *messages = refs
    elif first:
        middle, base, local, out_halo, ends = refs
    elif not last_call:
        base, result = refs
    else:
        base, mate, result_out, result, sem = refs

    def at(r):
        return r if closing else r - start

    def body(l, prev):
        stiff = values[l, STIFF]
        weights = (stiff * NEAR, stiff * FAR)
        alpha = values[l, DAMP]
        scale = values[l, SCALE]
        done = []
        for r in rows:
            v = [field[c, l, r] for c in range(3)]
            h = [heff[c, l, r] for c in range(3)]
            for c in range(3):
                for position, halo in halos:
                    for step in (1, 2):
                        beyond = step - 1 - abs(r - position)
                        if beyond >= 0:
                            h[c] += weights[step - 1] * halo[c, l, beyond]
            torque = cross(v, h)
            twice = cross(v, torque)
            mask_row = maskf[r]
            gain = scale * mask_row
            rate = [(torque[c] + alpha * twice[c]) * gain for c in range(3)]
            if first:
                m1 = unit([v[c] - 0.03 * rate[c] for c in range(3)])
                edge_row = dims.rows - 1 - r if start else r
                for c in range(3):
                    middle[c, l, at(r)] = m1[c]
                    base[c, l, at(r)] = v[c] - 0.015 * rate[c]
                    if edge_row < HALO:
                        out_halo[c, l, edge_row] = m1[c] * mask_row
                y = matvec(table(coefs, l, PIVOT_SOURCE), m1)
                drop = matvec(table(coefs, l, PIVOT_LOWER), prev[r - start])
                y = [a - b for a, b in zip(y, drop)]
                for c in range(3):
                    local[c, l, at(r)] = y[c]
                done.append(y)
                continue
            new = unit([base[c, l, r] - 0.015 * rate[c] for c in range(3)])
            for c in range(3):
                if last_call:
                    result[cells(dims, c, l, turned(dims, r)), :] = new[c]
                else:
                    result[c, l, r - start] = new[c]
        if last_call:
            for c in range(3):
                for r in mate_rows:
                    result[cells(dims, c, l, turned(dims, r)), :] = mate[c, l, r - offset]
            send_lines(dims, l, result, result_out, sem.at[0])
        return done

    if not first:
        loop(dims.layers, lambda l, carry: (body(l, None), carry)[1], 0)
        if last_call:
            pltpu.make_async_copy(result, result_out, sem.at[0]).wait()
        return

    def put(r, sent):
        group = lax.axis_index("depth")
        echo = matvec(table(links, group, ECHO), sent[LAST : LAST + 3])
        down = add(sent[FIRST : FIRST + 3], echo)
        for k, message in enumerate(messages, 1):
            value = [jnp.where(group + k < GROUPS, a, b) for a, b in zip(sent[LAST : LAST + 3], down)]
            value += [sent[p] for p in beside_part(k)]
            for place, tile in enumerate(value):
                message[place * dims.rows + r] = tile
        for c in range(3):
            own[c * dims.rows + r] = sent[LAST + c]

    zero = [[jnp.zeros(dims.tile, F32)] * 3 for _ in rows]
    last = loop(dims.layers, body, zero)
    lines = [(local, at(r)) for r in rows]
    head = sweep_back(dims, lines, lambda l: table(blocks, l, UPPER), zero)
    for r in rows:
        sent = [last[r - start][c] for c in range(3)] + [head[r - start][c] for c in range(3)]
        for l in (dims.layers - 1, 0):
            sent += [middle[c, l, at(r)] * maskf[r] for c in range(3)]
        if closing:
            put(r, sent)
        else:
            for p in range(PARTS):
                ends[p, at(r)] = sent[p]
    if not closing:
        return
    for r in mate_rows:
        put(r, [mate_ends[p, r - offset] for p in range(PARTS)])

    def merge(l, carry):
        for r in mate_rows:
            for c in range(3):
                middle[c, l, r] = mate_middle[c, l, r - offset]
                base[c, l, r] = mate_base[c, l, r - offset]
                local[c, l, r] = mate_local[c, l, r - offset]
        return carry

    lax.fori_loop(0, dims.layers, merge, 0)


def call(kernel, outs, args, scratch=(), ins=None, results=None):
    return pl.pallas_call(
        kernel,
        out_shape=outs,
        in_specs=ins or [vmem()] * len(args),
        out_specs=results or [vmem()] * len(outs),
        scratch_shapes=list(scratch),
        compiler_params=pltpu.CompilerParams(vmem_limit_bytes=VMEM_LIMIT),
        cost_estimate=pl.CostEstimate(flops=1000000, bytes_accessed=1000000, transcendentals=0),
    )(*args)


def ring(count, step):
    return [(i, (i + step) % count) for i in range(count)]


def local(
    magnet,
    mask,
    materials,
    exchange_strength,
    anisotropy,
    damping,
    source_strength,
    thermal_strength,
    pivots,
    lower,
    upper,
    noise_stream,
    counter,
):
    dims = Dims(
        magnet.shape[1],
        magnet.shape[2],
        magnet.shape[3],
        lax.axis_size("depth"),
        lax.axis_size("plane"),
    )
    lines = (3, dims.layers, dims.rows, dims.chunks, LANES)
    view = magnet.reshape(lines).transpose(0, 1, 3, 2, 4).reshape(-1, LANES)
    mask_view = mask.reshape(lines[2:]).transpose(1, 0, 2).reshape(-1, LANES)
    halo = shape(3, dims.layers, HALO, *dims.tile)
    field = shape(*dims.field())
    padded = [pltpu.VMEM((3, dims.layers + 2, dims.rows) + dims.tile, F32)]
    assert dims.depth == GROUPS
    message = PARTS * dims.rows
    edges = shape(6, dims.rows, *dims.tile)

    def across(values):
        pairs = [(i, (i + 1 if i % 2 else i - 1) % dims.plane) for i in range(dims.plane)]
        return lax.ppermute(values, "plane", pairs)

    def beside(values):
        return lax.ppermute(values, "plane", [(i, i ^ 1) for i in range(dims.plane)])

    def exchange(values, step):
        return lax.ppermute(values, "depth", [(i, i ^ step) for i in range(dims.depth)])

    def finish(first, start, stop, closing, halos, fields, heff, extra, outs, *rest):
        kernel = functools.partial(finish_kernel, dims, first, start, stop, closing)
        return call(kernel, outs, (*halos, fields, maskf, heff, coefs, blocks, values, *extra), *rest)

    seed = jnp.full(dims.tile, noise_stream[0] * HASH_B + counter[0] * HASH_C, jnp.int32)
    inputs = (
        view,
        mask_view,
        materials,
        exchange_strength,
        anisotropy,
        damping,
        source_strength,
        thermal_strength,
        pivots.transpose(1, 2, 0),
        lower.transpose(1, 2, 0),
        upper.transpose(1, 2, 0),
    )
    inputs = [pltpu.with_memory_space_constraint(x, pltpu.HBM) for x in inputs]
    spaces = [pltpu.VMEM] * 2 + [pltpu.SMEM] * 9
    held = [space(x.shape, x.dtype) for space, x in zip(spaces, inputs)]
    tiles, maskf, near, blocks, values = call(
        functools.partial(enter_kernel, dims),
        [
            field,
            shape(dims.rows, *dims.tile),
            halo,
            shape(dims.layers, BLOCK_COEFS, *dims.tile),
            shape(dims.layers, LAYER_VALUES, *dims.tile),
        ],
        inputs,
        held + [pltpu.SemaphoreType.DMA((len(inputs),))],
        [hbm()] * len(inputs),
    )
    near_halo = beside(near)
    solved, trail, sent, far = call(
        functools.partial(sweep_kernel, dims),
        [field, shape(3, dims.layers, 1, *dims.tile), shape(message + 6, *dims.tile), halo],
        (tiles, maskf, blocks, values),
    )
    mate = exchange(sent, 1)
    far_halo = across(far)
    (cross,) = call(
        functools.partial(cross_kernel, dims),
        [shape(6 * dims.rows + 6, *dims.tile)],
        (sent, mate),
    )
    other = exchange(cross, 2)
    (coefs,) = call(
        functools.partial(coefficient_kernel, dims),
        [shape(dims.layers, LAYER_COEFS, *dims.tile)],
        (trail, blocks, values),
    )
    links, *bounds = call(
        functools.partial(first_bound_kernel, dims),
        [shape(GROUPS, LINKS, *dims.tile), edges, edges],
        (sent, mate, cross, other),
    )
    heff, noise = call(
        functools.partial(local_kernel, dims, True),
        [field, field],
        (tiles, solved, maskf, values, seed),
        padded,
    )
    inner = dims.rows // 2
    part = shape(3, dims.layers, dims.rows - inner, *dims.tile)
    (heff,) = call(
        functools.partial(absorb_kernel, dims), [field], (heff, *bounds, coefs, values)
    )
    *near_half, near, ends = finish(
        True,
        inner,
        dims.rows,
        False,
        [near_halo],
        tiles,
        heff,
        (),
        [part, part, part, halo, shape(PARTS, dims.rows - inner, *dims.tile)],
    )
    near_halo = beside(near)
    middle, base, solved, far, own, *sent = finish(
        True,
        0,
        inner,
        True,
        [far_halo],
        tiles,
        heff,
        (links, *near_half, ends),
        [field, field, field, halo, shape(3 * dims.rows, *dims.tile)]
        + [shape((3 + len(beside_part(k))) * dims.rows, *dims.tile) for k in range(1, GROUPS)],
    )
    far_halo = across(far)
    others = [
        lax.ppermute(values, "depth", [(i, (i + k) % GROUPS) for i in range(GROUPS)])
        for k, values in enumerate(sent, 1)
    ]
    bounds = call(
        functools.partial(bound_kernel, dims),
        [edges, edges],
        (links, own, *others),
    )
    (heff,) = call(
        functools.partial(local_kernel, dims, False),
        [field],
        (middle, solved, maskf, values, noise),
        padded,
    )
    lined = shape(*view.shape)
    staging = [pltpu.VMEM(view.shape, F32), pltpu.SemaphoreType.DMA((1,))]
    heff, accum = call(
        functools.partial(absorb_kernel, dims),
        [field, lined],
        (heff, *bounds, coefs, values, solved),
        staging,
        None,
        [vmem(), hbm()],
    )
    (near_result,) = finish(
        False, inner, dims.rows, False, [near_halo], middle, heff, (base,), [part]
    )
    (result,) = finish(
        False,
        0,
        inner,
        True,
        [far_halo],
        middle,
        heff,
        (base, near_result),
        [lined],
        staging,
        None,
        [hbm()],
    )

    def whole(lines_view):
        cut = lines_view.reshape(3, dims.layers, dims.chunks, dims.rows, LANES)
        return cut.transpose(0, 1, 3, 2, 4).reshape(magnet.shape)

    return whole(result), whole(accum)


def solution(mesh):
    placed = (
        P(None, "depth", "plane", None),
        P("plane", None),
        P("depth"),
    ) + (P(),) * 10
    return jax.shard_map(
        local,
        mesh=mesh,
        in_specs=placed,
        out_specs=(P(None, "depth", "plane", None), P(None, "depth", "plane", None)),
        check_vma=False,
    )
```

```python
import functools

import jax
import jax.numpy as jnp
from jax import lax
from jax.experimental import pallas as pl
from jax.experimental.pallas import tpu as pltpu
from jax.sharding import PartitionSpec as P

LANES = 128
NEAR = 4.0 / 3.0
FAR = -1.0 / 12.0
HALO = 2
VMEM_LIMIT = 16 * 1024 * 1024
UNROLL = 4
F32 = jnp.float32


def wrapped(value):
    value &= 0xFFFFFFFF
    return value - (1 << 32) if value >= (1 << 31) else value


HASH_A = wrapped(739982445)
HASH_B = wrapped(695872825)
HASH_C = wrapped(1597334677)


class Dims:
    def __init__(self, layers, rows, width, depth, plane):
        self.layers = layers
        self.rows = rows
        self.width = width
        self.chunks = width // LANES
        self.depth = depth
        self.plane = plane
        self.tile = (self.chunks, LANES)

    def field(self):
        return (3, self.layers, self.rows) + self.tile


def shape(*dims):
    return jax.ShapeDtypeStruct(dims, F32)


def vmem():
    return pl.BlockSpec(memory_space=pltpu.VMEM)


def hbm():
    return pl.BlockSpec(memory_space=pltpu.HBM)


def turned(dims, position):
    odd = lax.axis_index("plane") % 2 == 1
    return jnp.where(odd, dims.rows - 1 - position, position)


def cells(dims, comp, layer, row):
    base = (comp * dims.layers + layer) * (dims.chunks * dims.rows) + row
    return pl.ds(base, dims.chunks, stride=dims.rows)


def matvec(get, vec):
    return [get(i, 0) * vec[0] + get(i, 1) * vec[1] + get(i, 2) * vec[2] for i in range(3)]


def add(a, b):
    return [x + y for x, y in zip(a, b)]


def cross(a, b):
    return [
        a[1] * b[2] - a[2] * b[1],
        a[2] * b[0] - a[0] * b[2],
        a[0] * b[1] - a[1] * b[0],
    ]


def unit(vec):
    scale = lax.rsqrt(vec[0] * vec[0] + vec[1] * vec[1] + vec[2] * vec[2])
    return [v * scale for v in vec]


PIVOT, LOWER, UPPER, BLOCK_COEFS = 0, 9, 18, 27
PIVOT_SOURCE, PIVOT_LOWER, FROM_Y, FROM_S, LAYER_COEFS = 0, 9, 18, 27, 36
STIFF, ANISO, DAMP, THERMAL, SCALE, SOURCE, LAYER_VALUES = 0, 1, 2, 3, 4, 5, 6
LAST, FIRST, TOP, BOTTOM, PARTS = 0, 3, 6, 9, 12
LAST_Y, FIRST_Y, FIRST_S, LINKS = 0, 9, 18, 27
SECOND = 8
GROUPS = 4


def table(ref, at, first):
    return lambda i, j: ref[at, first + 3 * i + j]


def column(value, j):
    return jnp.broadcast_to(value[:, j : j + 1], value.shape)


def columns(values, first):
    return [[column(values[i], first + j) for j in range(3)] for i in range(3)]


def entries(matrix):
    return lambda i, j: matrix[i][j]


def sweep_back(dims, lines, upper, start):
    def backward(k, after):
        l = dims.layers - 1 - k
        done = []
        for (ref, r), s in zip(lines, after):
            up = matvec(upper(l), s)
            s = [ref[c, l, r] - up[c] for c in range(3)]
            for c in range(3):
                ref[c, l, r] = s[c]
            done.append(s)
        return done

    return loop(dims.layers, backward, start)


def loop(count, body, start):
    step = max(k for k in range(1, UNROLL + 1) if count % k == 0)

    def steps(k, carry):
        for i in range(step):
            carry = body(k * step + i, carry)
        return carry

    if step == count:
        return steps(0, start)
    return lax.fori_loop(0, count // step, steps, start)


def fetch(inputs, held, sems):
    copies = [
        pltpu.make_async_copy(src, dst, sems.at[k])
        for k, (src, dst) in enumerate(zip(inputs, held))
    ]
    for copy in copies:
        copy.start()
    for copy in copies:
        copy.wait()


def enter_kernel(dims, *refs):
    inputs, refs = refs[:11], refs[11:]
    field, maskf, near, blocks, values, *held, sems = refs
    fetch(inputs, held, sems)
    magnet, mask, materials, stiffness, anisotropy, damping, source, thermal, *matrices = held
    group = lax.axis_index("depth")
    rows = range(dims.rows)
    lines = [turned(dims, r) for r in rows]
    for r in rows:
        maskf[r] = mask[pl.ds(lines[r], dims.chunks, stride=dims.rows), :].astype(F32)

    def layer(l, carry):
        for r in rows:
            mask_row = maskf[r]
            for c in range(3):
                v = magnet[cells(dims, c, l, lines[r]), :]
                field[c, l, r] = v
                if r >= dims.rows - HALO:
                    near[c, l, dims.rows - 1 - r] = v * mask_row
        at = group * dims.layers + l
        material = materials[l]
        for k, ref in enumerate(matrices):
            for i in range(3):
                for j in range(3):
                    blocks[l, 9 * k + 3 * i + j] = jnp.full(dims.tile, ref[i, j, at], F32)
        alpha = jnp.full(dims.tile, damping[material], F32)
        values[l, DAMP] = alpha
        values[l, SCALE] = 1.0 / (1.0 + alpha * alpha)
        rest = ((STIFF, stiffness), (ANISO, anisotropy), (THERMAL, thermal), (SOURCE, source))
        for k, ref in rest:
            values[l, k] = jnp.full(dims.tile, ref[material], F32)
        return carry

    loop(dims.layers, layer, 0)


def sweep_kernel(dims, field, maskf, blocks, values, local, trail, message, far):
    rows = range(dims.rows)

    def forward(l, prev):
        beta = values[l, SOURCE]
        done = []
        for r in [*rows, None]:
            drop = matvec(table(blocks, l, LOWER), prev[len(done)])
            f = [-a for a in drop] if r is None else [beta * field[c, l, r] - drop[c] for c in range(3)]
            y = matvec(table(blocks, l, PIVOT), f)
            for c in range(3):
                if r is None:
                    trail[c, l, 0] = y[c]
                else:
                    local[c, l, r] = y[c]
                    if r < HALO:
                        far[c, l, r] = field[c, l, r] * maskf[r]
            done.append(y)
        return done

    zero = [[jnp.zeros(dims.tile, F32)] * 3 for _ in rows]
    lane = lax.broadcasted_iota(jnp.int32, dims.tile, 1)
    before, after = [[(lane == first + c).astype(F32) for c in range(3)] for first in (0, 3)]
    last = loop(dims.layers, forward, zero + [before])
    lines = [(local, r) for r in rows] + [(trail, 0)]
    first = sweep_back(dims, lines, lambda l: table(blocks, l, UPPER), zero + [after])
    for c in range(3):
        message[PARTS * dims.rows + LAST + c] = last[-1][c]
        message[PARTS * dims.rows + FIRST + c] = first[-1][c]
    for r in rows:
        sent = [last[r][c] for c in range(3)] + [first[r][c] for c in range(3)]
        for l in (dims.layers - 1, 0):
            sent += [field[c, l, r] * maskf[r] for c in range(3)]
        for p in range(PARTS):
            message[p * dims.rows + r] = sent[p]


def coefficient_kernel(dims, trail, blocks, values, coefs):
    def layer(l, carry):
        pivot, low = table(blocks, l, PIVOT), table(blocks, l, LOWER)
        beta = values[l, SOURCE]
        for i in range(3):
            for j in range(3):
                coefs[l, PIVOT_SOURCE + 3 * i + j] = pivot(i, j) * beta
                coefs[l, PIVOT_LOWER + 3 * i + j] = (
                    pivot(i, 0) * low(0, j) + pivot(i, 1) * low(1, j) + pivot(i, 2) * low(2, j)
                )
                coefs[l, FROM_Y + 3 * i + j] = column(trail[i, l, 0], j)
                coefs[l, FROM_S + 3 * i + j] = column(trail[i, l, 0], 3 + j)
        return carry

    loop(dims.layers, layer, 0)


def for_each_group(body):
    group = lax.axis_index("depth")
    for g in range(GROUPS):

        @pl.when(group == g)
        def _():
            body(g)


def getter(dims, ref):
    return lambda part, r: [ref[(part + c) * dims.rows + r] for c in range(3)]


def getter(dims, ref):
    return lambda part, r: [ref[(part + c) * dims.rows + r] for c in range(3)]


def spread(dims, ref):
    base = PARTS * dims.rows
    return lambda part: [ref[base + part + c] for c in range(3)]


def cross_kernel(dims, own, mate, *refs):
    links, out = refs if len(refs) == 2 else (None, refs[0])

    def body(g):
        even, odd = (own, mate) if g % 2 == 0 else (mate, own)
        get_even, get_odd = getter(dims, even), getter(dims, odd)
        if links is not None:
            odd_y, odd_first, even_s = (
                table(links, h, at) for h, at in ((1, LAST_Y), (3, FIRST_Y), (2, FIRST_S))
            )
        elif g < 2:
            odd_y = entries(columns(spread(dims, odd)(LAST), 0))
        else:
            odd_first = entries(columns(spread(dims, odd)(FIRST), 0))
            even_s = entries(columns(spread(dims, even)(FIRST), 3))
        for r in range(dims.rows):
            if g < 2:
                value = add(get_odd(LAST, r), matvec(odd_y, get_even(LAST, r)))
                side = get_odd(TOP, r)
            else:
                value = add(get_odd(FIRST, r), matvec(odd_first, get_even(LAST, r)))
                value = add(get_even(FIRST, r), matvec(even_s, value))
                side = get_even(BOTTOM, r)
            for c in range(3):
                out[c * dims.rows + r] = value[c]
                out[(3 + c) * dims.rows + r] = side[c]
        if links is not None:
            for tile in range(6 * dims.rows, out.shape[0]):
                out[tile] = jnp.zeros(dims.tile, F32)
            return
        lane = lax.broadcasted_iota(jnp.int32, dims.tile, 1)
        for part in (LAST, FIRST):
            pair = zip(spread(dims, even)(part), spread(dims, odd)(part))
            for c, (a, b) in enumerate(pair):
                both = jnp.where(lane < SECOND, a, pltpu.roll(b, SECOND, 1))
                out[6 * dims.rows + part + c] = both

    for_each_group(body)


def bound_kernel(dims, first, own, mate, cross, other, links, bound, edge):
    def body(g):
        base = 6 * dims.rows
        even, odd = (own, mate) if g % 2 == 0 else (mate, own)
        pairs = (cross, other) if g < 2 else (other, cross)
        for pair, ref in enumerate(pairs if first else ()):
            for h in range(2):
                values = [[ref[base + part + c] for c in range(3)] for part in (LAST, FIRST)]
                matrices = (
                    (LAST_Y, columns(values[0], SECOND * h)),
                    (FIRST_Y, columns(values[1], SECOND * h)),
                    (FIRST_S, columns(values[1], SECOND * h + 3)),
                )
                for at, matrix in matrices:
                    for i in range(3):
                        for j in range(3):
                            links[2 * pair + h, at + 3 * i + j] = matrix[i][j]
        get_even, get_odd = getter(dims, even), getter(dims, odd)
        get_cross, get_other, get_mate = (getter(dims, ref) for ref in (cross, other, mate))
        zero = [jnp.zeros(dims.tile, F32)] * 3
        for r in range(dims.rows):
            if g < 2:
                s = matvec(table(links, 2, LAST_Y), get_cross(0, r))
                s = matvec(table(links, 2, FIRST_S), matvec(table(links, 3, FIRST_Y), s))
                s = add(s, matvec(table(links, 2, FIRST_Y), get_cross(0, r)))
                s = add(s, get_other(0, r))
                if g == 0:
                    y = zero
                    s = matvec(table(links, 1, FIRST_S), s)
                    s = add(s, matvec(table(links, 1, FIRST_Y), get_even(LAST, r)))
                    s = add(s, get_odd(FIRST, r))
                else:
                    y = get_even(LAST, r)
            else:
                y = get_other(0, r)
                after = add(get_even(LAST, r), matvec(table(links, 2, LAST_Y), y))
                if g == 2:
                    s = add(get_odd(FIRST, r), matvec(table(links, 3, FIRST_Y), after))
                else:
                    y, s = after, zero
            if g % 2 == 0:
                down = zero if g == 0 else get_other(3, r)
                up = get_mate(BOTTOM, r)
            else:
                down = get_mate(TOP, r)
                up = zero if g == GROUPS - 1 else get_other(3, r)
            for c in range(3):
                bound[c, r] = y[c]
                bound[3 + c, r] = s[c]
                edge[c, r] = down[c]
                edge[3 + c, r] = up[c]

    for_each_group(body)


def absorb_kernel(dims, heff, bound, edge, coefs, values, *refs):
    if len(refs) == 1:
        (out,) = refs
    else:
        local, out, accum = refs

    def body(l, carry):
        stiff = values[l, STIFF]
        down = jnp.where(l == 0, 0.5, 0.0) * stiff
        up = jnp.where(l == dims.layers - 1, 0.5, 0.0) * stiff
        for r in range(dims.rows):
            y = [bound[c, r] for c in range(3)]
            s = [bound[3 + c, r] for c in range(3)]
            fix = add(matvec(table(coefs, l, FROM_Y), y), matvec(table(coefs, l, FROM_S), s))
            for c in range(3):
                sides = down * edge[c, r] + up * edge[3 + c, r]
                out[c, l, r] = heff[c, l, r] + 0.5 * fix[c] + sides
                if len(refs) > 1:
                    accum[cells(dims, c, l, turned(dims, r)), :] = local[c, l, r] + fix[c]
        return carry

    loop(dims.layers, body, 0)


def send_lines(dims, layer, src, dst, sem):
    lines = dims.chunks * dims.rows
    for c in range(3):
        where = pl.ds((c * dims.layers + layer) * lines, lines)
        pltpu.make_async_copy(src.at[where], dst.at[where], sem).start()


def shifted_sum(dims, w, lane):
    after = pltpu.roll(w, dims.chunks - 1, 0)
    before = pltpu.roll(w, 1, 0)
    near = pltpu.roll(jnp.where(lane < 1, after, w), LANES - 1, 1)
    near += pltpu.roll(jnp.where(lane >= LANES - 1, before, w), 1, 1)
    far = pltpu.roll(jnp.where(lane < 2, after, w), LANES - 2, 1)
    far += pltpu.roll(jnp.where(lane >= LANES - 2, before, w), 2, 1)
    return NEAR * near + FAR * far


def hash_uniform(mixed):
    mixed = mixed ^ lax.shift_right_logical(mixed, jnp.int32(16))
    mixed = mixed * HASH_A
    mixed = mixed ^ lax.shift_right_logical(mixed, jnp.int32(15))
    mixed = mixed * HASH_B
    mixed = mixed ^ lax.shift_right_logical(mixed, jnp.int32(16))
    return (mixed & 65535).astype(F32) * (1.0 / 32767.5) - 1.0


def local_kernel(dims, first, *refs):
    field, solved, maskf, values, *refs = refs
    if first:
        seed, heff, noise, masked = refs
        group = lax.axis_index("depth")
        place = lax.axis_index("plane")
        within = (
            lax.broadcasted_iota(jnp.int32, dims.tile, 0) * LANES
            + lax.broadcasted_iota(jnp.int32, dims.tile, 1)
        ) * HASH_A + seed[...]
    else:
        noise, heff, masked = refs
    lane = lax.broadcasted_iota(jnp.int32, dims.tile, 1)
    rows = range(dims.rows)

    for c in range(3):
        for r in rows:
            masked[c, 0, r] = jnp.zeros(dims.tile, F32)
            masked[c, dims.layers + 1, r] = jnp.zeros(dims.tile, F32)

    def fill(l, carry):
        for r in rows:
            mask_row = maskf[r]
            for c in range(3):
                masked[c, l + 1, r] = field[c, l, r] * mask_row
        return carry

    lax.fori_loop(0, dims.layers, fill, 0)

    def body(l, carry):
        stiff = values[l, STIFF]
        aniso = values[l, ANISO]
        for c in range(3):
            w = [masked[c, l + 1, r] for r in rows]
            for r in rows:
                total = shifted_sum(dims, w[r], lane)
                for step, weight in ((1, NEAR), (2, FAR)):
                    inside = [w[q] for q in (r - step, r + step) if 0 <= q < dims.rows]
                    if inside:
                        total += weight * functools.reduce(jnp.add, inside)
                total += 0.5 * (masked[c, l, r] + masked[c, l + 2, r])
                h = stiff * total + 0.5 * solved[c, l, r]
                if c == 2:
                    h += aniso * field[c, l, r]
                if first:
                    layer = group * dims.layers + l
                    line = (c * (dims.depth * dims.layers) + layer) * (
                        dims.plane * dims.rows
                    ) + (place * dims.rows + turned(dims, r))
                    value = values[l, THERMAL] * hash_uniform(within + line * dims.width * HASH_A)
                    noise[c, l, r] = value
                    h += value
                else:
                    h += noise[c, l, r]
                heff[c, l, r] = h
        return carry

    lax.fori_loop(0, dims.layers, body, 0)


def largest(m):
    x, y, z = [jnp.abs(v) for v in m]
    first = x >= jnp.maximum(y, z)
    return first, jnp.logical_and(jnp.logical_not(first), y >= z)


def tangent_parts(m, change):
    first, second = largest(m)
    last = jnp.logical_or(first, second)
    return [jnp.where(first, change[1], change[0]), jnp.where(last, change[2], change[1])]


def tangent_whole(m, parts):
    first, second = largest(m)
    last = jnp.logical_or(first, second)
    a, b = parts
    rest = a * jnp.where(first, m[1], m[0]) + b * jnp.where(last, m[2], m[1])
    along = jnp.where(first, m[0], jnp.where(second, m[1], m[2]))
    c = -rest / jnp.where(along == 0.0, 1.0, along)
    return [
        jnp.where(first, c, a),
        jnp.where(first, a, jnp.where(second, c, b)),
        jnp.where(last, b, c),
    ]


def middle_halo(l, start_halo, change_halo):
    lines = []
    for k in range(HALO):
        w = [start_halo[c, l, k] for c in range(3)]
        change = tangent_whole(w, [change_halo[c, l, k] for c in range(2)])
        m1 = [w[c] - 0.03 * change[c] for c in range(3)]
        square = m1[0] * m1[0] + m1[1] * m1[1] + m1[2] * m1[2]
        scale = lax.rsqrt(jnp.maximum(square, 1e-30))
        lines.append([v * scale for v in m1])
    return lines


def first_halo(l, halo):
    return [[halo[c, l, k] for c in range(3)] for k in range(HALO)]


def rate(dims, l, r, halos, field, maskf, heff, values):
    stiff = values[l, STIFF]
    v = [field[c, l, r] for c in range(3)]
    h = [heff[c, l, r] for c in range(3)]
    for step, weight in ((1, NEAR), (2, FAR)):
        for position, halo in halos:
            beyond = step - 1 - abs(r - position)
            if beyond >= 0:
                h = [h[c] + (stiff * weight) * halo[beyond][c] for c in range(3)]
    torque = cross(v, h)
    twice = cross(v, torque)
    gain = values[l, SCALE] * maskf[r]
    return v, [(torque[c] + values[l, DAMP] * twice[c]) * gain for c in range(3)]


def first_rate_kernel(dims, *refs):
    far_halo, near_halo, field, maskf, heff, coefs, blocks, values, *refs = refs
    middle, base, local, far, near, message = refs
    rows = range(dims.rows)

    def body(l, prev):
        halos = [(0, first_halo(l, far_halo)), (dims.rows - 1, first_halo(l, near_halo))]
        done = []
        for r in rows:
            v, change = rate(dims, l, r, halos, field, maskf, heff, values)
            m1 = unit([v[c] - 0.03 * change[c] for c in range(3)])
            for c in range(3):
                middle[c, l, r] = m1[c]
                base[c, l, r] = v[c] - 0.015 * change[c]
            for c, part in enumerate(tangent_parts(v, change)):
                if r < HALO:
                    far[c, l, r] = part
                if r >= dims.rows - HALO:
                    near[c, l, dims.rows - 1 - r] = part
            y = matvec(table(coefs, l, PIVOT_SOURCE), m1)
            drop = matvec(table(coefs, l, PIVOT_LOWER), prev[r])
            y = [a - b for a, b in zip(y, drop)]
            for c in range(3):
                local[c, l, r] = y[c]
            done.append(y)
        return done

    zero = [[jnp.zeros(dims.tile, F32)] * 3 for _ in rows]
    last = loop(dims.layers, body, zero)
    head = sweep_back(dims, [(local, r) for r in rows], lambda l: table(blocks, l, UPPER), zero)
    for r in rows:
        sent = last[r] + head[r]
        for l in (dims.layers - 1, 0):
            sent += [middle[c, l, r] * maskf[r] for c in range(3)]
        for p in range(PARTS):
            message[p * dims.rows + r] = sent[p]


def second_rate_kernel(
    dims, rows, position, start_halo, change_halo, field, maskf, heff, values, base, *refs
):
    if len(refs) == 1:
        (out,) = refs
    else:
        mate, accum, result_out, accum_out, result, sem = refs
        accum_copy = pltpu.make_async_copy(accum, accum_out, sem.at[1])
        accum_copy.start()
        rest = [r for r in range(dims.rows) if r not in rows]

    def body(l, carry):
        halos = [(position, middle_halo(l, start_halo, change_halo))]
        for r in rows:
            _, change = rate(dims, l, r, halos, field, maskf, heff, values)
            new = unit([base[c, l, r] - 0.015 * change[c] for c in range(3)])
            for c in range(3):
                if len(refs) == 1:
                    out[c, l, r - rows[0]] = new[c]
                else:
                    result[cells(dims, c, l, turned(dims, r)), :] = new[c]
        if len(refs) > 1:
            for c in range(3):
                for r in rest:
                    result[cells(dims, c, l, turned(dims, r)), :] = mate[c, l, r - rest[0]]
            send_lines(dims, l, result, result_out, sem.at[0])
        return carry

    loop(dims.layers, body, 0)
    if len(refs) > 1:
        pltpu.make_async_copy(result, result_out, sem.at[0]).wait()
        accum_copy.wait()


def call(kernel, outs, args, scratch=(), ins=None, results=None):
    return pl.pallas_call(
        kernel,
        out_shape=outs,
        in_specs=ins or [vmem()] * len(args),
        out_specs=results or [vmem()] * len(outs),
        scratch_shapes=list(scratch),
        compiler_params=pltpu.CompilerParams(vmem_limit_bytes=VMEM_LIMIT),
        cost_estimate=pl.CostEstimate(flops=1000000, bytes_accessed=1000000, transcendentals=0),
    )(*args)


def ring(count, step):
    return [(i, (i + step) % count) for i in range(count)]


def local(
    magnet,
    mask,
    materials,
    exchange_strength,
    anisotropy,
    damping,
    source_strength,
    thermal_strength,
    pivots,
    lower,
    upper,
    noise_stream,
    counter,
):
    dims = Dims(
        magnet.shape[1],
        magnet.shape[2],
        magnet.shape[3],
        lax.axis_size("depth"),
        lax.axis_size("plane"),
    )
    lines = (3, dims.layers, dims.rows, dims.chunks, LANES)
    view = magnet.reshape(lines).transpose(0, 1, 3, 2, 4).reshape(-1, LANES)
    mask_view = mask.reshape(lines[2:]).transpose(1, 0, 2).reshape(-1, LANES)
    halo = shape(3, dims.layers, HALO, *dims.tile)
    rates = shape(2, dims.layers, HALO, *dims.tile)
    field = shape(*dims.field())
    padded = [pltpu.VMEM((3, dims.layers + 2, dims.rows) + dims.tile, F32)]
    assert dims.depth == GROUPS
    message = PARTS * dims.rows
    edges = shape(6, dims.rows, *dims.tile)

    def across(values):
        pairs = [(i, (i + 1 if i % 2 else i - 1) % dims.plane) for i in range(dims.plane)]
        return lax.ppermute(values, "plane", pairs)

    def beside(values):
        return lax.ppermute(values, "plane", [(i, i ^ 1) for i in range(dims.plane)])

    def exchange(values, step):
        return lax.ppermute(values, "depth", [(i, i ^ step) for i in range(dims.depth)])

    def second_rate(rows, position, halos, extra, outs, *rest):
        kernel = functools.partial(second_rate_kernel, dims, rows, position)
        return call(kernel, outs, (*halos, middle, maskf, heff, values, base, *extra), *rest)

    seed = jnp.full(dims.tile, noise_stream[0] * HASH_B + counter[0] * HASH_C, jnp.int32)
    inputs = (
        view,
        mask_view,
        materials,
        exchange_strength,
        anisotropy,
        damping,
        source_strength,
        thermal_strength,
        pivots.transpose(1, 2, 0),
        lower.transpose(1, 2, 0),
        upper.transpose(1, 2, 0),
    )
    inputs = [pltpu.with_memory_space_constraint(x, pltpu.HBM) for x in inputs]
    spaces = [pltpu.VMEM] * 2 + [pltpu.SMEM] * 9
    held = [space(x.shape, x.dtype) for space, x in zip(spaces, inputs)]
    tiles, maskf, near, blocks, values = call(
        functools.partial(enter_kernel, dims),
        [
            field,
            shape(dims.rows, *dims.tile),
            halo,
            shape(dims.layers, BLOCK_COEFS, *dims.tile),
            shape(dims.layers, LAYER_VALUES, *dims.tile),
        ],
        inputs,
        held + [pltpu.SemaphoreType.DMA((len(inputs),))],
        [hbm()] * len(inputs),
    )
    near_halo = beside(near)
    solved, trail, sent, far = call(
        functools.partial(sweep_kernel, dims),
        [field, shape(3, dims.layers, 1, *dims.tile), shape(message + 6, *dims.tile), halo],
        (tiles, maskf, blocks, values),
    )
    mate = exchange(sent, 1)
    far_halo = across(far)
    (cross,) = call(
        functools.partial(cross_kernel, dims),
        [shape(6 * dims.rows + 6, *dims.tile)],
        (sent, mate),
    )
    other = exchange(cross, 2)
    (coefs,) = call(
        functools.partial(coefficient_kernel, dims),
        [shape(dims.layers, LAYER_COEFS, *dims.tile)],
        (trail, blocks, values),
    )
    links, *bounds = call(
        functools.partial(bound_kernel, dims, True),
        [shape(GROUPS, LINKS, *dims.tile), edges, edges],
        (sent, mate, cross, other),
    )
    heff, noise = call(
        functools.partial(local_kernel, dims, True),
        [field, field],
        (tiles, solved, maskf, values, seed),
        padded,
    )
    (heff,) = call(
        functools.partial(absorb_kernel, dims), [field], (heff, *bounds, coefs, values)
    )
    middle, base, solved, far, near, sent = call(
        functools.partial(first_rate_kernel, dims),
        [field, field, field, rates, rates, shape(message, *dims.tile)],
        (far_halo, near_halo, tiles, maskf, heff, coefs, blocks, values),
    )
    mate = exchange(sent, 1)
    near_halos = [near_halo, beside(near)]
    far_halos = [far_halo, across(far)]
    (cross,) = call(
        functools.partial(cross_kernel, dims),
        [shape(6 * dims.rows, *dims.tile)],
        (sent, mate, links),
    )
    other = exchange(cross, 2)
    bounds = call(
        functools.partial(bound_kernel, dims, False),
        [edges, edges],
        (sent, mate, cross, other, links),
    )
    (heff,) = call(
        functools.partial(local_kernel, dims, False),
        [field],
        (middle, solved, maskf, values, noise),
        padded,
    )
    lined = shape(*view.shape)
    staging = [pltpu.VMEM(view.shape, F32), pltpu.SemaphoreType.DMA((2,))]
    heff, accum_lines = call(
        functools.partial(absorb_kernel, dims),
        [field, lined],
        (heff, *bounds, coefs, values, solved),
    )
    inner = dims.rows // 2
    part = shape(3, dims.layers, inner, *dims.tile)
    upper_rows, lower_rows = range(inner, dims.rows), range(inner)
    (near_result,) = second_rate(upper_rows, dims.rows - 1, near_halos, (), [part])
    result, accum = second_rate(
        lower_rows,
        0,
        far_halos,
        (near_result, accum_lines),
        [lined, lined],
        staging,
        None,
        [hbm(), hbm()],
    )

    def whole(lines_view):
        cut = lines_view.reshape(3, dims.layers, dims.chunks, dims.rows, LANES)
        return cut.transpose(0, 1, 3, 2, 4).reshape(magnet.shape)

    return whole(result), whole(accum)


def solution(mesh):
    placed = (
        P(None, "depth", "plane", None),
        P("plane", None),
        P("depth"),
    ) + (P(),) * 10
    return jax.shard_map(
        local,
        mesh=mesh,
        in_specs=placed,
        out_specs=(P(None, "depth", "plane", None), P(None, "depth", "plane", None)),
        check_vma=False,
    )
```

```python
import functools

import jax
import jax.numpy as jnp
from jax import lax
from jax.experimental import pallas as pl
from jax.experimental.pallas import tpu as pltpu
from jax.sharding import PartitionSpec as P

LANES = 128
NEAR = 4.0 / 3.0
FAR = -1.0 / 12.0
HALO = 2
VMEM_LIMIT = 16 * 1024 * 1024
UNROLL = 8
F32 = jnp.float32


def wrapped(value):
    value &= 0xFFFFFFFF
    return value - (1 << 32) if value >= (1 << 31) else value


HASH_A = wrapped(739982445)
HASH_B = wrapped(695872825)
HASH_C = wrapped(1597334677)


class Dims:
    def __init__(self, layers, rows, width, depth, plane):
        self.layers = layers
        self.rows = rows
        self.width = width
        self.chunks = width // LANES
        self.depth = depth
        self.plane = plane
        self.tile = (self.chunks, LANES)

    def field(self):
        return (3, self.layers, self.rows) + self.tile


def shape(*dims):
    return jax.ShapeDtypeStruct(dims, F32)


def vmem():
    return pl.BlockSpec(memory_space=pltpu.VMEM)


def hbm():
    return pl.BlockSpec(memory_space=pltpu.HBM)


def turned(dims, position):
    odd = lax.axis_index("plane") % 2 == 1
    return jnp.where(odd, dims.rows - 1 - position, position)


def cells(dims, comp, layer, row):
    base = (comp * dims.layers + layer) * (dims.chunks * dims.rows) + row
    return pl.ds(base, dims.chunks, stride=dims.rows)


def matvec(get, vec):
    return [get(i, 0) * vec[0] + get(i, 1) * vec[1] + get(i, 2) * vec[2] for i in range(3)]


def add(a, b):
    return [x + y for x, y in zip(a, b)]


def cross(a, b):
    return [
        a[1] * b[2] - a[2] * b[1],
        a[2] * b[0] - a[0] * b[2],
        a[0] * b[1] - a[1] * b[0],
    ]


def unit(vec):
    scale = lax.rsqrt(vec[0] * vec[0] + vec[1] * vec[1] + vec[2] * vec[2])
    return [v * scale for v in vec]


PIVOT, LOWER, UPPER, BLOCK_COEFS = 0, 9, 18, 27
PIVOT_SOURCE, PIVOT_LOWER, FROM_Y, FROM_S, LAYER_COEFS = 0, 9, 18, 27, 36
STIFF, ANISO, DAMP, THERMAL, SCALE, SOURCE, LAYER_VALUES = 0, 1, 2, 3, 4, 5, 6
LAST, FIRST, TOP, BOTTOM, PARTS = 0, 3, 6, 9, 12
LAST_Y, FIRST_Y, FIRST_S, LINKS = 0, 9, 18, 27
SECOND = 8
GROUPS = 4


def table(ref, at, first):
    return lambda i, j: ref[at, first + 3 * i + j]


def column(value, j):
    return jnp.broadcast_to(value[:, j : j + 1], value.shape)


def columns(values, first):
    return [[column(values[i], first + j) for j in range(3)] for i in range(3)]


def entries(matrix):
    return lambda i, j: matrix[i][j]


def sweep_back(dims, lines, upper, start):
    def backward(k, after):
        l = dims.layers - 1 - k
        done = []
        for (ref, r), s in zip(lines, after):
            up = matvec(upper(l), s)
            s = [ref[c, l, r] - up[c] for c in range(3)]
            for c in range(3):
                ref[c, l, r] = s[c]
            done.append(s)
        return done

    return loop(dims.layers, backward, start)


def loop(count, body, start):
    step = max(k for k in range(1, UNROLL + 1) if count % k == 0)

    def steps(k, carry):
        for i in range(step):
            carry = body(k * step + i, carry)
        return carry

    if step == count:
        return steps(0, start)
    return lax.fori_loop(0, count // step, steps, start)


def fetch(inputs, held, sems):
    copies = [
        pltpu.make_async_copy(src, dst, sems.at[k])
        for k, (src, dst) in enumerate(zip(inputs, held))
    ]
    for copy in copies:
        copy.start()
    return copies


def enter_kernel(dims, *refs):
    inputs, refs = refs[:11], refs[11:]
    field, maskf, near, blocks, values, *held, sems = refs
    copies = fetch(inputs, held, sems)
    magnet, mask, materials, stiffness, anisotropy, damping, source, thermal, *matrices = held
    group = lax.axis_index("depth")
    rows = range(dims.rows)
    lines = [turned(dims, r) for r in rows]
    for copy in copies[2:]:
        copy.wait()

    def coefficients(l, carry):
        at = group * dims.layers + l
        material = materials[l]
        for k, ref in enumerate(matrices):
            for i in range(3):
                for j in range(3):
                    blocks[l, 9 * k + 3 * i + j] = jnp.full(dims.tile, ref[i, j, at], F32)
        alpha = jnp.full(dims.tile, damping[material], F32)
        values[l, DAMP] = alpha
        values[l, SCALE] = 1.0 / (1.0 + alpha * alpha)
        rest = ((STIFF, stiffness), (ANISO, anisotropy), (THERMAL, thermal), (SOURCE, source))
        for k, ref in rest:
            values[l, k] = jnp.full(dims.tile, ref[material], F32)
        return carry

    def layer(l, carry):
        for r in rows:
            mask_row = maskf[r]
            for c in range(3):
                v = magnet[cells(dims, c, l, lines[r]), :]
                field[c, l, r] = v
                if r >= dims.rows - HALO:
                    near[c, l, dims.rows - 1 - r] = v * mask_row
        return carry

    loop(dims.layers, coefficients, 0)
    for copy in copies[:2]:
        copy.wait()
    for r in rows:
        maskf[r] = mask[pl.ds(lines[r], dims.chunks, stride=dims.rows), :].astype(F32)
    loop(dims.layers, layer, 0)


def sweep_kernel(dims, field, maskf, blocks, values, local, trail, message, far):
    rows = range(dims.rows)

    def forward(l, prev):
        beta = values[l, SOURCE]
        done = []
        for r in [*rows, None]:
            drop = matvec(table(blocks, l, LOWER), prev[len(done)])
            f = [-a for a in drop] if r is None else [beta * field[c, l, r] - drop[c] for c in range(3)]
            y = matvec(table(blocks, l, PIVOT), f)
            for c in range(3):
                if r is None:
                    trail[c, l, 0] = y[c]
                else:
                    local[c, l, r] = y[c]
                    if r < HALO:
                        far[c, l, r] = field[c, l, r] * maskf[r]
            done.append(y)
        return done

    zero = [[jnp.zeros(dims.tile, F32)] * 3 for _ in rows]
    lane = lax.broadcasted_iota(jnp.int32, dims.tile, 1)
    before, after = [[(lane == first + c).astype(F32) for c in range(3)] for first in (0, 3)]
    last = loop(dims.layers, forward, zero + [before])
    lines = [(local, r) for r in rows] + [(trail, 0)]
    first = sweep_back(dims, lines, lambda l: table(blocks, l, UPPER), zero + [after])
    for c in range(3):
        message[PARTS * dims.rows + LAST + c] = last[-1][c]
        message[PARTS * dims.rows + FIRST + c] = first[-1][c]
    for r in rows:
        sent = [last[r][c] for c in range(3)] + [first[r][c] for c in range(3)]
        for l in (dims.layers - 1, 0):
            sent += [field[c, l, r] * maskf[r] for c in range(3)]
        for p in range(PARTS):
            message[p * dims.rows + r] = sent[p]


def coefficient_kernel(dims, trail, blocks, values, coefs):
    def layer(l, carry):
        pivot, low = table(blocks, l, PIVOT), table(blocks, l, LOWER)
        beta = values[l, SOURCE]
        for i in range(3):
            for j in range(3):
                coefs[l, PIVOT_SOURCE + 3 * i + j] = pivot(i, j) * beta
                coefs[l, PIVOT_LOWER + 3 * i + j] = (
                    pivot(i, 0) * low(0, j) + pivot(i, 1) * low(1, j) + pivot(i, 2) * low(2, j)
                )
                coefs[l, FROM_Y + 3 * i + j] = column(trail[i, l, 0], j)
                coefs[l, FROM_S + 3 * i + j] = column(trail[i, l, 0], 3 + j)
        return carry

    loop(dims.layers, layer, 0)


def for_each_group(body):
    group = lax.axis_index("depth")
    for g in range(GROUPS):

        @pl.when(group == g)
        def _():
            body(g)


def getter(dims, ref):
    return lambda part, r: [ref[(part + c) * dims.rows + r] for c in range(3)]


def spread(dims, ref):
    base = PARTS * dims.rows
    return lambda part: [ref[base + part + c] for c in range(3)]


def cross_kernel(dims, own, mate, *refs):
    links, out = refs if len(refs) == 2 else (None, refs[0])

    def body(g):
        even, odd = (own, mate) if g % 2 == 0 else (mate, own)
        get_even, get_odd = getter(dims, even), getter(dims, odd)
        if links is not None:
            odd_y, odd_first, even_s = (
                table(links, h, at) for h, at in ((1, LAST_Y), (3, FIRST_Y), (2, FIRST_S))
            )
        elif g < 2:
            odd_y = entries(columns(spread(dims, odd)(LAST), 0))
        else:
            odd_first = entries(columns(spread(dims, odd)(FIRST), 0))
            even_s = entries(columns(spread(dims, even)(FIRST), 3))
        for r in range(dims.rows):
            if g < 2:
                value = add(get_odd(LAST, r), matvec(odd_y, get_even(LAST, r)))
                side = get_odd(TOP, r)
            else:
                value = add(get_odd(FIRST, r), matvec(odd_first, get_even(LAST, r)))
                value = add(get_even(FIRST, r), matvec(even_s, value))
                side = get_even(BOTTOM, r)
            for c in range(3):
                out[c * dims.rows + r] = value[c]
                out[(3 + c) * dims.rows + r] = side[c]
        if links is not None:
            for tile in range(6 * dims.rows, out.shape[0]):
                out[tile] = jnp.zeros(dims.tile, F32)
            return
        lane = lax.broadcasted_iota(jnp.int32, dims.tile, 1)
        for part in (LAST, FIRST):
            pair = zip(spread(dims, even)(part), spread(dims, odd)(part))
            for c, (a, b) in enumerate(pair):
                both = jnp.where(lane < SECOND, a, pltpu.roll(b, SECOND, 1))
                out[6 * dims.rows + part + c] = both

    for_each_group(body)


def bound_kernel(dims, first, own, mate, cross, other, links, bound, edge):
    def body(g):
        base = 6 * dims.rows
        even, odd = (own, mate) if g % 2 == 0 else (mate, own)
        pairs = (cross, other) if g < 2 else (other, cross)
        for pair, ref in enumerate(pairs if first else ()):
            for h in range(2):
                values = [[ref[base + part + c] for c in range(3)] for part in (LAST, FIRST)]
                matrices = (
                    (LAST_Y, columns(values[0], SECOND * h)),
                    (FIRST_Y, columns(values[1], SECOND * h)),
                    (FIRST_S, columns(values[1], SECOND * h + 3)),
                )
                for at, matrix in matrices:
                    for i in range(3):
                        for j in range(3):
                            links[2 * pair + h, at + 3 * i + j] = matrix[i][j]
        get_even, get_odd = getter(dims, even), getter(dims, odd)
        get_cross, get_other, get_mate = (getter(dims, ref) for ref in (cross, other, mate))
        zero = [jnp.zeros(dims.tile, F32)] * 3
        for r in range(dims.rows):
            if g < 2:
                s = matvec(table(links, 2, LAST_Y), get_cross(0, r))
                s = matvec(table(links, 2, FIRST_S), matvec(table(links, 3, FIRST_Y), s))
                s = add(s, matvec(table(links, 2, FIRST_Y), get_cross(0, r)))
                s = add(s, get_other(0, r))
                if g == 0:
                    y = zero
                    s = matvec(table(links, 1, FIRST_S), s)
                    s = add(s, matvec(table(links, 1, FIRST_Y), get_even(LAST, r)))
                    s = add(s, get_odd(FIRST, r))
                else:
                    y = get_even(LAST, r)
            else:
                y = get_other(0, r)
                after = add(get_even(LAST, r), matvec(table(links, 2, LAST_Y), y))
                if g == 2:
                    s = add(get_odd(FIRST, r), matvec(table(links, 3, FIRST_Y), after))
                else:
                    y, s = after, zero
            if g % 2 == 0:
                down = zero if g == 0 else get_other(3, r)
                up = get_mate(BOTTOM, r)
            else:
                down = get_mate(TOP, r)
                up = zero if g == GROUPS - 1 else get_other(3, r)
            for c in range(3):
                bound[c, r] = y[c]
                bound[3 + c, r] = s[c]
                edge[c, r] = down[c]
                edge[3 + c, r] = up[c]

    for_each_group(body)


def others_part(dims, l, r, bound, edge, coefs, values):
    stiff = values[l, STIFF]
    down = jnp.where(l == 0, 0.5, 0.0) * stiff
    up = jnp.where(l == dims.layers - 1, 0.5, 0.0) * stiff
    y = [bound[c, r] for c in range(3)]
    s = [bound[3 + c, r] for c in range(3)]
    fix = add(matvec(table(coefs, l, FROM_Y), y), matvec(table(coefs, l, FROM_S), s))
    field = [0.5 * fix[c] + down * edge[c, r] + up * edge[3 + c, r] for c in range(3)]
    return fix, field


def absorb_kernel(dims, heff, bound, edge, coefs, values, out):
    def body(l, carry):
        for r in range(dims.rows):
            _, more = others_part(dims, l, r, bound, edge, coefs, values)
            for c in range(3):
                out[c, l, r] = heff[c, l, r] + more[c]
        return carry

    loop(dims.layers, body, 0)


def halo_kernel(dims, rows, position, start_halo, change_halo, heff, values, out):
    def body(l, carry):
        lines = middle_halo(l, start_halo, change_halo)
        for r in rows:
            h = [heff[c, l, r] for c in range(3)]
            h = add_halos(h, l, r, [(position, lines)], values)
            for c in range(3):
                out[c, l, r - rows[0]] = h[c]
        return carry

    loop(dims.layers, body, 0)


def send_lines(dims, layer, src, dst, sem):
    lines = dims.chunks * dims.rows
    for c in range(3):
        where = pl.ds((c * dims.layers + layer) * lines, lines)
        pltpu.make_async_copy(src.at[where], dst.at[where], sem).start()


def shifted_sum(dims, w, lane):
    after = pltpu.roll(w, dims.chunks - 1, 0)
    before = pltpu.roll(w, 1, 0)
    near = pltpu.roll(jnp.where(lane < 1, after, w), LANES - 1, 1)
    near += pltpu.roll(jnp.where(lane >= LANES - 1, before, w), 1, 1)
    far = pltpu.roll(jnp.where(lane < 2, after, w), LANES - 2, 1)
    far += pltpu.roll(jnp.where(lane >= LANES - 2, before, w), 2, 1)
    return NEAR * near + FAR * far


def hash_uniform(mixed):
    mixed = mixed ^ lax.shift_right_logical(mixed, jnp.int32(16))
    mixed = mixed * HASH_A
    mixed = mixed ^ lax.shift_right_logical(mixed, jnp.int32(15))
    mixed = mixed * HASH_B
    mixed = mixed ^ lax.shift_right_logical(mixed, jnp.int32(16))
    return (mixed & 65535).astype(F32) * (1.0 / 32767.5) - 1.0


def local_kernel(dims, first, *refs):
    field, solved, maskf, values, *refs = refs
    if first:
        seed, heff, noise, masked = refs
        group = lax.axis_index("depth")
        place = lax.axis_index("plane")
        within = (
            lax.broadcasted_iota(jnp.int32, dims.tile, 0) * LANES
            + lax.broadcasted_iota(jnp.int32, dims.tile, 1)
        ) * HASH_A + seed[...]
    else:
        noise, heff, masked = refs
    lane = lax.broadcasted_iota(jnp.int32, dims.tile, 1)
    rows = range(dims.rows)

    for c in range(3):
        for r in rows:
            masked[c, 0, r] = jnp.zeros(dims.tile, F32)
            masked[c, dims.layers + 1, r] = jnp.zeros(dims.tile, F32)

    def fill(l, carry):
        for r in rows:
            mask_row = maskf[r]
            for c in range(3):
                masked[c, l + 1, r] = field[c, l, r] * mask_row
        return carry

    lax.fori_loop(0, dims.layers, fill, 0)

    def body(l, carry):
        stiff = values[l, STIFF]
        aniso = values[l, ANISO]
        for c in range(3):
            w = [masked[c, l + 1, r] for r in rows]
            for r in rows:
                total = shifted_sum(dims, w[r], lane)
                for step, weight in ((1, NEAR), (2, FAR)):
                    inside = [w[q] for q in (r - step, r + step) if 0 <= q < dims.rows]
                    if inside:
                        total += weight * functools.reduce(jnp.add, inside)
                total += 0.5 * (masked[c, l, r] + masked[c, l + 2, r])
                h = stiff * total + 0.5 * solved[c, l, r]
                if c == 2:
                    h += aniso * field[c, l, r]
                if first:
                    layer = group * dims.layers + l
                    line = (c * (dims.depth * dims.layers) + layer) * (
                        dims.plane * dims.rows
                    ) + (place * dims.rows + turned(dims, r))
                    value = values[l, THERMAL] * hash_uniform(within + line * dims.width * HASH_A)
                    noise[c, l, r] = value
                    h += value
                else:
                    h += noise[c, l, r]
                heff[c, l, r] = h
        return carry

    lax.fori_loop(0, dims.layers, body, 0)


def largest(m):
    x, y, z = [jnp.abs(v) for v in m]
    first = x >= jnp.maximum(y, z)
    return first, jnp.logical_and(jnp.logical_not(first), y >= z)


def tangent_parts(m, change):
    first, second = largest(m)
    last = jnp.logical_or(first, second)
    return [jnp.where(first, change[1], change[0]), jnp.where(last, change[2], change[1])]


def tangent_whole(m, parts):
    first, second = largest(m)
    last = jnp.logical_or(first, second)
    a, b = parts
    rest = a * jnp.where(first, m[1], m[0]) + b * jnp.where(last, m[2], m[1])
    along = jnp.where(first, m[0], jnp.where(second, m[1], m[2]))
    c = -rest / jnp.where(along == 0.0, 1.0, along)
    return [
        jnp.where(first, c, a),
        jnp.where(first, a, jnp.where(second, c, b)),
        jnp.where(last, b, c),
    ]


def middle_halo(l, start_halo, change_halo):
    lines = []
    for k in range(HALO):
        w = [start_halo[c, l, k] for c in range(3)]
        change = tangent_whole(w, [change_halo[c, l, k] for c in range(2)])
        m1 = [w[c] - 0.03 * change[c] for c in range(3)]
        square = m1[0] * m1[0] + m1[1] * m1[1] + m1[2] * m1[2]
        scale = lax.rsqrt(jnp.maximum(square, 1e-30))
        lines.append([v * scale for v in m1])
    return lines


def first_halo(l, halo):
    return [[halo[c, l, k] for c in range(3)] for k in range(HALO)]


def add_halos(h, l, r, halos, values):
    stiff = values[l, STIFF]
    for step, weight in ((1, NEAR), (2, FAR)):
        for position, halo in halos:
            beyond = step - 1 - abs(r - position)
            if beyond >= 0:
                h = [h[c] + (stiff * weight) * halo[beyond][c] for c in range(3)]
    return h


def rate(l, r, h, field, maskf, values):
    v = [field[c, l, r] for c in range(3)]
    torque = cross(v, h)
    twice = cross(v, torque)
    gain = values[l, SCALE] * maskf[r]
    return v, [(torque[c] + values[l, DAMP] * twice[c]) * gain for c in range(3)]


def first_rate_kernel(dims, *refs):
    far_halo, near_halo, field, maskf, heff, coefs, blocks, values, *refs = refs
    middle, base, local, far, near, message = refs
    rows = range(dims.rows)

    def body(l, prev):
        halos = [(0, first_halo(l, far_halo)), (dims.rows - 1, first_halo(l, near_halo))]
        done = []
        for r in rows:
            h = add_halos([heff[c, l, r] for c in range(3)], l, r, halos, values)
            v, change = rate(l, r, h, field, maskf, values)
            m1 = unit([v[c] - 0.03 * change[c] for c in range(3)])
            for c in range(3):
                middle[c, l, r] = m1[c]
                base[c, l, r] = v[c] - 0.015 * change[c]
            for c, part in enumerate(tangent_parts(v, change)):
                if r < HALO:
                    far[c, l, r] = part
                if r >= dims.rows - HALO:
                    near[c, l, dims.rows - 1 - r] = part
            y = matvec(table(coefs, l, PIVOT_SOURCE), m1)
            drop = matvec(table(coefs, l, PIVOT_LOWER), prev[r])
            y = [a - b for a, b in zip(y, drop)]
            for c in range(3):
                local[c, l, r] = y[c]
            done.append(y)
        return done

    zero = [[jnp.zeros(dims.tile, F32)] * 3 for _ in rows]
    last = loop(dims.layers, body, zero)
    head = sweep_back(dims, [(local, r) for r in rows], lambda l: table(blocks, l, UPPER), zero)
    for r in rows:
        sent = last[r] + head[r]
        for l in (dims.layers - 1, 0):
            sent += [middle[c, l, r] * maskf[r] for c in range(3)]
        for p in range(PARTS):
            message[p * dims.rows + r] = sent[p]


def last_kernel(dims, *refs):
    own, mate, cross, other, links, start_halo, change_halo, *refs = refs
    field, maskf, heff, upper_heff, coefs, values, base, local, *refs = refs
    result_out, accum_out, bound, edge, result, accum, sem = refs
    bound_kernel(dims, False, own, mate, cross, other, links, bound, edge)
    upper = dims.rows // 2

    def body(l, carry):
        halos = [(0, middle_halo(l, start_halo, change_halo))]
        for r in range(dims.rows):
            fix, more = others_part(dims, l, r, bound, edge, coefs, values)
            for c in range(3):
                accum[cells(dims, c, l, turned(dims, r)), :] = local[c, l, r] + fix[c]
            if r < upper:
                h = add_halos([heff[c, l, r] for c in range(3)], l, r, halos, values)
            else:
                h = [upper_heff[c, l, r - upper] for c in range(3)]
            _, change = rate(l, r, add(h, more), field, maskf, values)
            new = unit([base[c, l, r] - 0.015 * change[c] for c in range(3)])
            for c in range(3):
                result[cells(dims, c, l, turned(dims, r)), :] = new[c]
        send_lines(dims, l, accum, accum_out, sem.at[1])
        send_lines(dims, l, result, result_out, sem.at[0])
        return carry

    loop(dims.layers, body, 0)
    pltpu.make_async_copy(result, result_out, sem.at[0]).wait()
    pltpu.make_async_copy(accum, accum_out, sem.at[1]).wait()


def call(kernel, outs, args, scratch=(), ins=None, results=None):
    return pl.pallas_call(
        kernel,
        out_shape=outs,
        in_specs=ins or [vmem()] * len(args),
        out_specs=results or [vmem()] * len(outs),
        scratch_shapes=list(scratch),
        compiler_params=pltpu.CompilerParams(vmem_limit_bytes=VMEM_LIMIT),
        cost_estimate=pl.CostEstimate(flops=1000000, bytes_accessed=1000000, transcendentals=0),
    )(*args)


def ring(count, step):
    return [(i, (i + step) % count) for i in range(count)]


def local(
    magnet,
    mask,
    materials,
    exchange_strength,
    anisotropy,
    damping,
    source_strength,
    thermal_strength,
    pivots,
    lower,
    upper,
    noise_stream,
    counter,
):
    dims = Dims(
        magnet.shape[1],
        magnet.shape[2],
        magnet.shape[3],
        lax.axis_size("depth"),
        lax.axis_size("plane"),
    )
    lines = (3, dims.layers, dims.rows, dims.chunks, LANES)
    view = magnet.reshape(lines).transpose(0, 1, 3, 2, 4).reshape(-1, LANES)
    mask_view = mask.reshape(lines[2:]).transpose(1, 0, 2).reshape(-1, LANES)
    halo = shape(3, dims.layers, HALO, *dims.tile)
    rates = shape(2, dims.layers, HALO, *dims.tile)
    field = shape(*dims.field())
    padded = [pltpu.VMEM((3, dims.layers + 2, dims.rows) + dims.tile, F32)]
    assert dims.depth == GROUPS
    message = PARTS * dims.rows
    edges = shape(6, dims.rows, *dims.tile)

    def across(values):
        pairs = [(i, (i + 1 if i % 2 else i - 1) % dims.plane) for i in range(dims.plane)]
        return lax.ppermute(values, "plane", pairs)

    def beside(values):
        return lax.ppermute(values, "plane", [(i, i ^ 1) for i in range(dims.plane)])

    def exchange(values, step):
        return lax.ppermute(values, "depth", [(i, i ^ step) for i in range(dims.depth)])

    seed = jnp.full(dims.tile, noise_stream[0] * HASH_B + counter[0] * HASH_C, jnp.int32)
    inputs = (
        view,
        mask_view,
        materials,
        exchange_strength,
        anisotropy,
        damping,
        source_strength,
        thermal_strength,
        pivots.transpose(1, 2, 0),
        lower.transpose(1, 2, 0),
        upper.transpose(1, 2, 0),
    )
    inputs = [pltpu.with_memory_space_constraint(x, pltpu.HBM) for x in inputs]
    spaces = [pltpu.VMEM] * 2 + [pltpu.SMEM] * 9
    held = [space(x.shape, x.dtype) for space, x in zip(spaces, inputs)]
    tiles, maskf, near, blocks, values = call(
        functools.partial(enter_kernel, dims),
        [
            field,
            shape(dims.rows, *dims.tile),
            halo,
            shape(dims.layers, BLOCK_COEFS, *dims.tile),
            shape(dims.layers, LAYER_VALUES, *dims.tile),
        ],
        inputs,
        held + [pltpu.SemaphoreType.DMA((len(inputs),))],
        [hbm()] * len(inputs),
    )
    near_halo = beside(near)
    solved, trail, sent, far = call(
        functools.partial(sweep_kernel, dims),
        [field, shape(3, dims.layers, 1, *dims.tile), shape(message + 6, *dims.tile), halo],
        (tiles, maskf, blocks, values),
    )
    mate = exchange(sent, 1)
    far_halo = across(far)
    (cross,) = call(
        functools.partial(cross_kernel, dims),
        [shape(6 * dims.rows + 6, *dims.tile)],
        (sent, mate),
    )
    other = exchange(cross, 2)
    (coefs,) = call(
        functools.partial(coefficient_kernel, dims),
        [shape(dims.layers, LAYER_COEFS, *dims.tile)],
        (trail, blocks, values),
    )
    links, *bounds = call(
        functools.partial(bound_kernel, dims, True),
        [shape(GROUPS, LINKS, *dims.tile), edges, edges],
        (sent, mate, cross, other),
    )
    heff, noise = call(
        functools.partial(local_kernel, dims, True),
        [field, field],
        (tiles, solved, maskf, values, seed),
        padded,
    )
    (heff,) = call(
        functools.partial(absorb_kernel, dims), [field], (heff, *bounds, coefs, values)
    )
    middle, base, solved, far, near, sent = call(
        functools.partial(first_rate_kernel, dims),
        [field, field, field, rates, rates, shape(message, *dims.tile)],
        (far_halo, near_halo, tiles, maskf, heff, coefs, blocks, values),
    )
    mate = exchange(sent, 1)
    near_halos = [near_halo, beside(near)]
    far_halos = [far_halo, across(far)]
    (cross,) = call(
        functools.partial(cross_kernel, dims),
        [shape(6 * dims.rows, *dims.tile)],
        (sent, mate, links),
    )
    other = exchange(cross, 2)
    (heff,) = call(
        functools.partial(local_kernel, dims, False),
        [field],
        (middle, solved, maskf, values, noise),
        padded,
    )
    lined = shape(*view.shape)
    inner = dims.rows // 2
    (upper_heff,) = call(
        functools.partial(halo_kernel, dims, range(inner, dims.rows), dims.rows - 1),
        [shape(3, dims.layers, dims.rows - inner, *dims.tile)],
        (*near_halos, heff, values),
    )
    result, accum = call(
        functools.partial(last_kernel, dims),
        [lined, lined],
        (
            sent,
            mate,
            cross,
            other,
            links,
            *far_halos,
            middle,
            maskf,
            heff,
            upper_heff,
            coefs,
            values,
            base,
            solved,
        ),
        [pltpu.VMEM(edges.shape, F32)] * 2
        + [pltpu.VMEM(view.shape, F32)] * 2
        + [pltpu.SemaphoreType.DMA((2,))],
        None,
        [hbm(), hbm()],
    )

    def whole(lines_view):
        cut = lines_view.reshape(3, dims.layers, dims.chunks, dims.rows, LANES)
        return cut.transpose(0, 1, 3, 2, 4).reshape(magnet.shape)

    return whole(result), whole(accum)


def solution(mesh):
    placed = (
        P(None, "depth", "plane", None),
        P("plane", None),
        P("depth"),
    ) + (P(),) * 10
    return jax.shard_map(
        local,
        mesh=mesh,
        in_specs=placed,
        out_specs=(P(None, "depth", "plane", None), P(None, "depth", "plane", None)),
        check_vma=False,
    )
```

```python
import functools

import jax
import jax.numpy as jnp
from jax import lax
from jax.experimental import pallas as pl
from jax.experimental.pallas import tpu as pltpu
from jax.sharding import PartitionSpec as P

LANES = 128
NEAR = 4.0 / 3.0
FAR = -1.0 / 12.0
HALO = 2
VMEM_LIMIT = 16 * 1024 * 1024
UNROLL = 8
F32 = jnp.float32


def wrapped(value):
    value &= 0xFFFFFFFF
    return value - (1 << 32) if value >= (1 << 31) else value


HASH_A = wrapped(739982445)
HASH_B = wrapped(695872825)
HASH_C = wrapped(1597334677)


class Dims:
    def __init__(self, layers, rows, width, depth, plane):
        self.layers = layers
        self.rows = rows
        self.width = width
        self.chunks = width // LANES
        self.depth = depth
        self.plane = plane
        self.tile = (self.chunks, LANES)

    def field(self):
        return (3, self.layers, self.rows) + self.tile


def shape(*dims):
    return jax.ShapeDtypeStruct(dims, F32)


def vmem():
    return pl.BlockSpec(memory_space=pltpu.VMEM)


def hbm():
    return pl.BlockSpec(memory_space=pltpu.HBM)


def turned(dims, position):
    odd = lax.axis_index("plane") % 2 == 1
    return jnp.where(odd, dims.rows - 1 - position, position)


def cells(dims, comp, layer, row):
    base = (comp * dims.layers + layer) * (dims.chunks * dims.rows) + row
    return pl.ds(base, dims.chunks, stride=dims.rows)


def matvec(get, vec):
    return [get(i, 0) * vec[0] + get(i, 1) * vec[1] + get(i, 2) * vec[2] for i in range(3)]


def add(a, b):
    return [x + y for x, y in zip(a, b)]


def cross(a, b):
    return [
        a[1] * b[2] - a[2] * b[1],
        a[2] * b[0] - a[0] * b[2],
        a[0] * b[1] - a[1] * b[0],
    ]


def unit(vec):
    scale = lax.rsqrt(vec[0] * vec[0] + vec[1] * vec[1] + vec[2] * vec[2])
    return [v * scale for v in vec]


PIVOT, LOWER, UPPER, BLOCK_COEFS = 0, 9, 18, 27
PIVOT_SOURCE, PIVOT_LOWER, FROM_Y, FROM_S, LAYER_COEFS = 0, 9, 18, 27, 36
STIFF, ANISO, DAMP, THERMAL, SCALE, LAYER_VALUES = 0, 1, 2, 3, 4, 5
LAST, FIRST, TOP, BOTTOM, PARTS = 0, 3, 6, 9, 12
LAST_Y, FIRST_Y, FIRST_S, LINKS = 0, 9, 18, 27
SECOND = 8
GROUPS = 4


def table(ref, at, first):
    return lambda i, j: ref[at, first + 3 * i + j]


def column(value, j):
    return jnp.broadcast_to(value[:, j : j + 1], value.shape)


def columns(values, first):
    return [[column(values[i], first + j) for j in range(3)] for i in range(3)]


def entries(matrix):
    return lambda i, j: matrix[i][j]


def sweep_back(dims, lines, upper, start):
    def backward(k, after):
        l = dims.layers - 1 - k
        done = []
        for (ref, r), s in zip(lines, after):
            up = matvec(upper(l), s)
            s = [ref[c, l, r] - up[c] for c in range(3)]
            for c in range(3):
                ref[c, l, r] = s[c]
            done.append(s)
        return done

    return loop(dims.layers, backward, start)


def loop(count, body, start):
    step = max(k for k in range(1, UNROLL + 1) if count % k == 0)

    def steps(k, carry):
        for i in range(step):
            carry = body(k * step + i, carry)
        return carry

    if step == count:
        return steps(0, start)
    return lax.fori_loop(0, count // step, steps, start)


def fetch(inputs, held, sems):
    copies = [
        pltpu.make_async_copy(src, dst, sems.at[k])
        for k, (src, dst) in enumerate(zip(inputs, held))
    ]
    for copy in reversed(copies):
        copy.start()
    return copies


def enter_kernel(dims, *refs):
    inputs, refs = refs[:7], refs[7:]
    field, maskf, near, blocks, beta, *held, sems = refs
    copies = fetch(inputs, held, sems)
    magnet, mask, materials, source, *matrices = held
    group = lax.axis_index("depth")
    rows = range(dims.rows)
    lines = [turned(dims, r) for r in rows]
    for copy in copies[2:]:
        copy.wait()

    def coefficients(l, carry):
        at = group * dims.layers + l
        beta[l] = jnp.full(dims.tile, source[materials[l]], F32)
        for k, ref in enumerate(matrices):
            for i in range(3):
                for j in range(3):
                    blocks[l, 9 * k + 3 * i + j] = jnp.full(dims.tile, ref[i, j, at], F32)
        return carry

    def layer(l, carry):
        for r in rows:
            mask_row = maskf[r]
            for c in range(3):
                v = magnet[cells(dims, c, l, lines[r]), :]
                field[c, l, r] = v
                if r >= dims.rows - HALO:
                    near[c, l, dims.rows - 1 - r] = v * mask_row
        return carry

    loop(dims.layers, coefficients, 0)
    for copy in copies[:2]:
        copy.wait()
    for r in rows:
        maskf[r] = mask[pl.ds(lines[r], dims.chunks, stride=dims.rows), :].astype(F32)
    loop(dims.layers, layer, 0)


def sweep_kernel(dims, field, maskf, blocks, source, local, trail, message, far):
    rows = range(dims.rows)

    def forward(l, prev):
        beta = source[l]
        done = []
        for r in [*rows, None]:
            drop = matvec(table(blocks, l, LOWER), prev[len(done)])
            f = [-a for a in drop] if r is None else [beta * field[c, l, r] - drop[c] for c in range(3)]
            y = matvec(table(blocks, l, PIVOT), f)
            for c in range(3):
                if r is None:
                    trail[c, l, 0] = y[c]
                else:
                    local[c, l, r] = y[c]
                    if r < HALO:
                        far[c, l, r] = field[c, l, r] * maskf[r]
            done.append(y)
        return done

    zero = [[jnp.zeros(dims.tile, F32)] * 3 for _ in rows]
    lane = lax.broadcasted_iota(jnp.int32, dims.tile, 1)
    before, after = [[(lane == first + c).astype(F32) for c in range(3)] for first in (0, 3)]
    last = loop(dims.layers, forward, zero + [before])
    lines = [(local, r) for r in rows] + [(trail, 0)]
    first = sweep_back(dims, lines, lambda l: table(blocks, l, UPPER), zero + [after])
    for c in range(3):
        message[PARTS * dims.rows + LAST + c] = last[-1][c]
        message[PARTS * dims.rows + FIRST + c] = first[-1][c]
    for r in rows:
        sent = [last[r][c] for c in range(3)] + [first[r][c] for c in range(3)]
        for l in (dims.layers - 1, 0):
            sent += [field[c, l, r] * maskf[r] for c in range(3)]
        for p in range(PARTS):
            message[p * dims.rows + r] = sent[p]


def coefficient_kernel(dims, trail, blocks, source, *refs):
    inputs, (coefs, values, *held, sems) = refs[:5], refs[5:]
    copies = fetch(inputs, held, sems)
    materials, stiffness, anisotropy, damping, thermal = held

    def constants(l, carry):
        material = materials[l]
        alpha = jnp.full(dims.tile, damping[material], F32)
        values[l, DAMP] = alpha
        values[l, SCALE] = 1.0 / (1.0 + alpha * alpha)
        for k, ref in ((STIFF, stiffness), (ANISO, anisotropy), (THERMAL, thermal)):
            values[l, k] = jnp.full(dims.tile, ref[material], F32)
        return carry

    def layer(l, carry):
        pivot, low = table(blocks, l, PIVOT), table(blocks, l, LOWER)
        beta = source[l]
        for i in range(3):
            for j in range(3):
                coefs[l, PIVOT_SOURCE + 3 * i + j] = pivot(i, j) * beta
                coefs[l, PIVOT_LOWER + 3 * i + j] = (
                    pivot(i, 0) * low(0, j) + pivot(i, 1) * low(1, j) + pivot(i, 2) * low(2, j)
                )
                coefs[l, FROM_Y + 3 * i + j] = column(trail[i, l, 0], j)
                coefs[l, FROM_S + 3 * i + j] = column(trail[i, l, 0], 3 + j)
        return carry

    loop(dims.layers, layer, 0)
    for copy in copies:
        copy.wait()
    loop(dims.layers, constants, 0)


def for_each_group(body):
    group = lax.axis_index("depth")
    for g in range(GROUPS):

        @pl.when(group == g)
        def _():
            body(g)


def getter(dims, ref):
    return lambda part, r: [ref[(part + c) * dims.rows + r] for c in range(3)]


def spread(dims, ref):
    base = PARTS * dims.rows
    return lambda part: [ref[base + part + c] for c in range(3)]


def cross_kernel(dims, own, mate, *refs):
    links, out = refs if len(refs) == 2 else (None, refs[0])

    def body(g):
        even, odd = (own, mate) if g % 2 == 0 else (mate, own)
        get_even, get_odd = getter(dims, even), getter(dims, odd)
        if links is not None:
            odd_y, odd_first, even_s = (
                table(links, h, at) for h, at in ((1, LAST_Y), (3, FIRST_Y), (2, FIRST_S))
            )
        elif g < 2:
            odd_y = entries(columns(spread(dims, odd)(LAST), 0))
        else:
            odd_first = entries(columns(spread(dims, odd)(FIRST), 0))
            even_s = entries(columns(spread(dims, even)(FIRST), 3))
        for r in range(dims.rows):
            if g < 2:
                value = add(get_odd(LAST, r), matvec(odd_y, get_even(LAST, r)))
                side = get_odd(TOP, r)
            else:
                value = add(get_odd(FIRST, r), matvec(odd_first, get_even(LAST, r)))
                value = add(get_even(FIRST, r), matvec(even_s, value))
                side = get_even(BOTTOM, r)
            for c in range(3):
                out[c * dims.rows + r] = value[c]
                out[(3 + c) * dims.rows + r] = side[c]
        if links is not None:
            for tile in range(6 * dims.rows, out.shape[0]):
                out[tile] = jnp.zeros(dims.tile, F32)
            return
        lane = lax.broadcasted_iota(jnp.int32, dims.tile, 1)
        for part in (LAST, FIRST):
            pair = zip(spread(dims, even)(part), spread(dims, odd)(part))
            for c, (a, b) in enumerate(pair):
                both = jnp.where(lane < SECOND, a, pltpu.roll(b, SECOND, 1))
                out[6 * dims.rows + part + c] = both

    for_each_group(body)


def bound_kernel(dims, first, own, mate, cross, other, links, bound, edge):
    def body(g):
        base = 6 * dims.rows
        even, odd = (own, mate) if g % 2 == 0 else (mate, own)
        pairs = (cross, other) if g < 2 else (other, cross)
        for pair, ref in enumerate(pairs if first else ()):
            for h in range(2):
                values = [[ref[base + part + c] for c in range(3)] for part in (LAST, FIRST)]
                matrices = (
                    (LAST_Y, columns(values[0], SECOND * h)),
                    (FIRST_Y, columns(values[1], SECOND * h)),
                    (FIRST_S, columns(values[1], SECOND * h + 3)),
                )
                for at, matrix in matrices:
                    for i in range(3):
                        for j in range(3):
                            links[2 * pair + h, at + 3 * i + j] = matrix[i][j]
        get_even, get_odd = getter(dims, even), getter(dims, odd)
        get_cross, get_other, get_mate = (getter(dims, ref) for ref in (cross, other, mate))
        zero = [jnp.zeros(dims.tile, F32)] * 3
        for r in range(dims.rows):
            if g < 2:
                s = matvec(table(links, 2, LAST_Y), get_cross(0, r))
                s = matvec(table(links, 2, FIRST_S), matvec(table(links, 3, FIRST_Y), s))
                s = add(s, matvec(table(links, 2, FIRST_Y), get_cross(0, r)))
                s = add(s, get_other(0, r))
                if g == 0:
                    y = zero
                    s = matvec(table(links, 1, FIRST_S), s)
                    s = add(s, matvec(table(links, 1, FIRST_Y), get_even(LAST, r)))
                    s = add(s, get_odd(FIRST, r))
                else:
                    y = get_even(LAST, r)
            else:
                y = get_other(0, r)
                after = add(get_even(LAST, r), matvec(table(links, 2, LAST_Y), y))
                if g == 2:
                    s = add(get_odd(FIRST, r), matvec(table(links, 3, FIRST_Y), after))
                else:
                    y, s = after, zero
            if g % 2 == 0:
                down = zero if g == 0 else get_other(3, r)
                up = get_mate(BOTTOM, r)
            else:
                down = get_mate(TOP, r)
                up = zero if g == GROUPS - 1 else get_other(3, r)
            for c in range(3):
                bound[c, r] = y[c]
                bound[3 + c, r] = s[c]
                edge[c, r] = down[c]
                edge[3 + c, r] = up[c]

    for_each_group(body)


def others_part(dims, l, r, bound, edge, coefs, values):
    stiff = values[l, STIFF]
    down = jnp.where(l == 0, 0.5, 0.0) * stiff
    up = jnp.where(l == dims.layers - 1, 0.5, 0.0) * stiff
    y = [bound[c, r] for c in range(3)]
    s = [bound[3 + c, r] for c in range(3)]
    fix = add(matvec(table(coefs, l, FROM_Y), y), matvec(table(coefs, l, FROM_S), s))
    field = [0.5 * fix[c] + down * edge[c, r] + up * edge[3 + c, r] for c in range(3)]
    return fix, field


def absorb_kernel(dims, heff, bound, edge, coefs, values, out):
    def body(l, carry):
        for r in range(dims.rows):
            _, more = others_part(dims, l, r, bound, edge, coefs, values)
            for c in range(3):
                out[c, l, r] = heff[c, l, r] + more[c]
        return carry

    loop(dims.layers, body, 0)


def halo_kernel(dims, rows, position, start_halo, change_halo, heff, values, out):
    def body(l, carry):
        lines = middle_halo(l, start_halo, change_halo)
        for r in rows:
            h = [heff[c, l, r] for c in range(3)]
            h = add_halos(h, l, r, [(position, lines)], values)
            for c in range(3):
                out[c, l, r - rows[0]] = h[c]
        return carry

    loop(dims.layers, body, 0)


def send_lines(dims, layer, src, dst, sem):
    lines = dims.chunks * dims.rows
    for c in range(3):
        where = pl.ds((c * dims.layers + layer) * lines, lines)
        pltpu.make_async_copy(src.at[where], dst.at[where], sem).start()


def shifted_sum(dims, w, lane):
    after = pltpu.roll(w, dims.chunks - 1, 0)
    before = pltpu.roll(w, 1, 0)
    near = pltpu.roll(jnp.where(lane < 1, after, w), LANES - 1, 1)
    near += pltpu.roll(jnp.where(lane >= LANES - 1, before, w), 1, 1)
    far = pltpu.roll(jnp.where(lane < 2, after, w), LANES - 2, 1)
    far += pltpu.roll(jnp.where(lane >= LANES - 2, before, w), 2, 1)
    return NEAR * near + FAR * far


def hash_uniform(mixed):
    mixed = mixed ^ lax.shift_right_logical(mixed, jnp.int32(16))
    mixed = mixed * HASH_A
    mixed = mixed ^ lax.shift_right_logical(mixed, jnp.int32(15))
    mixed = mixed * HASH_B
    mixed = mixed ^ lax.shift_right_logical(mixed, jnp.int32(16))
    return (mixed & 65535).astype(F32) * (1.0 / 32767.5) - 1.0


def local_kernel(dims, first, *refs):
    field, solved, maskf, values, *refs = refs
    if first:
        seed, heff, noise, masked = refs
        group = lax.axis_index("depth")
        place = lax.axis_index("plane")
        within = (
            lax.broadcasted_iota(jnp.int32, dims.tile, 0) * LANES
            + lax.broadcasted_iota(jnp.int32, dims.tile, 1)
        ) * HASH_A + seed[...]
    else:
        noise, heff, masked = refs
    lane = lax.broadcasted_iota(jnp.int32, dims.tile, 1)
    rows = range(dims.rows)

    for c in range(3):
        for r in rows:
            masked[c, 0, r] = jnp.zeros(dims.tile, F32)
            masked[c, dims.layers + 1, r] = jnp.zeros(dims.tile, F32)

    def fill(l, carry):
        for r in rows:
            mask_row = maskf[r]
            for c in range(3):
                masked[c, l + 1, r] = field[c, l, r] * mask_row
        return carry

    lax.fori_loop(0, dims.layers, fill, 0)

    def body(l, carry):
        stiff = values[l, STIFF]
        aniso = values[l, ANISO]
        for c in range(3):
            w = [masked[c, l + 1, r] for r in rows]
            for r in rows:
                total = shifted_sum(dims, w[r], lane)
                for step, weight in ((1, NEAR), (2, FAR)):
                    inside = [w[q] for q in (r - step, r + step) if 0 <= q < dims.rows]
                    if inside:
                        total += weight * functools.reduce(jnp.add, inside)
                total += 0.5 * (masked[c, l, r] + masked[c, l + 2, r])
                h = stiff * total + 0.5 * solved[c, l, r]
                if c == 2:
                    h += aniso * field[c, l, r]
                if first:
                    layer = group * dims.layers + l
                    line = (c * (dims.depth * dims.layers) + layer) * (
                        dims.plane * dims.rows
                    ) + (place * dims.rows + turned(dims, r))
                    value = values[l, THERMAL] * hash_uniform(within + line * dims.width * HASH_A)
                    noise[c, l, r] = value
                    h += value
                else:
                    h += noise[c, l, r]
                heff[c, l, r] = h
        return carry

    lax.fori_loop(0, dims.layers, body, 0)


def largest(m):
    x, y, z = [jnp.abs(v) for v in m]
    first = x >= jnp.maximum(y, z)
    return first, jnp.logical_and(jnp.logical_not(first), y >= z)


def tangent_parts(m, change):
    first, second = largest(m)
    last = jnp.logical_or(first, second)
    return [jnp.where(first, change[1], change[0]), jnp.where(last, change[2], change[1])]


def tangent_whole(m, parts):
    first, second = largest(m)
    last = jnp.logical_or(first, second)
    a, b = parts
    rest = a * jnp.where(first, m[1], m[0]) + b * jnp.where(last, m[2], m[1])
    along = jnp.where(first, m[0], jnp.where(second, m[1], m[2]))
    c = -rest / jnp.where(along == 0.0, 1.0, along)
    return [
        jnp.where(first, c, a),
        jnp.where(first, a, jnp.where(second, c, b)),
        jnp.where(last, b, c),
    ]


def middle_halo(l, start_halo, change_halo):
    lines = []
    for k in range(HALO):
        w = [start_halo[c, l, k] for c in range(3)]
        change = tangent_whole(w, [change_halo[c, l, k] for c in range(2)])
        m1 = [w[c] - 0.03 * change[c] for c in range(3)]
        square = m1[0] * m1[0] + m1[1] * m1[1] + m1[2] * m1[2]
        scale = lax.rsqrt(jnp.maximum(square, 1e-30))
        lines.append([v * scale for v in m1])
    return lines


def first_halo(l, halo):
    return [[halo[c, l, k] for c in range(3)] for k in range(HALO)]


def add_halos(h, l, r, halos, values):
    stiff = values[l, STIFF]
    for step, weight in ((1, NEAR), (2, FAR)):
        for position, halo in halos:
            beyond = step - 1 - abs(r - position)
            if beyond >= 0:
                h = [h[c] + (stiff * weight) * halo[beyond][c] for c in range(3)]
    return h


def rate(l, r, h, field, maskf, values):
    v = [field[c, l, r] for c in range(3)]
    torque = cross(v, h)
    twice = cross(v, torque)
    gain = values[l, SCALE] * maskf[r]
    return v, [(torque[c] + values[l, DAMP] * twice[c]) * gain for c in range(3)]


def first_rate_kernel(dims, *refs):
    far_halo, near_halo, field, maskf, heff, coefs, blocks, values, *refs = refs
    middle, base, local, far, near, message = refs
    rows = range(dims.rows)

    def body(l, prev):
        halos = [(0, first_halo(l, far_halo)), (dims.rows - 1, first_halo(l, near_halo))]
        done = []
        for r in rows:
            h = add_halos([heff[c, l, r] for c in range(3)], l, r, halos, values)
            v, change = rate(l, r, h, field, maskf, values)
            m1 = unit([v[c] - 0.03 * change[c] for c in range(3)])
            for c in range(3):
                middle[c, l, r] = m1[c]
                base[c, l, r] = v[c] - 0.015 * change[c]
            for c, part in enumerate(tangent_parts(v, change)):
                if r < HALO:
                    far[c, l, r] = part
                if r >= dims.rows - HALO:
                    near[c, l, dims.rows - 1 - r] = part
            y = matvec(table(coefs, l, PIVOT_SOURCE), m1)
            drop = matvec(table(coefs, l, PIVOT_LOWER), prev[r])
            y = [a - b for a, b in zip(y, drop)]
            for c in range(3):
                local[c, l, r] = y[c]
            done.append(y)
        return done

    zero = [[jnp.zeros(dims.tile, F32)] * 3 for _ in rows]
    last = loop(dims.layers, body, zero)
    head = sweep_back(dims, [(local, r) for r in rows], lambda l: table(blocks, l, UPPER), zero)
    for r in rows:
        sent = last[r] + head[r]
        for l in (dims.layers - 1, 0):
            sent += [middle[c, l, r] * maskf[r] for c in range(3)]
        for p in range(PARTS):
            message[p * dims.rows + r] = sent[p]


def last_kernel(dims, *refs):
    own, mate, cross, other, links, start_halo, change_halo, *refs = refs
    field, maskf, heff, upper_heff, coefs, values, base, local, *refs = refs
    result_out, accum_out, bound, edge, result, accum, sem = refs
    bound_kernel(dims, False, own, mate, cross, other, links, bound, edge)
    upper = dims.rows // 2

    def body(l, carry):
        halos = [(0, middle_halo(l, start_halo, change_halo))]
        for r in range(dims.rows):
            fix, more = others_part(dims, l, r, bound, edge, coefs, values)
            for c in range(3):
                accum[cells(dims, c, l, turned(dims, r)), :] = local[c, l, r] + fix[c]
            if r < upper:
                h = add_halos([heff[c, l, r] for c in range(3)], l, r, halos, values)
            else:
                h = [upper_heff[c, l, r - upper] for c in range(3)]
            _, change = rate(l, r, add(h, more), field, maskf, values)
            new = unit([base[c, l, r] - 0.015 * change[c] for c in range(3)])
            for c in range(3):
                result[cells(dims, c, l, turned(dims, r)), :] = new[c]
        send_lines(dims, l, accum, accum_out, sem.at[1])
        send_lines(dims, l, result, result_out, sem.at[0])
        return carry

    loop(dims.layers, body, 0)
    pltpu.make_async_copy(result, result_out, sem.at[0]).wait()
    pltpu.make_async_copy(accum, accum_out, sem.at[1]).wait()


def call(kernel, outs, args, scratch=(), ins=None, results=None):
    return pl.pallas_call(
        kernel,
        out_shape=outs,
        in_specs=ins or [vmem()] * len(args),
        out_specs=results or [vmem()] * len(outs),
        scratch_shapes=list(scratch),
        compiler_params=pltpu.CompilerParams(vmem_limit_bytes=VMEM_LIMIT),
        cost_estimate=pl.CostEstimate(flops=1000000, bytes_accessed=1000000, transcendentals=0),
    )(*args)


def ring(count, step):
    return [(i, (i + step) % count) for i in range(count)]


def local(
    magnet,
    mask,
    materials,
    exchange_strength,
    anisotropy,
    damping,
    source_strength,
    thermal_strength,
    pivots,
    lower,
    upper,
    noise_stream,
    counter,
):
    dims = Dims(
        magnet.shape[1],
        magnet.shape[2],
        magnet.shape[3],
        lax.axis_size("depth"),
        lax.axis_size("plane"),
    )
    lines = (3, dims.layers, dims.rows, dims.chunks, LANES)
    view = magnet.reshape(lines).transpose(0, 1, 3, 2, 4).reshape(-1, LANES)
    mask_view = mask.reshape(lines[2:]).transpose(1, 0, 2).reshape(-1, LANES)
    halo = shape(3, dims.layers, HALO, *dims.tile)
    rates = shape(2, dims.layers, HALO, *dims.tile)
    field = shape(*dims.field())
    padded = [pltpu.VMEM((3, dims.layers + 2, dims.rows) + dims.tile, F32)]
    assert dims.depth == GROUPS
    message = PARTS * dims.rows
    edges = shape(6, dims.rows, *dims.tile)

    def across(values):
        pairs = [(i, (i + 1 if i % 2 else i - 1) % dims.plane) for i in range(dims.plane)]
        return lax.ppermute(values, "plane", pairs)

    def beside(values):
        return lax.ppermute(values, "plane", [(i, i ^ 1) for i in range(dims.plane)])

    def exchange(values, step):
        return lax.ppermute(values, "depth", [(i, i ^ step) for i in range(dims.depth)])

    seed = jnp.full(dims.tile, noise_stream[0] * HASH_B + counter[0] * HASH_C, jnp.int32)
    inputs = (
        view,
        mask_view,
        materials,
        source_strength,
        pivots.transpose(1, 2, 0),
        lower.transpose(1, 2, 0),
        upper.transpose(1, 2, 0),
    )
    constants = (
        materials,
        exchange_strength,
        anisotropy,
        damping,
        thermal_strength,
    )
    inputs = [pltpu.with_memory_space_constraint(x, pltpu.HBM) for x in inputs]
    constants = [pltpu.with_memory_space_constraint(x, pltpu.HBM) for x in constants]
    spaces = [pltpu.VMEM] * 2 + [pltpu.SMEM] * 5
    held = [space(x.shape, x.dtype) for space, x in zip(spaces, inputs)]
    tiles, maskf, near, blocks, source = call(
        functools.partial(enter_kernel, dims),
        [
            field,
            shape(dims.rows, *dims.tile),
            halo,
            shape(dims.layers, BLOCK_COEFS, *dims.tile),
            shape(dims.layers, *dims.tile),
        ],
        inputs,
        held + [pltpu.SemaphoreType.DMA((len(inputs),))],
        [hbm()] * len(inputs),
    )
    near_halo = beside(near)
    solved, trail, sent, far = call(
        functools.partial(sweep_kernel, dims),
        [field, shape(3, dims.layers, 1, *dims.tile), shape(message + 6, *dims.tile), halo],
        (tiles, maskf, blocks, source),
    )
    mate = exchange(sent, 1)
    far_halo = across(far)
    (cross,) = call(
        functools.partial(cross_kernel, dims),
        [shape(6 * dims.rows + 6, *dims.tile)],
        (sent, mate),
    )
    other = exchange(cross, 2)
    coefs, values = call(
        functools.partial(coefficient_kernel, dims),
        [
            shape(dims.layers, LAYER_COEFS, *dims.tile),
            shape(dims.layers, LAYER_VALUES, *dims.tile),
        ],
        (trail, blocks, source, *constants),
        [pltpu.SMEM(x.shape, x.dtype) for x in constants]
        + [pltpu.SemaphoreType.DMA((len(constants),))],
        [vmem()] * 3 + [hbm()] * len(constants),
    )
    links, *bounds = call(
        functools.partial(bound_kernel, dims, True),
        [shape(GROUPS, LINKS, *dims.tile), edges, edges],
        (sent, mate, cross, other),
    )
    heff, noise = call(
        functools.partial(local_kernel, dims, True),
        [field, field],
        (tiles, solved, maskf, values, seed),
        padded,
    )
    (heff,) = call(
        functools.partial(absorb_kernel, dims), [field], (heff, *bounds, coefs, values)
    )
    middle, base, solved, far, near, sent = call(
        functools.partial(first_rate_kernel, dims),
        [field, field, field, rates, rates, shape(message, *dims.tile)],
        (far_halo, near_halo, tiles, maskf, heff, coefs, blocks, values),
    )
    mate = exchange(sent, 1)
    near_halos = [near_halo, beside(near)]
    far_halos = [far_halo, across(far)]
    (cross,) = call(
        functools.partial(cross_kernel, dims),
        [shape(6 * dims.rows, *dims.tile)],
        (sent, mate, links),
    )
    other = exchange(cross, 2)
    (heff,) = call(
        functools.partial(local_kernel, dims, False),
        [field],
        (middle, solved, maskf, values, noise),
        padded,
    )
    lined = shape(*view.shape)
    inner = dims.rows // 2
    (upper_heff,) = call(
        functools.partial(halo_kernel, dims, range(inner, dims.rows), dims.rows - 1),
        [shape(3, dims.layers, dims.rows - inner, *dims.tile)],
        (*near_halos, heff, values),
    )
    result, accum = call(
        functools.partial(last_kernel, dims),
        [lined, lined],
        (
            sent,
            mate,
            cross,
            other,
            links,
            *far_halos,
            middle,
            maskf,
            heff,
            upper_heff,
            coefs,
            values,
            base,
            solved,
        ),
        [pltpu.VMEM(edges.shape, F32)] * 2
        + [pltpu.VMEM(view.shape, F32)] * 2
        + [pltpu.SemaphoreType.DMA((2,))],
        None,
        [hbm(), hbm()],
    )

    def whole(lines_view):
        cut = lines_view.reshape(3, dims.layers, dims.chunks, dims.rows, LANES)
        return cut.transpose(0, 1, 3, 2, 4).reshape(magnet.shape)

    return whole(result), whole(accum)


def solution(mesh):
    placed = (
        P(None, "depth", "plane", None),
        P("plane", None),
        P("depth"),
    ) + (P(),) * 10
    return jax.shard_map(
        local,
        mesh=mesh,
        in_specs=placed,
        out_specs=(P(None, "depth", "plane", None), P(None, "depth", "plane", None)),
        check_vma=False,
    )
```

```python
import functools

import jax
import jax.numpy as jnp
from jax import lax
from jax.experimental import pallas as pl
from jax.experimental.pallas import tpu as pltpu
from jax.sharding import PartitionSpec as P

LANES = 128
NEAR = 4.0 / 3.0
FAR = -1.0 / 12.0
HALO = 2
VMEM_LIMIT = 16 * 1024 * 1024
UNROLL = 8
F32 = jnp.float32


def wrapped(value):
    value &= 0xFFFFFFFF
    return value - (1 << 32) if value >= (1 << 31) else value


HASH_A = wrapped(739982445)
HASH_B = wrapped(695872825)
HASH_C = wrapped(1597334677)


class Dims:
    def __init__(self, layers, rows, width, depth, plane):
        self.layers = layers
        self.rows = rows
        self.width = width
        self.chunks = width // LANES
        self.depth = depth
        self.plane = plane
        self.tile = (self.chunks, LANES)

    def field(self):
        return (3, self.layers, self.rows) + self.tile


def shape(*dims):
    return jax.ShapeDtypeStruct(dims, F32)


def vmem():
    return pl.BlockSpec(memory_space=pltpu.VMEM)


def hbm():
    return pl.BlockSpec(memory_space=pltpu.HBM)


def turned(dims, position):
    odd = lax.axis_index("plane") % 2 == 1
    return jnp.where(odd, dims.rows - 1 - position, position)


def cells(dims, comp, layer, row):
    base = (comp * dims.layers + layer) * (dims.chunks * dims.rows) + row
    return pl.ds(base, dims.chunks, stride=dims.rows)


def matvec(get, vec):
    return [get(i, 0) * vec[0] + get(i, 1) * vec[1] + get(i, 2) * vec[2] for i in range(3)]


def add(a, b):
    return [x + y for x, y in zip(a, b)]


def cross(a, b):
    return [
        a[1] * b[2] - a[2] * b[1],
        a[2] * b[0] - a[0] * b[2],
        a[0] * b[1] - a[1] * b[0],
    ]


def unit(vec):
    scale = lax.rsqrt(vec[0] * vec[0] + vec[1] * vec[1] + vec[2] * vec[2])
    return [v * scale for v in vec]


PIVOT, LOWER, UPPER, BLOCK_COEFS = 0, 9, 18, 27
PIVOT_SOURCE, PIVOT_LOWER, FROM_Y, FROM_S, LAYER_COEFS = 0, 9, 18, 27, 36
STIFF, ANISO, DAMP, THERMAL, SCALE, LAYER_VALUES = 0, 1, 2, 3, 4, 5
LAST, FIRST, TOP, BOTTOM, PARTS = 0, 3, 6, 9, 12
LAST_Y, FIRST_Y, FIRST_S, LINKS = 0, 9, 18, 27
SECOND = 8
GROUPS = 4


def table(ref, at, first):
    return lambda i, j: ref[at, first + 3 * i + j]


def column(value, j):
    return jnp.broadcast_to(value[:, j : j + 1], value.shape)


def columns(values, first):
    return [[column(values[i], first + j) for j in range(3)] for i in range(3)]


def entries(matrix):
    return lambda i, j: matrix[i][j]


def sweep_back(dims, lines, upper, start):
    def backward(k, after):
        l = dims.layers - 1 - k
        done = []
        for (ref, r), s in zip(lines, after):
            up = matvec(upper(l), s)
            s = [ref[c, l, r] - up[c] for c in range(3)]
            for c in range(3):
                ref[c, l, r] = s[c]
            done.append(s)
        return done

    return loop(dims.layers, backward, start)


def loop(count, body, start):
    step = max(k for k in range(1, UNROLL + 1) if count % k == 0)

    def steps(k, carry):
        for i in range(step):
            carry = body(k * step + i, carry)
        return carry

    if step == count:
        return steps(0, start)
    return lax.fori_loop(0, count // step, steps, start)


def fetch(inputs, held, sems):
    copies = [
        pltpu.make_async_copy(src, dst, sems.at[k])
        for k, (src, dst) in enumerate(zip(inputs, held))
    ]
    for copy in reversed(copies):
        copy.start()
    return copies


def enter_kernel(dims, *refs):
    inputs, refs = refs[:7], refs[7:]
    field, maskf, near, blocks, beta, local, trail, message, *held, sems = refs
    copies = fetch(inputs, held, sems)
    magnet, mask, materials, source, *matrices = held
    group = lax.axis_index("depth")
    rows = range(dims.rows)
    lines = [turned(dims, r) for r in rows]
    for copy in copies[2:]:
        copy.wait()

    def coefficients(l, carry):
        at = group * dims.layers + l
        beta[l] = jnp.full(dims.tile, source[materials[l]], F32)
        for k, ref in enumerate(matrices):
            for i in range(3):
                for j in range(3):
                    blocks[l, 9 * k + 3 * i + j] = jnp.full(dims.tile, ref[i, j, at], F32)
        return carry

    def forward(l, prev):
        done = []
        for r in [*rows, None]:
            f = [0.0] * 3
            if r is not None:
                v = [magnet[cells(dims, c, l, lines[r]), :] for c in range(3)]
                f = [beta[l] * a for a in v]
                for c in range(3):
                    field[c, l, r] = v[c]
                    if r >= dims.rows - HALO:
                        near[c, l, dims.rows - 1 - r] = v[c] * maskf[r]
            drop = matvec(table(blocks, l, LOWER), prev[len(done)])
            y = matvec(table(blocks, l, PIVOT), [a - b for a, b in zip(f, drop)])
            for c in range(3):
                if r is None:
                    trail[c, l, 0] = y[c]
                else:
                    local[c, l, r] = y[c]
            done.append(y)
        return done

    loop(dims.layers, coefficients, 0)
    for copy in copies[:2]:
        copy.wait()
    for r in rows:
        maskf[r] = mask[pl.ds(lines[r], dims.chunks, stride=dims.rows), :].astype(F32)
    zero = [[jnp.zeros(dims.tile, F32)] * 3 for _ in rows]
    lane = lax.broadcasted_iota(jnp.int32, dims.tile, 1)
    before, after = [[(lane == first + c).astype(F32) for c in range(3)] for first in (0, 3)]
    last = loop(dims.layers, forward, zero + [before])
    back = [(local, r) for r in rows] + [(trail, 0)]
    first = sweep_back(dims, back, lambda l: table(blocks, l, UPPER), zero + [after])
    for c in range(3):
        message[PARTS * dims.rows + LAST + c] = last[-1][c]
        message[PARTS * dims.rows + FIRST + c] = first[-1][c]
    for r in rows:
        sent = [last[r][c] for c in range(3)] + [first[r][c] for c in range(3)]
        for l in (dims.layers - 1, 0):
            sent += [field[c, l, r] * maskf[r] for c in range(3)]
        for p in range(PARTS):
            message[p * dims.rows + r] = sent[p]


def coefficient_kernel(dims, trail, blocks, source, *refs):
    inputs, (coefs, values, *held, sems) = refs[:5], refs[5:]
    copies = fetch(inputs, held, sems)
    materials, stiffness, anisotropy, damping, thermal = held

    def constants(l, carry):
        material = materials[l]
        alpha = jnp.full(dims.tile, damping[material], F32)
        values[l, DAMP] = alpha
        values[l, SCALE] = 1.0 / (1.0 + alpha * alpha)
        for k, ref in ((STIFF, stiffness), (ANISO, anisotropy), (THERMAL, thermal)):
            values[l, k] = jnp.full(dims.tile, ref[material], F32)
        return carry

    def layer(l, carry):
        pivot, low = table(blocks, l, PIVOT), table(blocks, l, LOWER)
        beta = source[l]
        for i in range(3):
            for j in range(3):
                coefs[l, PIVOT_SOURCE + 3 * i + j] = pivot(i, j) * beta
                coefs[l, PIVOT_LOWER + 3 * i + j] = (
                    pivot(i, 0) * low(0, j) + pivot(i, 1) * low(1, j) + pivot(i, 2) * low(2, j)
                )
                coefs[l, FROM_Y + 3 * i + j] = column(trail[i, l, 0], j)
                coefs[l, FROM_S + 3 * i + j] = column(trail[i, l, 0], 3 + j)
        return carry

    loop(dims.layers, layer, 0)
    for copy in copies:
        copy.wait()
    loop(dims.layers, constants, 0)


def for_each_group(body):
    group = lax.axis_index("depth")
    for g in range(GROUPS):

        @pl.when(group == g)
        def _():
            body(g)


def getter(dims, ref):
    return lambda part, r: [ref[(part + c) * dims.rows + r] for c in range(3)]


def spread(dims, ref):
    base = PARTS * dims.rows
    return lambda part: [ref[base + part + c] for c in range(3)]


def cross_kernel(dims, own, mate, *refs):
    links = None
    if len(refs) == 2:
        links, out = refs
    else:
        field, maskf, out, far = refs
        for l in range(dims.layers):
            for r in range(HALO):
                for c in range(3):
                    far[c, l, r] = field[c, l, r] * maskf[r]

    def body(g):
        even, odd = (own, mate) if g % 2 == 0 else (mate, own)
        get_even, get_odd = getter(dims, even), getter(dims, odd)
        if links is not None:
            odd_y, odd_first, even_s = (
                table(links, h, at) for h, at in ((1, LAST_Y), (3, FIRST_Y), (2, FIRST_S))
            )
        elif g < 2:
            odd_y = entries(columns(spread(dims, odd)(LAST), 0))
        else:
            odd_first = entries(columns(spread(dims, odd)(FIRST), 0))
            even_s = entries(columns(spread(dims, even)(FIRST), 3))
        for r in range(dims.rows):
            if g < 2:
                value = add(get_odd(LAST, r), matvec(odd_y, get_even(LAST, r)))
                side = get_odd(TOP, r)
            else:
                value = add(get_odd(FIRST, r), matvec(odd_first, get_even(LAST, r)))
                value = add(get_even(FIRST, r), matvec(even_s, value))
                side = get_even(BOTTOM, r)
            for c in range(3):
                out[c * dims.rows + r] = value[c]
                out[(3 + c) * dims.rows + r] = side[c]
        if links is not None:
            for tile in range(6 * dims.rows, out.shape[0]):
                out[tile] = jnp.zeros(dims.tile, F32)
            return
        lane = lax.broadcasted_iota(jnp.int32, dims.tile, 1)
        for part in (LAST, FIRST):
            pair = zip(spread(dims, even)(part), spread(dims, odd)(part))
            for c, (a, b) in enumerate(pair):
                both = jnp.where(lane < SECOND, a, pltpu.roll(b, SECOND, 1))
                out[6 * dims.rows + part + c] = both

    for_each_group(body)


def bound_kernel(dims, first, own, mate, cross, other, links, bound, edge):
    def body(g):
        base = 6 * dims.rows
        even, odd = (own, mate) if g % 2 == 0 else (mate, own)
        pairs = (cross, other) if g < 2 else (other, cross)
        for pair, ref in enumerate(pairs if first else ()):
            for h in range(2):
                values = [[ref[base + part + c] for c in range(3)] for part in (LAST, FIRST)]
                matrices = (
                    (LAST_Y, columns(values[0], SECOND * h)),
                    (FIRST_Y, columns(values[1], SECOND * h)),
                    (FIRST_S, columns(values[1], SECOND * h + 3)),
                )
                for at, matrix in matrices:
                    for i in range(3):
                        for j in range(3):
                            links[2 * pair + h, at + 3 * i + j] = matrix[i][j]
        get_even, get_odd = getter(dims, even), getter(dims, odd)
        get_cross, get_other, get_mate = (getter(dims, ref) for ref in (cross, other, mate))
        zero = [jnp.zeros(dims.tile, F32)] * 3
        for r in range(dims.rows):
            if g < 2:
                s = matvec(table(links, 2, LAST_Y), get_cross(0, r))
                s = matvec(table(links, 2, FIRST_S), matvec(table(links, 3, FIRST_Y), s))
                s = add(s, matvec(table(links, 2, FIRST_Y), get_cross(0, r)))
                s = add(s, get_other(0, r))
                if g == 0:
                    y = zero
                    s = matvec(table(links, 1, FIRST_S), s)
                    s = add(s, matvec(table(links, 1, FIRST_Y), get_even(LAST, r)))
                    s = add(s, get_odd(FIRST, r))
                else:
                    y = get_even(LAST, r)
            else:
                y = get_other(0, r)
                after = add(get_even(LAST, r), matvec(table(links, 2, LAST_Y), y))
                if g == 2:
                    s = add(get_odd(FIRST, r), matvec(table(links, 3, FIRST_Y), after))
                else:
                    y, s = after, zero
            if g % 2 == 0:
                down = zero if g == 0 else get_other(3, r)
                up = get_mate(BOTTOM, r)
            else:
                down = get_mate(TOP, r)
                up = zero if g == GROUPS - 1 else get_other(3, r)
            for c in range(3):
                bound[c, r] = y[c]
                bound[3 + c, r] = s[c]
                edge[c, r] = down[c]
                edge[3 + c, r] = up[c]

    for_each_group(body)


def others_part(dims, l, r, bound, edge, coefs, values):
    stiff = values[l, STIFF]
    down = jnp.where(l == 0, 0.5, 0.0) * stiff
    up = jnp.where(l == dims.layers - 1, 0.5, 0.0) * stiff
    y = [bound[c, r] for c in range(3)]
    s = [bound[3 + c, r] for c in range(3)]
    fix = add(matvec(table(coefs, l, FROM_Y), y), matvec(table(coefs, l, FROM_S), s))
    field = [0.5 * fix[c] + down * edge[c, r] + up * edge[3 + c, r] for c in range(3)]
    return fix, field


def absorb_kernel(dims, heff, bound, edge, coefs, values, out):
    def body(l, carry):
        for r in range(dims.rows):
            _, more = others_part(dims, l, r, bound, edge, coefs, values)
            for c in range(3):
                out[c, l, r] = heff[c, l, r] + more[c]
        return carry

    loop(dims.layers, body, 0)


def halo_kernel(dims, rows, position, start_halo, change_halo, heff, values, out):
    def body(l, carry):
        lines = middle_halo(l, start_halo, change_halo)
        for r in rows:
            h = [heff[c, l, r] for c in range(3)]
            h = add_halos(h, l, r, [(position, lines)], values)
            for c in range(3):
                out[c, l, r - rows[0]] = h[c]
        return carry

    loop(dims.layers, body, 0)


def send_lines(dims, layer, src, dst, sem):
    lines = dims.chunks * dims.rows
    for c in range(3):
        where = pl.ds((c * dims.layers + layer) * lines, lines)
        pltpu.make_async_copy(src.at[where], dst.at[where], sem).start()


def shifted_sum(dims, w, lane):
    after = pltpu.roll(w, dims.chunks - 1, 0)
    before = pltpu.roll(w, 1, 0)
    near = pltpu.roll(jnp.where(lane < 1, after, w), LANES - 1, 1)
    near += pltpu.roll(jnp.where(lane >= LANES - 1, before, w), 1, 1)
    far = pltpu.roll(jnp.where(lane < 2, after, w), LANES - 2, 1)
    far += pltpu.roll(jnp.where(lane >= LANES - 2, before, w), 2, 1)
    return NEAR * near + FAR * far


def hash_uniform(mixed):
    mixed = mixed ^ lax.shift_right_logical(mixed, jnp.int32(16))
    mixed = mixed * HASH_A
    mixed = mixed ^ lax.shift_right_logical(mixed, jnp.int32(15))
    mixed = mixed * HASH_B
    mixed = mixed ^ lax.shift_right_logical(mixed, jnp.int32(16))
    return (mixed & 65535).astype(F32) * (1.0 / 32767.5) - 1.0


def local_kernel(dims, first, *refs):
    field, solved, maskf, values, *refs = refs
    if first:
        seed, heff, noise, masked = refs
        group = lax.axis_index("depth")
        place = lax.axis_index("plane")
        within = (
            lax.broadcasted_iota(jnp.int32, dims.tile, 0) * LANES
            + lax.broadcasted_iota(jnp.int32, dims.tile, 1)
        ) * HASH_A + seed[...]
    else:
        noise, heff, masked = refs
    lane = lax.broadcasted_iota(jnp.int32, dims.tile, 1)
    rows = range(dims.rows)

    for c in range(3):
        for r in rows:
            masked[c, 0, r] = jnp.zeros(dims.tile, F32)
            masked[c, dims.layers + 1, r] = jnp.zeros(dims.tile, F32)

    def fill(l, carry):
        for r in rows:
            mask_row = maskf[r]
            for c in range(3):
                masked[c, l + 1, r] = field[c, l, r] * mask_row
        return carry

    lax.fori_loop(0, dims.layers, fill, 0)

    def body(l, carry):
        stiff = values[l, STIFF]
        aniso = values[l, ANISO]
        for c in range(3):
            w = [masked[c, l + 1, r] for r in rows]
            for r in rows:
                total = shifted_sum(dims, w[r], lane)
                for step, weight in ((1, NEAR), (2, FAR)):
                    inside = [w[q] for q in (r - step, r + step) if 0 <= q < dims.rows]
                    if inside:
                        total += weight * functools.reduce(jnp.add, inside)
                total += 0.5 * (masked[c, l, r] + masked[c, l + 2, r])
                h = stiff * total + 0.5 * solved[c, l, r]
                if c == 2:
                    h += aniso * field[c, l, r]
                if first:
                    layer = group * dims.layers + l
                    line = (c * (dims.depth * dims.layers) + layer) * (
                        dims.plane * dims.rows
                    ) + (place * dims.rows + turned(dims, r))
                    value = values[l, THERMAL] * hash_uniform(within + line * dims.width * HASH_A)
                    noise[c, l, r] = value
                    h += value
                else:
                    h += noise[c, l, r]
                heff[c, l, r] = h
        return carry

    lax.fori_loop(0, dims.layers, body, 0)


def largest(m):
    x, y, z = [jnp.abs(v) for v in m]
    first = x >= jnp.maximum(y, z)
    return first, jnp.logical_and(jnp.logical_not(first), y >= z)


def tangent_parts(m, change):
    first, second = largest(m)
    last = jnp.logical_or(first, second)
    return [jnp.where(first, change[1], change[0]), jnp.where(last, change[2], change[1])]


def tangent_whole(m, parts):
    first, second = largest(m)
    last = jnp.logical_or(first, second)
    a, b = parts
    rest = a * jnp.where(first, m[1], m[0]) + b * jnp.where(last, m[2], m[1])
    along = jnp.where(first, m[0], jnp.where(second, m[1], m[2]))
    c = -rest / jnp.where(along == 0.0, 1.0, along)
    return [
        jnp.where(first, c, a),
        jnp.where(first, a, jnp.where(second, c, b)),
        jnp.where(last, b, c),
    ]


def middle_halo(l, start_halo, change_halo):
    lines = []
    for k in range(HALO):
        w = [start_halo[c, l, k] for c in range(3)]
        change = tangent_whole(w, [change_halo[c, l, k] for c in range(2)])
        m1 = [w[c] - 0.03 * change[c] for c in range(3)]
        square = m1[0] * m1[0] + m1[1] * m1[1] + m1[2] * m1[2]
        scale = lax.rsqrt(jnp.maximum(square, 1e-30))
        lines.append([v * scale for v in m1])
    return lines


def first_halo(l, halo):
    return [[halo[c, l, k] for c in range(3)] for k in range(HALO)]


def add_halos(h, l, r, halos, values):
    stiff = values[l, STIFF]
    for step, weight in ((1, NEAR), (2, FAR)):
        for position, halo in halos:
            beyond = step - 1 - abs(r - position)
            if beyond >= 0:
                h = [h[c] + (stiff * weight) * halo[beyond][c] for c in range(3)]
    return h


def rate(l, r, h, field, maskf, values):
    v = [field[c, l, r] for c in range(3)]
    torque = cross(v, h)
    twice = cross(v, torque)
    gain = values[l, SCALE] * maskf[r]
    return v, [(torque[c] + values[l, DAMP] * twice[c]) * gain for c in range(3)]


def first_rate_kernel(dims, *refs):
    far_halo, near_halo, field, maskf, heff, coefs, blocks, values, *refs = refs
    middle, base, local, far, near, message = refs
    rows = range(dims.rows)

    def body(l, prev):
        halos = [(0, first_halo(l, far_halo)), (dims.rows - 1, first_halo(l, near_halo))]
        done = []
        for r in rows:
            h = add_halos([heff[c, l, r] for c in range(3)], l, r, halos, values)
            v, change = rate(l, r, h, field, maskf, values)
            m1 = unit([v[c] - 0.03 * change[c] for c in range(3)])
            for c in range(3):
                middle[c, l, r] = m1[c]
                base[c, l, r] = v[c] - 0.015 * change[c]
            for c, part in enumerate(tangent_parts(v, change)):
                if r < HALO:
                    far[c, l, r] = part
                if r >= dims.rows - HALO:
                    near[c, l, dims.rows - 1 - r] = part
            y = matvec(table(coefs, l, PIVOT_SOURCE), m1)
            drop = matvec(table(coefs, l, PIVOT_LOWER), prev[r])
            y = [a - b for a, b in zip(y, drop)]
            for c in range(3):
                local[c, l, r] = y[c]
            done.append(y)
        return done

    zero = [[jnp.zeros(dims.tile, F32)] * 3 for _ in rows]
    last = loop(dims.layers, body, zero)
    head = sweep_back(dims, [(local, r) for r in rows], lambda l: table(blocks, l, UPPER), zero)
    for r in rows:
        sent = last[r] + head[r]
        for l in (dims.layers - 1, 0):
            sent += [middle[c, l, r] * maskf[r] for c in range(3)]
        for p in range(PARTS):
            message[p * dims.rows + r] = sent[p]


def last_kernel(dims, *refs):
    own, mate, cross, other, links, start_halo, change_halo, *refs = refs
    field, maskf, heff, upper_heff, coefs, values, base, local, *refs = refs
    result_out, accum_out, bound, edge, result, accum, sem = refs
    bound_kernel(dims, False, own, mate, cross, other, links, bound, edge)
    upper = dims.rows // 2

    def body(l, carry):
        halos = [(0, middle_halo(l, start_halo, change_halo))]
        for r in range(dims.rows):
            fix, more = others_part(dims, l, r, bound, edge, coefs, values)
            for c in range(3):
                accum[cells(dims, c, l, turned(dims, r)), :] = local[c, l, r] + fix[c]
            if r < upper:
                h = add_halos([heff[c, l, r] for c in range(3)], l, r, halos, values)
            else:
                h = [upper_heff[c, l, r - upper] for c in range(3)]
            _, change = rate(l, r, add(h, more), field, maskf, values)
            new = unit([base[c, l, r] - 0.015 * change[c] for c in range(3)])
            for c in range(3):
                result[cells(dims, c, l, turned(dims, r)), :] = new[c]
        send_lines(dims, l, accum, accum_out, sem.at[1])
        send_lines(dims, l, result, result_out, sem.at[0])
        return carry

    loop(dims.layers, body, 0)
    pltpu.make_async_copy(result, result_out, sem.at[0]).wait()
    pltpu.make_async_copy(accum, accum_out, sem.at[1]).wait()


def call(kernel, outs, args, scratch=(), ins=None, results=None):
    return pl.pallas_call(
        kernel,
        out_shape=outs,
        in_specs=ins or [vmem()] * len(args),
        out_specs=results or [vmem()] * len(outs),
        scratch_shapes=list(scratch),
        compiler_params=pltpu.CompilerParams(vmem_limit_bytes=VMEM_LIMIT),
        cost_estimate=pl.CostEstimate(flops=1000000, bytes_accessed=1000000, transcendentals=0),
    )(*args)


def ring(count, step):
    return [(i, (i + step) % count) for i in range(count)]


def local(
    magnet,
    mask,
    materials,
    exchange_strength,
    anisotropy,
    damping,
    source_strength,
    thermal_strength,
    pivots,
    lower,
    upper,
    noise_stream,
    counter,
):
    dims = Dims(
        magnet.shape[1],
        magnet.shape[2],
        magnet.shape[3],
        lax.axis_size("depth"),
        lax.axis_size("plane"),
    )
    lines = (3, dims.layers, dims.rows, dims.chunks, LANES)
    view = magnet.reshape(lines).transpose(0, 1, 3, 2, 4).reshape(-1, LANES)
    mask_view = mask.reshape(lines[2:]).transpose(1, 0, 2).reshape(-1, LANES)
    halo = shape(3, dims.layers, HALO, *dims.tile)
    rates = shape(2, dims.layers, HALO, *dims.tile)
    field = shape(*dims.field())
    padded = [pltpu.VMEM((3, dims.layers + 2, dims.rows) + dims.tile, F32)]
    assert dims.depth == GROUPS
    message = PARTS * dims.rows
    edges = shape(6, dims.rows, *dims.tile)

    def across(values):
        pairs = [(i, (i + 1 if i % 2 else i - 1) % dims.plane) for i in range(dims.plane)]
        return lax.ppermute(values, "plane", pairs)

    def beside(values):
        return lax.ppermute(values, "plane", [(i, i ^ 1) for i in range(dims.plane)])

    def exchange(values, step):
        return lax.ppermute(values, "depth", [(i, i ^ step) for i in range(dims.depth)])

    seed = jnp.full(dims.tile, noise_stream[0] * HASH_B + counter[0] * HASH_C, jnp.int32)
    inputs = (
        view,
        mask_view,
        materials,
        source_strength,
        pivots.transpose(1, 2, 0),
        lower.transpose(1, 2, 0),
        upper.transpose(1, 2, 0),
    )
    constants = (
        materials,
        exchange_strength,
        anisotropy,
        damping,
        thermal_strength,
    )
    inputs = [pltpu.with_memory_space_constraint(x, pltpu.HBM) for x in inputs]
    constants = [pltpu.with_memory_space_constraint(x, pltpu.HBM) for x in constants]
    spaces = [pltpu.VMEM] * 2 + [pltpu.SMEM] * 5
    held = [space(x.shape, x.dtype) for space, x in zip(spaces, inputs)]
    tiles, maskf, near, blocks, source, solved, trail, sent = call(
        functools.partial(enter_kernel, dims),
        [
            field,
            shape(dims.rows, *dims.tile),
            halo,
            shape(dims.layers, BLOCK_COEFS, *dims.tile),
            shape(dims.layers, *dims.tile),
            field,
            shape(3, dims.layers, 1, *dims.tile),
            shape(message + 6, *dims.tile),
        ],
        inputs,
        held + [pltpu.SemaphoreType.DMA((len(inputs),))],
        [hbm()] * len(inputs),
    )
    near_halo = beside(near)
    mate = exchange(sent, 1)
    cross, far = call(
        functools.partial(cross_kernel, dims),
        [shape(6 * dims.rows + 6, *dims.tile), halo],
        (sent, mate, tiles, maskf),
    )
    far_halo = across(far)
    other = exchange(cross, 2)
    coefs, values = call(
        functools.partial(coefficient_kernel, dims),
        [
            shape(dims.layers, LAYER_COEFS, *dims.tile),
            shape(dims.layers, LAYER_VALUES, *dims.tile),
        ],
        (trail, blocks, source, *constants),
        [pltpu.SMEM(x.shape, x.dtype) for x in constants]
        + [pltpu.SemaphoreType.DMA((len(constants),))],
        [vmem()] * 3 + [hbm()] * len(constants),
    )
    links, *bounds = call(
        functools.partial(bound_kernel, dims, True),
        [shape(GROUPS, LINKS, *dims.tile), edges, edges],
        (sent, mate, cross, other),
    )
    heff, noise = call(
        functools.partial(local_kernel, dims, True),
        [field, field],
        (tiles, solved, maskf, values, seed),
        padded,
    )
    (heff,) = call(
        functools.partial(absorb_kernel, dims), [field], (heff, *bounds, coefs, values)
    )
    middle, base, solved, far, near, sent = call(
        functools.partial(first_rate_kernel, dims),
        [field, field, field, rates, rates, shape(message, *dims.tile)],
        (far_halo, near_halo, tiles, maskf, heff, coefs, blocks, values),
    )
    mate = exchange(sent, 1)
    near_halos = [near_halo, beside(near)]
    far_halos = [far_halo, across(far)]
    (cross,) = call(
        functools.partial(cross_kernel, dims),
        [shape(6 * dims.rows, *dims.tile)],
        (sent, mate, links),
    )
    other = exchange(cross, 2)
    (heff,) = call(
        functools.partial(local_kernel, dims, False),
        [field],
        (middle, solved, maskf, values, noise),
        padded,
    )
    lined = shape(*view.shape)
    inner = dims.rows // 2
    (upper_heff,) = call(
        functools.partial(halo_kernel, dims, range(inner, dims.rows), dims.rows - 1),
        [shape(3, dims.layers, dims.rows - inner, *dims.tile)],
        (*near_halos, heff, values),
    )
    result, accum = call(
        functools.partial(last_kernel, dims),
        [lined, lined],
        (
            sent,
            mate,
            cross,
            other,
            links,
            *far_halos,
            middle,
            maskf,
            heff,
            upper_heff,
            coefs,
            values,
            base,
            solved,
        ),
        [pltpu.VMEM(edges.shape, F32)] * 2
        + [pltpu.VMEM(view.shape, F32)] * 2
        + [pltpu.SemaphoreType.DMA((2,))],
        None,
        [hbm(), hbm()],
    )

    def whole(lines_view):
        cut = lines_view.reshape(3, dims.layers, dims.chunks, dims.rows, LANES)
        return cut.transpose(0, 1, 3, 2, 4).reshape(magnet.shape)

    return whole(result), whole(accum)


def solution(mesh):
    placed = (
        P(None, "depth", "plane", None),
        P("plane", None),
        P("depth"),
    ) + (P(),) * 10
    return jax.shard_map(
        local,
        mesh=mesh,
        in_specs=placed,
        out_specs=(P(None, "depth", "plane", None), P(None, "depth", "plane", None)),
        check_vma=False,
    )
```

```python
import functools

import jax
import jax.numpy as jnp
from jax import lax
from jax.experimental import pallas as pl
from jax.experimental.pallas import tpu as pltpu
from jax.sharding import PartitionSpec as P

LANES = 128
NEAR = 4.0 / 3.0
FAR = -1.0 / 12.0
HALO = 2
VMEM_LIMIT = 16 * 1024 * 1024
UNROLL = 8
F32 = jnp.float32


def wrapped(value):
    value &= 0xFFFFFFFF
    return value - (1 << 32) if value >= (1 << 31) else value


HASH_A = wrapped(739982445)
HASH_B = wrapped(695872825)
HASH_C = wrapped(1597334677)


class Dims:
    def __init__(self, layers, rows, width, depth, plane):
        self.layers = layers
        self.rows = rows
        self.width = width
        self.chunks = width // LANES
        self.depth = depth
        self.plane = plane
        self.tile = (self.chunks, LANES)

    def field(self):
        return (3, self.layers, self.rows) + self.tile


def shape(*dims):
    return jax.ShapeDtypeStruct(dims, F32)


def vmem():
    return pl.BlockSpec(memory_space=pltpu.VMEM)


def hbm():
    return pl.BlockSpec(memory_space=pltpu.HBM)


def turned(dims, position):
    odd = lax.axis_index("plane") % 2 == 1
    return jnp.where(odd, dims.rows - 1 - position, position)


def cells(dims, comp, layer, row):
    base = (comp * dims.layers + layer) * (dims.chunks * dims.rows) + row
    return pl.ds(base, dims.chunks, stride=dims.rows)


def matvec(get, vec):
    return [get(i, 0) * vec[0] + get(i, 1) * vec[1] + get(i, 2) * vec[2] for i in range(3)]


def add(a, b):
    return [x + y for x, y in zip(a, b)]


def cross(a, b):
    return [
        a[1] * b[2] - a[2] * b[1],
        a[2] * b[0] - a[0] * b[2],
        a[0] * b[1] - a[1] * b[0],
    ]


def unit(vec):
    scale = lax.rsqrt(vec[0] * vec[0] + vec[1] * vec[1] + vec[2] * vec[2])
    return [v * scale for v in vec]


PIVOT, LOWER, UPPER, BLOCK_COEFS = 0, 9, 18, 27
PIVOT_SOURCE, PIVOT_LOWER, FROM_Y, FROM_S, LAYER_COEFS = 0, 9, 18, 27, 36
STIFF, ANISO, DAMP, THERMAL, SCALE, LAYER_VALUES = 0, 1, 2, 3, 4, 5
LAST, FIRST, TOP, BOTTOM, PARTS = 0, 3, 6, 9, 12
LAST_Y, FIRST_Y, FIRST_S, LINKS = 0, 9, 18, 27
SECOND = 8
GROUPS = 4


def table(ref, at, first):
    return lambda i, j: ref[at, first + 3 * i + j]


def column(value, j):
    return jnp.broadcast_to(value[:, j : j + 1], value.shape)


def columns(values, first):
    return [[column(values[i], first + j) for j in range(3)] for i in range(3)]


def entries(matrix):
    return lambda i, j: matrix[i][j]


def sweep_back(dims, lines, upper, start):
    def backward(k, after):
        l = dims.layers - 1 - k
        done = []
        for (ref, r), s in zip(lines, after):
            up = matvec(upper(l), s)
            s = [ref[c, l, r] - up[c] for c in range(3)]
            for c in range(3):
                ref[c, l, r] = s[c]
            done.append(s)
        return done

    return loop(dims.layers, backward, start)


def loop(count, body, start):
    step = max(k for k in range(1, UNROLL + 1) if count % k == 0)

    def steps(k, carry):
        for i in range(step):
            carry = body(k * step + i, carry)
        return carry

    if step == count:
        return steps(0, start)
    return lax.fori_loop(0, count // step, steps, start)


def fetch(inputs, held, sems):
    copies = [
        pltpu.make_async_copy(src, dst, sems.at[k])
        for k, (src, dst) in enumerate(zip(inputs, held))
    ]
    for copy in reversed(copies):
        copy.start()
    return copies


def enter_kernel(dims, *refs):
    inputs, refs = refs[:7], refs[7:]
    field, maskf, near, blocks, beta, *held, sems = refs
    copies = fetch(inputs, held, sems)
    magnet, mask, materials, source, *matrices = held
    group = lax.axis_index("depth")
    rows = range(dims.rows)
    lines = [turned(dims, r) for r in rows]
    for copy in copies[2:]:
        copy.wait()

    def coefficients(l, carry):
        at = group * dims.layers + l
        beta[l] = jnp.full(dims.tile, source[materials[l]], F32)
        for k, ref in enumerate(matrices):
            for i in range(3):
                for j in range(3):
                    blocks[l, 9 * k + 3 * i + j] = jnp.full(dims.tile, ref[i, j, at], F32)
        return carry

    def layer(l, carry):
        for r in rows:
            mask_row = maskf[r]
            for c in range(3):
                v = magnet[cells(dims, c, l, lines[r]), :]
                field[c, l, r] = v
                if r >= dims.rows - HALO:
                    near[c, l, dims.rows - 1 - r] = v * mask_row
        return carry

    loop(dims.layers, coefficients, 0)
    for copy in copies[:2]:
        copy.wait()
    for r in rows:
        maskf[r] = mask[pl.ds(lines[r], dims.chunks, stride=dims.rows), :].astype(F32)
    loop(dims.layers, layer, 0)


def sweep_kernel(dims, field, maskf, blocks, source, local, trail, message, far):
    rows = range(dims.rows)

    def forward(l, prev):
        beta = source[l]
        done = []
        for r in [*rows, None]:
            drop = matvec(table(blocks, l, LOWER), prev[len(done)])
            f = [-a for a in drop] if r is None else [beta * field[c, l, r] - drop[c] for c in range(3)]
            y = matvec(table(blocks, l, PIVOT), f)
            for c in range(3):
                if r is None:
                    trail[c, l, 0] = y[c]
                else:
                    local[c, l, r] = y[c]
                    if r < HALO:
                        far[c, l, r] = field[c, l, r] * maskf[r]
            done.append(y)
        return done

    zero = [[jnp.zeros(dims.tile, F32)] * 3 for _ in rows]
    lane = lax.broadcasted_iota(jnp.int32, dims.tile, 1)
    before, after = [[(lane == first + c).astype(F32) for c in range(3)] for first in (0, 3)]
    last = loop(dims.layers, forward, zero + [before])
    lines = [(local, r) for r in rows] + [(trail, 0)]
    first = sweep_back(dims, lines, lambda l: table(blocks, l, UPPER), zero + [after])
    for c in range(3):
        message[PARTS * dims.rows + LAST + c] = last[-1][c]
        message[PARTS * dims.rows + FIRST + c] = first[-1][c]
    for r in rows:
        sent = [last[r][c] for c in range(3)] + [first[r][c] for c in range(3)]
        for l in (dims.layers - 1, 0):
            sent += [field[c, l, r] * maskf[r] for c in range(3)]
        for p in range(PARTS):
            message[p * dims.rows + r] = sent[p]


def coefficient_kernel(dims, trail, blocks, source, *refs):
    inputs, (coefs, values, *held, sems) = refs[:5], refs[5:]
    copies = fetch(inputs, held, sems)
    materials, stiffness, anisotropy, damping, thermal = held

    def constants(l, carry):
        material = materials[l]
        alpha = jnp.full(dims.tile, damping[material], F32)
        values[l, DAMP] = alpha
        values[l, SCALE] = 1.0 / (1.0 + alpha * alpha)
        for k, ref in ((STIFF, stiffness), (ANISO, anisotropy), (THERMAL, thermal)):
            values[l, k] = jnp.full(dims.tile, ref[material], F32)
        return carry

    def layer(l, carry):
        pivot, low = table(blocks, l, PIVOT), table(blocks, l, LOWER)
        beta = source[l]
        for i in range(3):
            for j in range(3):
                coefs[l, PIVOT_SOURCE + 3 * i + j] = pivot(i, j) * beta
                coefs[l, PIVOT_LOWER + 3 * i + j] = (
                    pivot(i, 0) * low(0, j) + pivot(i, 1) * low(1, j) + pivot(i, 2) * low(2, j)
                )
                coefs[l, FROM_Y + 3 * i + j] = column(trail[i, l, 0], j)
                coefs[l, FROM_S + 3 * i + j] = column(trail[i, l, 0], 3 + j)
        return carry

    loop(dims.layers, layer, 0)
    for copy in copies:
        copy.wait()
    loop(dims.layers, constants, 0)


def for_each_group(body):
    group = lax.axis_index("depth")
    for g in range(GROUPS):

        @pl.when(group == g)
        def _():
            body(g)


def getter(dims, ref):
    return lambda part, r: [ref[(part + c) * dims.rows + r] for c in range(3)]


def spread(dims, ref):
    base = PARTS * dims.rows
    return lambda part: [ref[base + part + c] for c in range(3)]


def cross_kernel(dims, own, mate, *refs):
    links, out = refs if len(refs) == 2 else (None, refs[0])

    def body(g):
        even, odd = (own, mate) if g % 2 == 0 else (mate, own)
        get_even, get_odd = getter(dims, even), getter(dims, odd)
        if links is not None:
            odd_y, odd_first, even_s = (
                table(links, h, at) for h, at in ((1, LAST_Y), (3, FIRST_Y), (2, FIRST_S))
            )
        elif g < 2:
            odd_y = entries(columns(spread(dims, odd)(LAST), 0))
        else:
            odd_first = entries(columns(spread(dims, odd)(FIRST), 0))
            even_s = entries(columns(spread(dims, even)(FIRST), 3))
        for r in range(dims.rows):
            if g < 2:
                value = add(get_odd(LAST, r), matvec(odd_y, get_even(LAST, r)))
                side = get_odd(TOP, r)
            else:
                value = add(get_odd(FIRST, r), matvec(odd_first, get_even(LAST, r)))
                value = add(get_even(FIRST, r), matvec(even_s, value))
                side = get_even(BOTTOM, r)
            for c in range(3):
                out[c * dims.rows + r] = value[c]
                out[(3 + c) * dims.rows + r] = side[c]
        if links is not None:
            for tile in range(6 * dims.rows, out.shape[0]):
                out[tile] = jnp.zeros(dims.tile, F32)
            return
        lane = lax.broadcasted_iota(jnp.int32, dims.tile, 1)
        for part in (LAST, FIRST):
            pair = zip(spread(dims, even)(part), spread(dims, odd)(part))
            for c, (a, b) in enumerate(pair):
                both = jnp.where(lane < SECOND, a, pltpu.roll(b, SECOND, 1))
                out[6 * dims.rows + part + c] = both

    for_each_group(body)


def bound_kernel(dims, first, own, mate, cross, other, links, bound, edge):
    def body(g):
        base = 6 * dims.rows
        even, odd = (own, mate) if g % 2 == 0 else (mate, own)
        pairs = (cross, other) if g < 2 else (other, cross)
        for pair, ref in enumerate(pairs if first else ()):
            for h in range(2):
                values = [[ref[base + part + c] for c in range(3)] for part in (LAST, FIRST)]
                matrices = (
                    (LAST_Y, columns(values[0], SECOND * h)),
                    (FIRST_Y, columns(values[1], SECOND * h)),
                    (FIRST_S, columns(values[1], SECOND * h + 3)),
                )
                for at, matrix in matrices:
                    for i in range(3):
                        for j in range(3):
                            links[2 * pair + h, at + 3 * i + j] = matrix[i][j]
        get_even, get_odd = getter(dims, even), getter(dims, odd)
        get_cross, get_other, get_mate = (getter(dims, ref) for ref in (cross, other, mate))
        zero = [jnp.zeros(dims.tile, F32)] * 3
        for r in range(dims.rows):
            if g < 2:
                s = matvec(table(links, 2, LAST_Y), get_cross(0, r))
                s = matvec(table(links, 2, FIRST_S), matvec(table(links, 3, FIRST_Y), s))
                s = add(s, matvec(table(links, 2, FIRST_Y), get_cross(0, r)))
                s = add(s, get_other(0, r))
                if g == 0:
                    y = zero
                    s = matvec(table(links, 1, FIRST_S), s)
                    s = add(s, matvec(table(links, 1, FIRST_Y), get_even(LAST, r)))
                    s = add(s, get_odd(FIRST, r))
                else:
                    y = get_even(LAST, r)
            else:
                y = get_other(0, r)
                after = add(get_even(LAST, r), matvec(table(links, 2, LAST_Y), y))
                if g == 2:
                    s = add(get_odd(FIRST, r), matvec(table(links, 3, FIRST_Y), after))
                else:
                    y, s = after, zero
            if g % 2 == 0:
                down = zero if g == 0 else get_other(3, r)
                up = get_mate(BOTTOM, r)
            else:
                down = get_mate(TOP, r)
                up = zero if g == GROUPS - 1 else get_other(3, r)
            for c in range(3):
                bound[c, r] = y[c]
                bound[3 + c, r] = s[c]
                edge[c, r] = down[c]
                edge[3 + c, r] = up[c]

    for_each_group(body)


def others_part(dims, l, r, bound, edge, coefs, values):
    stiff = values[l, STIFF]
    down = jnp.where(l == 0, 0.5, 0.0) * stiff
    up = jnp.where(l == dims.layers - 1, 0.5, 0.0) * stiff
    y = [bound[c, r] for c in range(3)]
    s = [bound[3 + c, r] for c in range(3)]
    fix = add(matvec(table(coefs, l, FROM_Y), y), matvec(table(coefs, l, FROM_S), s))
    field = [0.5 * fix[c] + down * edge[c, r] + up * edge[3 + c, r] for c in range(3)]
    return fix, field


def absorb_kernel(dims, heff, bound, edge, coefs, values, out):
    def body(l, carry):
        for r in range(dims.rows):
            _, more = others_part(dims, l, r, bound, edge, coefs, values)
            for c in range(3):
                out[c, l, r] = heff[c, l, r] + more[c]
        return carry

    loop(dims.layers, body, 0)


def halo_kernel(dims, rows, position, start_halo, change_halo, heff, values, out):
    def body(l, carry):
        lines = middle_halo(l, start_halo, change_halo)
        for r in rows:
            h = [heff[c, l, r] for c in range(3)]
            h = add_halos(h, l, r, [(position, lines)], values)
            for c in range(3):
                out[c, l, r - rows[0]] = h[c]
        return carry

    loop(dims.layers, body, 0)


def send_lines(dims, layer, src, dst, sem):
    lines = dims.chunks * dims.rows
    for c in range(3):
        where = pl.ds((c * dims.layers + layer) * lines, lines)
        pltpu.make_async_copy(src.at[where], dst.at[where], sem).start()


def shifted_sum(dims, w, lane):
    after = pltpu.roll(w, dims.chunks - 1, 0)
    before = pltpu.roll(w, 1, 0)
    near = pltpu.roll(jnp.where(lane < 1, after, w), LANES - 1, 1)
    near += pltpu.roll(jnp.where(lane >= LANES - 1, before, w), 1, 1)
    far = pltpu.roll(jnp.where(lane < 2, after, w), LANES - 2, 1)
    far += pltpu.roll(jnp.where(lane >= LANES - 2, before, w), 2, 1)
    return NEAR * near + FAR * far


def hash_uniform(mixed):
    mixed = mixed ^ lax.shift_right_logical(mixed, jnp.int32(16))
    mixed = mixed * HASH_A
    mixed = mixed ^ lax.shift_right_logical(mixed, jnp.int32(15))
    mixed = mixed * HASH_B
    mixed = mixed ^ lax.shift_right_logical(mixed, jnp.int32(16))
    return (mixed & 65535).astype(F32) * (1.0 / 32767.5) - 1.0


def others_part(dims, l, r, bound, edge, coefs, values):
    stiff = values[l, STIFF]
    down = jnp.where(l == 0, 0.5, 0.0) * stiff
    up = jnp.where(l == dims.layers - 1, 0.5, 0.0) * stiff
    y = [bound[c, r] for c in range(3)]
    s = [bound[3 + c, r] for c in range(3)]
    fix = add(matvec(table(coefs, l, FROM_Y), y), matvec(table(coefs, l, FROM_S), s))
    field = [0.5 * fix[c] + down * edge[c, r] + up * edge[3 + c, r] for c in range(3)]
    return fix, field


def absorb_kernel(dims, heff, bound, edge, coefs, values, out):
    def body(l, carry):
        for r in range(dims.rows):
            _, more = others_part(dims, l, r, bound, edge, coefs, values)
            for c in range(3):
                out[c, l, r] = heff[c, l, r] + more[c]
        return carry

    loop(dims.layers, body, 0)


def halo_kernel(dims, rows, position, start_halo, change_halo, heff, values, out):
    def body(l, carry):
        lines = middle_halo(l, start_halo, change_halo)
        for r in rows:
            h = [heff[c, l, r] for c in range(3)]
            h = add_halos(h, l, r, [(position, lines)], values)
            for c in range(3):
                out[c, l, r - rows[0]] = h[c]
        return carry

    loop(dims.layers, body, 0)


def send_lines(dims, layer, src, dst, sem):
    lines = dims.chunks * dims.rows
    for c in range(3):
        where = pl.ds((c * dims.layers + layer) * lines, lines)
        pltpu.make_async_copy(src.at[where], dst.at[where], sem).start()


def shifted_sum(dims, w, lane):
    after = pltpu.roll(w, dims.chunks - 1, 0)
    before = pltpu.roll(w, 1, 0)
    near = pltpu.roll(jnp.where(lane < 1, after, w), LANES - 1, 1)
    near += pltpu.roll(jnp.where(lane >= LANES - 1, before, w), 1, 1)
    far = pltpu.roll(jnp.where(lane < 2, after, w), LANES - 2, 1)
    far += pltpu.roll(jnp.where(lane >= LANES - 2, before, w), 2, 1)
    return NEAR * near + FAR * far


def hash_uniform(mixed):
    mixed = mixed ^ lax.shift_right_logical(mixed, jnp.int32(16))
    mixed = mixed * HASH_A
    mixed = mixed ^ lax.shift_right_logical(mixed, jnp.int32(15))
    mixed = mixed * HASH_B
    mixed = mixed ^ lax.shift_right_logical(mixed, jnp.int32(16))
    return (mixed & 65535).astype(F32) * (1.0 / 32767.5) - 1.0


def local_kernel(dims, first, *refs):
    field, solved, maskf, values, *refs = refs
    if first:
        seed, heff, noise, masked = refs
        group = lax.axis_index("depth")
        place = lax.axis_index("plane")
        within = (
            lax.broadcasted_iota(jnp.int32, dims.tile, 0) * LANES
            + lax.broadcasted_iota(jnp.int32, dims.tile, 1)
        ) * HASH_A + seed[...]
    else:
        noise, heff, masked = refs
    lane = lax.broadcasted_iota(jnp.int32, dims.tile, 1)
    rows = range(dims.rows)

    for c in range(3):
        for r in rows:
            masked[c, 0, r] = jnp.zeros(dims.tile, F32)
            masked[c, dims.layers + 1, r] = jnp.zeros(dims.tile, F32)

    def fill(l, carry):
        for r in rows:
            mask_row = maskf[r]
            for c in range(3):
                masked[c, l + 1, r] = field[c, l, r] * mask_row
        return carry

    loop(dims.layers, fill, 0)

    def body(l, carry):
        stiff = values[l, STIFF]
        aniso = values[l, ANISO]
        for c in range(3):
            w = [masked[c, l + 1, r] for r in rows]
            for r in rows:
                total = shifted_sum(dims, w[r], lane)
                for step, weight in ((1, NEAR), (2, FAR)):
                    inside = [w[q] for q in (r - step, r + step) if 0 <= q < dims.rows]
                    if inside:
                        total += weight * functools.reduce(jnp.add, inside)
                total += 0.5 * (masked[c, l, r] + masked[c, l + 2, r])
                h = stiff * total + 0.5 * solved[c, l, r]
                if c == 2:
                    h += aniso * field[c, l, r]
                if first:
                    layer = group * dims.layers + l
                    line = (c * (dims.depth * dims.layers) + layer) * (
                        dims.plane * dims.rows
                    ) + (place * dims.rows + turned(dims, r))
                    value = values[l, THERMAL] * hash_uniform(within + line * dims.width * HASH_A)
                    noise[c, l, r] = value
                    h += value
                else:
                    h += noise[c, l, r]
                heff[c, l, r] = h
        return carry

    loop(dims.layers, body, 0)


def largest(m):
    x, y, z = [jnp.abs(v) for v in m]
    first = x >= jnp.maximum(y, z)
    return first, jnp.logical_and(jnp.logical_not(first), y >= z)


def tangent_parts(m, change):
    first, second = largest(m)
    last = jnp.logical_or(first, second)
    return [jnp.where(first, change[1], change[0]), jnp.where(last, change[2], change[1])]


def tangent_whole(m, parts):
    first, second = largest(m)
    last = jnp.logical_or(first, second)
    a, b = parts
    rest = a * jnp.where(first, m[1], m[0]) + b * jnp.where(last, m[2], m[1])
    along = jnp.where(first, m[0], jnp.where(second, m[1], m[2]))
    c = -rest / jnp.where(along == 0.0, 1.0, along)
    return [
        jnp.where(first, c, a),
        jnp.where(first, a, jnp.where(second, c, b)),
        jnp.where(last, b, c),
    ]


def middle_halo(l, start_halo, change_halo):
    lines = []
    for k in range(HALO):
        w = [start_halo[c, l, k] for c in range(3)]
        change = tangent_whole(w, [change_halo[c, l, k] for c in range(2)])
        m1 = [w[c] - 0.03 * change[c] for c in range(3)]
        square = m1[0] * m1[0] + m1[1] * m1[1] + m1[2] * m1[2]
        scale = lax.rsqrt(jnp.maximum(square, 1e-30))
        lines.append([v * scale for v in m1])
    return lines


def first_halo(l, halo):
    return [[halo[c, l, k] for c in range(3)] for k in range(HALO)]


def add_halos(h, l, r, halos, values):
    stiff = values[l, STIFF]
    for step, weight in ((1, NEAR), (2, FAR)):
        for position, halo in halos:
            beyond = step - 1 - abs(r - position)
            if beyond >= 0:
                h = [h[c] + (stiff * weight) * halo[beyond][c] for c in range(3)]
    return h


def rate(l, r, h, field, maskf, values):
    v = [field[c, l, r] for c in range(3)]
    torque = cross(v, h)
    twice = cross(v, torque)
    gain = values[l, SCALE] * maskf[r]
    return v, [(torque[c] + values[l, DAMP] * twice[c]) * gain for c in range(3)]


def first_rate_kernel(dims, *refs):
    far_halo, near_halo, field, maskf, heff, coefs, blocks, values, *refs = refs
    middle, base, local, far, near, message = refs
    rows = range(dims.rows)

    def body(l, prev):
        halos = [(0, first_halo(l, far_halo)), (dims.rows - 1, first_halo(l, near_halo))]
        done = []
        for r in rows:
            h = add_halos([heff[c, l, r] for c in range(3)], l, r, halos, values)
            v, change = rate(l, r, h, field, maskf, values)
            m1 = unit([v[c] - 0.03 * change[c] for c in range(3)])
            for c in range(3):
                middle[c, l, r] = m1[c]
                base[c, l, r] = v[c] - 0.015 * change[c]
            for c, part in enumerate(tangent_parts(v, change)):
                if r < HALO:
                    far[c, l, r] = part
                if r >= dims.rows - HALO:
                    near[c, l, dims.rows - 1 - r] = part
            y = matvec(table(coefs, l, PIVOT_SOURCE), m1)
            drop = matvec(table(coefs, l, PIVOT_LOWER), prev[r])
            y = [a - b for a, b in zip(y, drop)]
            for c in range(3):
                local[c, l, r] = y[c]
            done.append(y)
        return done

    zero = [[jnp.zeros(dims.tile, F32)] * 3 for _ in rows]
    last = loop(dims.layers, body, zero)
    head = sweep_back(dims, [(local, r) for r in rows], lambda l: table(blocks, l, UPPER), zero)
    for r in rows:
        sent = last[r] + head[r]
        for l in (dims.layers - 1, 0):
            sent += [middle[c, l, r] * maskf[r] for c in range(3)]
        for p in range(PARTS):
            message[p * dims.rows + r] = sent[p]


def last_kernel(dims, *refs):
    own, mate, cross, other, links, start_halo, change_halo, *refs = refs
    field, maskf, heff, upper_heff, coefs, values, base, local, *refs = refs
    result_out, accum_out, bound, edge, result, accum, sem = refs
    bound_kernel(dims, False, own, mate, cross, other, links, bound, edge)
    upper = dims.rows // 2

    def body(l, carry):
        halos = [(0, middle_halo(l, start_halo, change_halo))]
        for r in range(dims.rows):
            fix, more = others_part(dims, l, r, bound, edge, coefs, values)
            for c in range(3):
                accum[cells(dims, c, l, turned(dims, r)), :] = local[c, l, r] + fix[c]
            if r < upper:
                h = add_halos([heff[c, l, r] for c in range(3)], l, r, halos, values)
            else:
                h = [upper_heff[c, l, r - upper] for c in range(3)]
            _, change = rate(l, r, add(h, more), field, maskf, values)
            new = unit([base[c, l, r] - 0.015 * change[c] for c in range(3)])
            for c in range(3):
                result[cells(dims, c, l, turned(dims, r)), :] = new[c]
        send_lines(dims, l, accum, accum_out, sem.at[1])
        send_lines(dims, l, result, result_out, sem.at[0])
        return carry

    loop(dims.layers, body, 0)
    pltpu.make_async_copy(result, result_out, sem.at[0]).wait()
    pltpu.make_async_copy(accum, accum_out, sem.at[1]).wait()


def call(kernel, outs, args, scratch=(), ins=None, results=None):
    return pl.pallas_call(
        kernel,
        out_shape=outs,
        in_specs=ins or [vmem()] * len(args),
        out_specs=results or [vmem()] * len(outs),
        scratch_shapes=list(scratch),
        compiler_params=pltpu.CompilerParams(vmem_limit_bytes=VMEM_LIMIT),
        cost_estimate=pl.CostEstimate(flops=1000000, bytes_accessed=1000000, transcendentals=0),
    )(*args)


def ring(count, step):
    return [(i, (i + step) % count) for i in range(count)]


def local(
    magnet,
    mask,
    materials,
    exchange_strength,
    anisotropy,
    damping,
    source_strength,
    thermal_strength,
    pivots,
    lower,
    upper,
    noise_stream,
    counter,
):
    dims = Dims(
        magnet.shape[1],
        magnet.shape[2],
        magnet.shape[3],
        lax.axis_size("depth"),
        lax.axis_size("plane"),
    )
    lines = (3, dims.layers, dims.rows, dims.chunks, LANES)
    view = magnet.reshape(lines).transpose(0, 1, 3, 2, 4).reshape(-1, LANES)
    mask_view = mask.reshape(lines[2:]).transpose(1, 0, 2).reshape(-1, LANES)
    halo = shape(3, dims.layers, HALO, *dims.tile)
    rates = shape(2, dims.layers, HALO, *dims.tile)
    field = shape(*dims.field())
    padded = [pltpu.VMEM((3, dims.layers + 2, dims.rows) + dims.tile, F32)]
    assert dims.depth == GROUPS
    message = PARTS * dims.rows
    edges = shape(6, dims.rows, *dims.tile)

    def across(values):
        pairs = [(i, (i + 1 if i % 2 else i - 1) % dims.plane) for i in range(dims.plane)]
        return lax.ppermute(values, "plane", pairs)

    def beside(values):
        return lax.ppermute(values, "plane", [(i, i ^ 1) for i in range(dims.plane)])

    def exchange(values, step):
        return lax.ppermute(values, "depth", [(i, i ^ step) for i in range(dims.depth)])

    seed = jnp.full(dims.tile, noise_stream[0] * HASH_B + counter[0] * HASH_C, jnp.int32)
    inputs = (
        view,
        mask_view,
        materials,
        source_strength,
        pivots.transpose(1, 2, 0),
        lower.transpose(1, 2, 0),
        upper.transpose(1, 2, 0),
    )
    constants = (
        materials,
        exchange_strength,
        anisotropy,
        damping,
        thermal_strength,
    )
    inputs = [pltpu.with_memory_space_constraint(x, pltpu.HBM) for x in inputs]
    constants = [pltpu.with_memory_space_constraint(x, pltpu.HBM) for x in constants]
    spaces = [pltpu.VMEM] * 2 + [pltpu.SMEM] * 5
    held = [space(x.shape, x.dtype) for space, x in zip(spaces, inputs)]
    tiles, maskf, near, blocks, source = call(
        functools.partial(enter_kernel, dims),
        [
            field,
            shape(dims.rows, *dims.tile),
            halo,
            shape(dims.layers, BLOCK_COEFS, *dims.tile),
            shape(dims.layers, *dims.tile),
        ],
        inputs,
        held + [pltpu.SemaphoreType.DMA((len(inputs),))],
        [hbm()] * len(inputs),
    )
    near_halo = beside(near)
    solved, trail, sent, far = call(
        functools.partial(sweep_kernel, dims),
        [field, shape(3, dims.layers, 1, *dims.tile), shape(message + 6, *dims.tile), halo],
        (tiles, maskf, blocks, source),
    )
    mate = exchange(sent, 1)
    far_halo = across(far)
    (cross,) = call(
        functools.partial(cross_kernel, dims),
        [shape(6 * dims.rows + 6, *dims.tile)],
        (sent, mate),
    )
    other = exchange(cross, 2)
    coefs, values = call(
        functools.partial(coefficient_kernel, dims),
        [
            shape(dims.layers, LAYER_COEFS, *dims.tile),
            shape(dims.layers, LAYER_VALUES, *dims.tile),
        ],
        (trail, blocks, source, *constants),
        [pltpu.SMEM(x.shape, x.dtype) for x in constants]
        + [pltpu.SemaphoreType.DMA((len(constants),))],
        [vmem()] * 3 + [hbm()] * len(constants),
    )
    links, *bounds = call(
        functools.partial(bound_kernel, dims, True),
        [shape(GROUPS, LINKS, *dims.tile), edges, edges],
        (sent, mate, cross, other),
    )
    heff, noise = call(
        functools.partial(local_kernel, dims, True),
        [field, field],
        (tiles, solved, maskf, values, seed),
        padded,
    )
    (heff,) = call(
        functools.partial(absorb_kernel, dims), [field], (heff, *bounds, coefs, values)
    )
    middle, base, solved, far, near, sent = call(
        functools.partial(first_rate_kernel, dims),
        [field, field, field, rates, rates, shape(message, *dims.tile)],
        (far_halo, near_halo, tiles, maskf, heff, coefs, blocks, values),
    )
    mate = exchange(sent, 1)
    near_halos = [near_halo, beside(near)]
    far_halos = [far_halo, across(far)]
    (cross,) = call(
        functools.partial(cross_kernel, dims),
        [shape(6 * dims.rows, *dims.tile)],
        (sent, mate, links),
    )
    other = exchange(cross, 2)
    (heff,) = call(
        functools.partial(local_kernel, dims, False),
        [field],
        (middle, solved, maskf, values, noise),
        padded,
    )
    lined = shape(*view.shape)
    inner = dims.rows // 2
    (upper_heff,) = call(
        functools.partial(halo_kernel, dims, range(inner, dims.rows), dims.rows - 1),
        [shape(3, dims.layers, dims.rows - inner, *dims.tile)],
        (*near_halos, heff, values),
    )
    result, accum = call(
        functools.partial(last_kernel, dims),
        [lined, lined],
        (
            sent,
            mate,
            cross,
            other,
            links,
            *far_halos,
            middle,
            maskf,
            heff,
            upper_heff,
            coefs,
            values,
            base,
            solved,
        ),
        [pltpu.VMEM(edges.shape, F32)] * 2
        + [pltpu.VMEM(view.shape, F32)] * 2
        + [pltpu.SemaphoreType.DMA((2,))],
        None,
        [hbm(), hbm()],
    )

    def whole(lines_view):
        cut = lines_view.reshape(3, dims.layers, dims.chunks, dims.rows, LANES)
        return cut.transpose(0, 1, 3, 2, 4).reshape(magnet.shape)

    return whole(result), whole(accum)


def solution(mesh):
    placed = (
        P(None, "depth", "plane", None),
        P("plane", None),
        P("depth"),
    ) + (P(),) * 10
    return jax.shard_map(
        local,
        mesh=mesh,
        in_specs=placed,
        out_specs=(P(None, "depth", "plane", None), P(None, "depth", "plane", None)),
        check_vma=False,
    )
```
